32 devices in a mesh: tpair: 8 (over z, x), col: 4 (over y, core).
Axes of the slice: x: 2, y: 2, z: 4, core: 2. Of those that a mesh axis runs over, the one named last changes fastest.
Arguments:
- peramb: bfloat16 [8, 2, 2048, 2048], P('tpair', None, None, 'col'), may hold values from -6 to 6
- sink_ops: bfloat16 [8, 2, 2, 512, 512], P('tpair'), may hold values from -0.1875 to 0.1875
- op_table: bfloat16 [2048, 2, 512], P('tpair'), may hold values from -0.1875 to 0.1875
- row_slot: int32 [2048], replicated, may hold values from 0 to 2047, each once
- pair_source: int32 [8], P('tpair'), may hold values from 0 to 1
- op_index: int32 [16, 2], P('tpair'), may hold values from 0 to 1
- listed_rows: int32 [16, 128], P('tpair'), may hold values from 0 to 511
Outputs:
- contracted: bfloat16 [16, 4, 128, 2, 2048], P('tpair', None, 'col')
The draws below stay inside these ranges and needn't reach their ends.
Inputs may be any that keep to these rules, and one draw needn't show every extreme that they name: `row_slot`: every position of 0 to 2047 appears once.
All inputs are finite; a program needn't handle non-finite values.
Results may differ from the reference program's by a relative error of at most 0.0049.
Values may be sent and summed in bfloat16 or wider, within the bound.
No kernel may reach another device: no remote copies, remote signals or barrier semaphores. Data moves between devices by JAX's collectives and lax.ppermute only.
A program may use at most 64 MiB of HBM per device.

```python
import jax
import jax.numpy as jnp
from jax import lax

NV = 512
NS = 4
ORDER = 2048
NOPS = 2
NSRC = 2
ROWS = 2048
SEL = 128
PROD_DEV = 2
PAIRS = 8
PROD_ALL = 16


def with_ends(entries, rng, low, top_value):
    extent = entries.shape
    place = [jax.random.randint(jax.random.fold_in(rng, axis), (), 0, extent[axis]) for axis in range(len(extent))]
    entries = entries.at[tuple(place)].set(low)
    longest = extent.index(max(extent))
    place[longest] = (place[longest] + 1) % extent[longest]
    return entries.at[tuple(place)].set(top_value)


def levels(own_key, extent, cuts, least, top_value):
    level, own = 1.0, jax.random.fold_in(own_key, 6)
    for position, blocks in cuts:
        draws = jnp.exp(jax.random.uniform(jax.random.fold_in(own, position), (blocks,), jnp.float32, least / len(cuts), top_value / len(cuts)))
        level = level * jnp.repeat(draws, extent[position] // blocks).reshape([-1 if axis == position else 1 for axis in range(len(extent))])
    return level


def scatter_about(own_key, shape, width, limit, shards=(), kind=jnp.bfloat16):
    level = levels(own_key, shape, shards, -0.22, 0.18) if shards else 1.0
    array = jax.random.normal(own_key, shape, jnp.float32) * width * level
    return jnp.minimum(jnp.maximum(array, -limit), limit).astype(kind)


def setup_inputs(seed: int = 0) -> dict:
    key_list = jax.random.split(jax.random.key(seed), 8)
    peramb = scatter_about(key_list[0], (PAIRS, 2, ORDER, ORDER), 1.0, 6.0, ((0, 8), (3, 4)))
    sink_ops = scatter_about(key_list[1], (PAIRS, NOPS, 2, NV, NV), (2 * NV) ** -0.5, 0.1875, ((0, 8),))
    op_table = scatter_about(key_list[2], (ROWS, 2, NV), (2 * NV) ** -0.5, 0.1875, ((0, 8),))
    row_slot = jax.random.permutation(key_list[3], ROWS).astype(jnp.int32)
    pair_source = with_ends(jax.random.randint(key_list[4], (PAIRS,), 0, NSRC), jax.random.fold_in(key_list[4], 1), 0, NSRC - 1).astype(jnp.int32)
    op_index = with_ends(jax.random.randint(key_list[5], (PROD_ALL, 2), 0, NOPS), jax.random.fold_in(key_list[5], 1), 0, NOPS - 1).astype(jnp.int32)
    listed_rows = with_ends(jax.random.randint(key_list[6], (PROD_ALL, SEL), 0, NV), jax.random.fold_in(key_list[6], 1), 0, NV - 1).astype(jnp.int32)
    return dict(peramb=peramb, sink_ops=sink_ops, op_table=op_table, row_slot=row_slot, pair_source=pair_source, op_index=op_index, listed_rows=listed_rows)


def reference(peramb, sink_ops, op_table, row_slot, pair_source, op_index, listed_rows):
    stored = op_table.astype(jnp.float32)

    def one_product(k):
        pair_id = k // PROD_DEV
        pair = lax.dynamic_index_in_dim(peramb, pair_id, 0, keepdims=False)
        pair = pair.astype(jnp.float32).reshape(2, NS, NV, ORDER)
        chosen = lax.dynamic_index_in_dim(op_index, k, 0, keepdims=False)
        listed = lax.dynamic_index_in_dim(listed_rows, k, 0, keepdims=False)
        sink_all = lax.dynamic_index_in_dim(sink_ops, pair_id, 0, keepdims=False)
        sink_one = lax.dynamic_index_in_dim(sink_all, chosen[0], 0, keepdims=False).astype(jnp.float32)
        left = sink_one[:, listed, :]
        source = lax.dynamic_index_in_dim(pair_source, pair_id, 0, keepdims=False)
        right = stored[row_slot[(source * NOPS + chosen[1]) * NV + jnp.arange(NV, dtype=jnp.int32)]]
        mixed_re = jnp.einsum("iv,svc->sic", left[0], pair[0]) - jnp.einsum("iv,svc->sic", left[1], pair[1])
        mixed_im = jnp.einsum("iv,svc->sic", left[0], pair[1]) + jnp.einsum("iv,svc->sic", left[1], pair[0])
        mixed = jnp.stack([mixed_re, mixed_im]).astype(jnp.bfloat16)
        mixed = lax.optimization_barrier(mixed).astype(jnp.float32).reshape(2, NS, SEL, NS, NV)
        right_re = right[:, 0]
        right_im = right[:, 1]
        out_re = jnp.einsum("sitv,vw->sitw", mixed[0], right_re) - jnp.einsum("sitv,vw->sitw", mixed[1], right_im)
        out_im = jnp.einsum("sitv,vw->sitw", mixed[0], right_im) + jnp.einsum("sitv,vw->sitw", mixed[1], right_re)
        joined = jnp.stack([out_re, out_im], 2).reshape(NS, SEL, 2, ORDER)
        return joined.astype(jnp.bfloat16)

    return lax.map(one_product, jnp.arange(PROD_ALL, dtype=jnp.int32))
```

```python
import functools

import jax
import jax.numpy as jnp
from jax import lax
from jax.experimental import pallas as pl
from jax.experimental.pallas import tpu as pltpu
from jax.sharding import PartitionSpec as P

NS = 4
VMEM_LIMIT = 56 * 1024 * 1024


def signed_pairs(rows_even, rows_odd):
    odd = lax.broadcasted_iota(jnp.int32, rows_even.shape, 0) % 2 == 1
    return jnp.where(odd, rows_odd, rows_even)


def mix_kernel(op_ref, listed_ref, sink_ref, peramb_ref, out_ref, left):
    products, pair_rows = listed_ref.shape[0], listed_ref.shape[1]
    eigen = sink_ref.shape[-1]
    n_cols, own2 = out_ref.shape[0], out_ref.shape[3]

    @pl.when(pl.program_id(0) == 0)
    def _():
        for k in range(products):
            op = op_ref[k, 0]
            chosen = lax.broadcasted_iota(jnp.int32, (pair_rows, eigen), 1) == listed_ref[k]
            onehot = jnp.where(chosen, 1.0, 0.0).astype(jnp.bfloat16)
            real = jnp.dot(onehot, sink_ref[0, op, 0], preferred_element_type=jnp.float32)
            imag = jnp.dot(onehot, sink_ref[0, op, 1], preferred_element_type=jnp.float32)
            rows = pl.ds(k * pair_rows, pair_rows)
            left[rows, 0:eigen] = signed_pairs(real, imag).astype(jnp.bfloat16)
            left[rows, eigen : 2 * eigen] = signed_pairs(-imag, real).astype(jnp.bfloat16)

    for k in range(products):
        rows = pl.ds(k * pair_rows, pair_rows)
        mixed = jnp.dot(
            left[rows, 0:eigen], peramb_ref[0, 0], preferred_element_type=jnp.float32
        ) + jnp.dot(
            left[rows, eigen : 2 * eigen], peramb_ref[0, 1], preferred_element_type=jnp.float32
        )
        mixed = mixed.astype(jnp.bfloat16)
        for d in range(n_cols):
            out_ref[d, k, 0] = mixed[d * own2 : (d + 1) * own2]


def mix(op_index, listed2, sink_ops, peramb, n_cols):
    products, pair_rows = listed2.shape[0], listed2.shape[1]
    eigen = sink_ops.shape[-1]
    local_cols = peramb.shape[3]
    own2 = pair_rows // n_cols
    return pl.pallas_call(
        mix_kernel,
        grid_spec=pltpu.PrefetchScalarGridSpec(
            num_scalar_prefetch=1,
            grid=(NS,),
            in_specs=[
                pl.BlockSpec(listed2.shape, lambda s, op: (0, 0, 0)),
                pl.BlockSpec(sink_ops.shape, lambda s, op: (0, 0, 0, 0, 0)),
                pl.BlockSpec((1, 2, eigen, local_cols), lambda s, op: (0, 0, s, 0)),
            ],
            out_specs=pl.BlockSpec(
                (n_cols, products, 1, own2, local_cols), lambda s, op: (0, 0, s, 0, 0)
            ),
            scratch_shapes=[pltpu.VMEM((products * pair_rows, 2 * eigen), jnp.bfloat16)],
        ),
        out_shape=jax.ShapeDtypeStruct((n_cols, products, NS, own2, local_cols), jnp.bfloat16),
        compiler_params=pltpu.CompilerParams(vmem_limit_bytes=VMEM_LIMIT),
        cost_estimate=pl.CostEstimate(
            flops=2 * NS * products * pair_rows * 2 * eigen * local_cols,
            bytes_accessed=2 * (peramb.size + sink_ops.size),
            transcendentals=0,
        ),
        name="mix",
    )(op_index, listed2, sink_ops, peramb)


def contract_kernel(n_pieces, base_ref, pos_ref, x_ref, *refs):
    pieces, out_ref, right = refs[:n_pieces], refs[n_pieces], refs[n_pieces + 1]
    n_cols, own2, local_cols = x_ref.shape[0], x_ref.shape[3], x_ref.shape[4]
    eigen = pos_ref.shape[1]
    step = min(256, eigen)
    rows = NS * own2
    for v in range(0, eigen, step):
        pos = pos_ref[0, v : v + step, :]
        total = jnp.zeros((step, 2 * eigen), jnp.float32)
        for n in range(0, n_pieces, 2):
            some = range(n, min(n + 2, n_pieces))
            chosen = [
                lax.broadcasted_iota(jnp.int32, (step, pieces[m].shape[0]), 1) == pos - base_ref[m]
                for m in some
            ]
            onehot = jnp.concatenate([jnp.where(c, 1.0, 0.0) for c in chosen], axis=1)
            table = jnp.concatenate([pieces[m][...] for m in some], axis=0)
            total += jnp.dot(
                onehot.astype(jnp.bfloat16), table, preferred_element_type=jnp.float32
            )
        total = total.astype(jnp.bfloat16)
        right[v : v + step] = total[:, :eigen]
        right[eigen + v : eigen + v + step] = total[:, eigen:]
    per_time = eigen // local_cols
    for t in range(n_cols // per_time):
        parts = [
            x_ref[j, 0].reshape(rows, local_cols) for j in range(t * per_time, (t + 1) * per_time)
        ]
        x = parts[0] if per_time == 1 else jnp.concatenate(parts, axis=1)
        wide = x.astype(jnp.float32)
        turned = signed_pairs(-pltpu.roll(wide, rows - 1, 0), pltpu.roll(wide, 1, 0))
        both = jnp.concatenate([x, turned.astype(jnp.bfloat16)], axis=1)
        result = jnp.dot(both, right[...], preferred_element_type=jnp.float32)
        result = result.astype(jnp.bfloat16).reshape(NS, own2 // 2, 2, eigen)
        out_ref[0, :, :, :, t * eigen : (t + 1) * eigen] = result


def contract(bases, pos, regrouped, pieces):
    n_cols, products, _, own2, local_cols = regrouped.shape
    eigen = pos.shape[1]
    order = n_cols * local_cols
    table_rows = sum(piece.shape[0] for piece in pieces)
    return pl.pallas_call(
        functools.partial(contract_kernel, len(pieces)),
        grid_spec=pltpu.PrefetchScalarGridSpec(
            num_scalar_prefetch=1,
            grid=(products,),
            in_specs=[
                pl.BlockSpec((1, eigen, 1), lambda k, base: (k, 0, 0)),
                pl.BlockSpec(
                    (n_cols, 1, NS, own2, local_cols), lambda k, base: (0, k, 0, 0, 0)
                ),
            ]
            + [pl.BlockSpec(piece.shape, lambda k, base: (0, 0)) for piece in pieces],
            out_specs=pl.BlockSpec(
                (1, NS, own2 // 2, 2, order), lambda k, base: (k, 0, 0, 0, 0)
            ),
            scratch_shapes=[pltpu.VMEM((2 * eigen, eigen), jnp.bfloat16)],
        ),
        out_shape=jax.ShapeDtypeStruct((products, NS, own2 // 2, 2, order), jnp.bfloat16),
        compiler_params=pltpu.CompilerParams(vmem_limit_bytes=VMEM_LIMIT),
        cost_estimate=pl.CostEstimate(
            flops=2 * products * eigen * 2 * eigen * (table_rows + NS * own2 * order // eigen),
            bytes_accessed=4 * regrouped.size,
            transcendentals=0,
        ),
        name="contract",
    )(bases, pos, regrouped, *pieces)


def gather_table(op_table, n_pair, n_cols):
    rows, eigen = op_table.shape[0], op_table.shape[2]
    me = lax.axis_index("tpair")
    if n_cols % 2 or n_pair % 2 or n_pair > 16 or rows % 32:
        own = jnp.concatenate([op_table[:, 0], op_table[:, 1]], axis=1)
        return [lax.all_gather(own, "tpair", axis=0, tiled=True)], jnp.zeros((1,), jnp.int32)
    half = rows // 2
    side = lax.axis_index("col") % 2
    own = lax.dynamic_slice_in_dim(op_table, side * half, half, 0)
    own = jnp.concatenate([own[:, 0], own[:, 1]], axis=1)
    outer = n_pair // 2

    def swap_inner(piece):
        return lax.ppermute(piece, "tpair", [(i, i ^ 1) for i in range(n_pair)])

    def swap_side(piece):
        return lax.ppermute(piece, "col", [(i, i ^ 1) for i in range(n_cols)])

    held, places = [own], [me]
    for shift in range(1, outer):
        moves = [(i, (i + 2 * shift) % n_pair) for i in range(n_pair)]
        held.append(lax.ppermute(own, "tpair", moves))
        places.append((me + n_pair - 2 * shift) % n_pair)
    held += [swap_inner(piece) for piece in held]
    places += [place ^ 1 for place in places]
    pieces, bases = [], []
    for piece, place in zip(held, places):
        pieces += [piece, swap_side(piece)]
        bases += [place * rows + side * half, place * rows + (1 - side) * half]
    return pieces, jnp.stack(bases).astype(jnp.int32)


def per_device(peramb, sink_ops, op_table, row_slot, pair_source, op_index, listed_rows):
    n_cols = lax.axis_size("col")
    n_pair = lax.axis_size("tpair")
    eigen = op_table.shape[2]
    nops = sink_ops.shape[1]
    products = op_index.shape[0]
    pieces, bases = gather_table(op_table, n_pair, n_cols)
    listed2 = jnp.repeat(listed_rows, 2, axis=1)[:, :, None]
    mixed = mix(op_index, listed2, sink_ops, peramb, n_cols)
    regrouped = lax.all_to_all(mixed, "col", split_axis=0, concat_axis=0, tiled=True)
    pos = jnp.stack(
        [
            lax.dynamic_slice_in_dim(
                row_slot, (pair_source[0] * nops + op_index[k, 1]) * eigen, eigen
            )
            for k in range(products)
        ]
    )[:, :, None]
    return contract(bases, pos, regrouped, pieces)


def solution(mesh):
    in_specs = (
        P("tpair", None, None, "col"),
        P("tpair", None, None, None, None),
        P("tpair", None, None),
        P(),
        P("tpair"),
        P("tpair", None),
        P("tpair", None),
    )
    out_specs = P("tpair", None, "col", None, None)
    return jax.shard_map(
        per_device, mesh=mesh, in_specs=in_specs, out_specs=out_specs, check_vma=False
    )
```

```python
import functools

import jax
import jax.numpy as jnp
from jax import lax
from jax.experimental import pallas as pl
from jax.experimental.pallas import tpu as pltpu
from jax.sharding import PartitionSpec as P

NS = 4
LANES = 128
VMEM_LIMIT = 56 * 1024 * 1024
BF16, F32 = jnp.bfloat16, jnp.float32


def iota(shape, dim):
    return lax.broadcasted_iota(jnp.int32, shape, dim)


def dot(a, b):
    return jnp.dot(a, b, preferred_element_type=F32)


def column(row):
    wide = jnp.broadcast_to(row, (LANES, LANES)).astype(F32)
    return jnp.transpose(wide).astype(jnp.int32)


def one_hot(col, first, width):
    tiles = [
        jnp.where(col - (first + n) == iota((col.shape[0], LANES), 1), 1.0, 0.0)
        for n in range(0, width, LANES)
    ]
    return jnp.concatenate(tiles, axis=1).astype(BF16)


def mix_kernel(op_ref, listed_ref, sink_ref, peramb_ref, *refs):
    outs, left = refs[:-1], refs[-1]
    n_cols = len(outs)
    products, listed = listed_ref.shape
    eigen = sink_ref.shape[-1]
    own2 = 2 * listed // n_cols

    @pl.when(pl.program_id(0) == 0)
    def _():
        me = lax.axis_index("col")
        row = iota((2 * listed, 2 * listed), 0)
        wanted = ((row // own2) ^ me) * (own2 // 2) + (row % own2) // 2 + (row % 2) * listed
        order = jnp.where(wanted == iota((2 * listed, 2 * listed), 1), 1.0, 0.0).astype(BF16)
        for k in range(products):
            op = op_ref[k, 0]
            onehot = one_hot(column(listed_ref[k : k + 1, :]), 0, eigen)
            real = dot(onehot, sink_ref[0, op, 0])
            imag = dot(onehot, sink_ref[0, op, 1])
            top = jnp.concatenate([real, -imag], axis=1)
            bottom = jnp.concatenate([imag, real], axis=1)
            both = jnp.concatenate([top, bottom], axis=0).astype(BF16)
            rows = dot(order, both).astype(BF16)
            for j in range(n_cols):
                at = (j * products + k) * own2
                left[at : at + own2, :] = rows[j * own2 : (j + 1) * own2]

    mixed = dot(left[:, :eigen], peramb_ref[0, 0]) + dot(left[:, eigen:], peramb_ref[0, 1])
    mixed = mixed.astype(BF16)
    for j in range(n_cols):
        for k in range(products):
            at = (j * products + k) * own2
            outs[j][k, 0] = mixed[at : at + own2]


def mix(op_index, listed_rows, sink_ops, peramb, n_cols):
    products, listed = listed_rows.shape
    eigen = sink_ops.shape[-1]
    local_cols = peramb.shape[3]
    own2 = 2 * listed // n_cols
    block = jax.ShapeDtypeStruct((products, NS, own2, local_cols), BF16)
    return pl.pallas_call(
        mix_kernel,
        grid_spec=pltpu.PrefetchScalarGridSpec(
            num_scalar_prefetch=1,
            grid=(NS,),
            in_specs=[
                pl.BlockSpec(listed_rows.shape, lambda s, op: (0, 0)),
                pl.BlockSpec(sink_ops.shape, lambda s, op: (0, 0, 0, 0, 0)),
                pl.BlockSpec((1, 2, eigen, local_cols), lambda s, op: (0, 0, s, 0)),
            ],
            out_specs=[
                pl.BlockSpec((products, 1, own2, local_cols), lambda s, op: (0, s, 0, 0))
            ]
            * n_cols,
            scratch_shapes=[pltpu.VMEM((products * 2 * listed, 2 * eigen), BF16)],
        ),
        out_shape=[block] * n_cols,
        compiler_params=pltpu.CompilerParams(vmem_limit_bytes=VMEM_LIMIT),
        cost_estimate=pl.CostEstimate(flops=1000, bytes_accessed=1000, transcendentals=0),
        name="mix",
    )(op_index, listed_rows, sink_ops, peramb)


def add_pieces(places, scalars_ref, slot_ref, pieces, products, eigen):
    source_ref, op_ref = scalars_ref
    blocks = eigen // LANES
    nops = slot_ref.shape[0] // blocks // 2
    pair, side = lax.axis_index("tpair"), lax.axis_index("col") % 2
    cols = []
    for k in range(products):
        op = source_ref[0] * nops + op_ref[k, 1]
        cols += [
            column(slot_ref[pl.ds(op * blocks + b, 1), :]) for b in range(blocks)
        ]
    col = jnp.concatenate(cols, axis=0)
    tiles, tables = [], []
    for place, piece in zip(places, pieces):
        height = piece.shape[0]
        first = place
        if isinstance(place, tuple):
            first = (2 * (pair ^ place[0]) + (side ^ place[1])) * height
        tiles.append(one_hot(col, first, height))
        tables.append(piece[...])
    return dot(jnp.concatenate(tiles, axis=1), jnp.concatenate(tables, axis=0))


def assemble_kernel(places, source_ref, op_ref, slot_ref, *refs):
    pieces, out_ref = refs[:-1], refs[-1]
    products, eigen = out_ref.shape[0], out_ref.shape[2]
    total = add_pieces(places, (source_ref, op_ref), slot_ref, pieces, products, eigen)
    total = total.astype(BF16)
    for k in range(products):
        rows = slice(k * eigen, (k + 1) * eigen)
        out_ref[k, :eigen] = total[rows, :eigen]
        out_ref[k, eigen:] = total[rows, eigen:]


def assemble(places, pieces, source, op_index, slots, eigen):
    products = op_index.shape[0]
    vmem = pl.BlockSpec(memory_space=pltpu.VMEM)
    smem = pl.BlockSpec(memory_space=pltpu.SMEM)
    return pl.pallas_call(
        functools.partial(assemble_kernel, places),
        in_specs=[smem, smem] + [vmem] * (1 + len(pieces)),
        out_specs=vmem,
        out_shape=jax.ShapeDtypeStruct((products, 2 * eigen, eigen), BF16),
        compiler_params=pltpu.CompilerParams(vmem_limit_bytes=VMEM_LIMIT),
        cost_estimate=pl.CostEstimate(flops=1000, bytes_accessed=1000, transcendentals=0),
        name="assemble",
    )(source, op_index, slots, *pieces)


def contract_kernel(places, n_cols, source_ref, op_ref, slot_ref, partial_ref, *refs):
    n_pieces = len(places)
    pieces, blocks = refs[:n_pieces], refs[n_pieces : n_pieces + n_cols]
    out_ref, right = refs[-2], refs[-1]
    own2, local_cols = blocks[0].shape[2], blocks[0].shape[3]
    products, eigen = right.shape[0], right.shape[2]
    rows = NS * own2
    k = pl.program_id(0)

    @pl.when(k == 0)
    def _():
        total = add_pieces(places, (source_ref, op_ref), slot_ref, pieces, products, eigen)
        total = total.astype(BF16)
        for p in range(products):
            some = slice(p * eigen, (p + 1) * eigen)
            right[p, :eigen] = partial_ref[p, :eigen] + total[some, :eigen]
            right[p, eigen:] = partial_ref[p, eigen:] + total[some, eigen:]

    me = lax.axis_index("col")
    per_time = eigen // local_cols
    odd = iota((rows, local_cols), 0) % 2 == 1
    for g in range(0, n_cols, per_time):
        result = None
        for j in range(g, g + per_time):
            x = blocks[j][0].reshape(rows, local_cols)
            wide = x.astype(F32)
            turned = jnp.where(odd, pltpu.roll(wide, 1, 0), -pltpu.roll(wide, rows - 1, 0))
            if per_time == 1:
                part = dot(jnp.concatenate([x, turned.astype(BF16)], axis=1), right[k])
            else:
                first = pl.multiple_of(((me ^ j) % per_time) * local_cols, local_cols)
                part = dot(x, right[k, pl.ds(first, local_cols), :])
                second = pl.multiple_of(eigen + first, local_cols)
                part += dot(turned.astype(BF16), right[k, pl.ds(second, local_cols), :])
            result = part if result is None else result + part
        result = result.astype(BF16).reshape(NS, own2 // 2, 2, eigen)
        at = pl.multiple_of(((me ^ g) // per_time) * eigen, eigen)
        out_ref[0, :, :, :, pl.ds(at, eigen)] = result


def contract(places, pieces, partial, source, op_index, slots, blocks):
    products, _, own2, local_cols = blocks[0].shape
    n_cols = len(blocks)
    eigen = partial.shape[2]
    order = n_cols * local_cols
    return pl.pallas_call(
        functools.partial(contract_kernel, places, n_cols),
        grid_spec=pltpu.PrefetchScalarGridSpec(
            num_scalar_prefetch=2,
            grid=(products,),
            in_specs=[
                pl.BlockSpec(slots.shape, lambda k, *_: (0, 0)),
                pl.BlockSpec(partial.shape, lambda k, *_: (0, 0, 0)),
            ]
            + [pl.BlockSpec(piece.shape, lambda k, *_: (0, 0)) for piece in pieces]
            + [pl.BlockSpec((1, NS, own2, local_cols), lambda k, *_: (k, 0, 0, 0))] * n_cols,
            out_specs=pl.BlockSpec(
                (1, NS, own2 // 2, 2, order), lambda k, *_: (k, 0, 0, 0, 0)
            ),
            scratch_shapes=[pltpu.VMEM((products, 2 * eigen, eigen), BF16)],
        ),
        out_shape=jax.ShapeDtypeStruct((products, NS, own2 // 2, 2, order), BF16),
        compiler_params=pltpu.CompilerParams(vmem_limit_bytes=VMEM_LIMIT),
        cost_estimate=pl.CostEstimate(
            flops=4 * products * eigen * NS * own2 * order, bytes_accessed=0, transcendentals=0
        ),
        name="contract",
    )(source, op_index, slots, partial, *pieces, *blocks)


def swap(array, axis, size, mask):
    return lax.ppermute(array, axis, [(i, i ^ mask) for i in range(size)])


def gather_table(op_table, n_pair, n_cols):
    rows = op_table.shape[0]
    if n_cols % 2 or n_pair % 2 or n_pair > 16 or rows % 32:
        own = jnp.concatenate([op_table[:, 0], op_table[:, 1]], axis=1)
        whole = lax.all_gather(own, "tpair", axis=0, tiled=True)
        half = whole.shape[0] // 2
        return [0, half], [whole[:half], whole[half:]]
    half = rows // 2
    own = lax.dynamic_slice_in_dim(op_table, lax.axis_index("col") % 2 * half, half, 0)
    own = jnp.concatenate([own[:, 0], own[:, 1]], axis=1)
    places, pieces = [], []
    for mask in range(0, n_pair, 2):
        outer = own if mask == 0 else swap(own, "tpair", n_pair, mask)
        inner = swap(outer, "tpair", n_pair, 1)
        places += [(mask, 0), (mask, 1), (mask + 1, 0), (mask + 1, 1)]
        pieces += [outer, swap(outer, "col", n_cols, 1), inner, swap(inner, "col", n_cols, 1)]
    return places, pieces


def per_device(peramb, sink_ops, op_table, row_slot, pair_source, op_index, listed_rows):
    n_cols = lax.axis_size("col")
    n_pair = lax.axis_size("tpair")
    eigen = op_table.shape[2]
    places, pieces = gather_table(op_table, n_pair, n_cols)
    blocks = mix(op_index, listed_rows, sink_ops, peramb, n_cols)
    blocks = [blocks[0]] + [swap(blocks[j], "col", n_cols, j) for j in range(1, n_cols)]
    slots = row_slot.reshape(-1, LANES)
    late = 4 if len(pieces) > 4 else 1
    partial = assemble(places[:-late], pieces[:-late], pair_source, op_index, slots, eigen)
    return contract(
        places[-late:], pieces[-late:], partial, pair_source, op_index, slots, blocks
    )


def solution(mesh):
    in_specs = (
        P("tpair", None, None, "col"),
        P("tpair", None, None, None, None),
        P("tpair", None, None),
        P(),
        P("tpair"),
        P("tpair", None),
        P("tpair", None),
    )
    out_specs = P("tpair", None, "col", None, None)
    return jax.shard_map(
        per_device, mesh=mesh, in_specs=in_specs, out_specs=out_specs, check_vma=False
    )
```

```python
import functools

import jax
import jax.numpy as jnp
from jax import lax
from jax.experimental import pallas as pl
from jax.experimental.pallas import tpu as pltpu
from jax.sharding import PartitionSpec as P

NS = 4
LANES = 128
VMEM_LIMIT = 24 * 1024 * 1024
BF16, F32 = jnp.bfloat16, jnp.float32


def iota(shape, dim):
    return lax.broadcasted_iota(jnp.int32, shape, dim)


def dot(a, b):
    return jnp.dot(a, b, preferred_element_type=F32)


def column(row):
    wide = jnp.broadcast_to(row, (LANES, LANES)).astype(F32)
    return jnp.transpose(wide).astype(jnp.int32)


def one_hot(col, first, width):
    tiles = [
        jnp.where(col - (first + n) == iota((col.shape[0], LANES), 1), 1.0, 0.0)
        for n in range(0, width, LANES)
    ]
    return jnp.concatenate(tiles, axis=1).astype(BF16)


def mix_kernel(op_ref, listed_ref, sink_ref, peramb_ref, *refs):
    outs, left = refs[:-1], refs[-1]
    n_cols = len(outs)
    products, listed = listed_ref.shape
    eigen, local_cols = sink_ref.shape[-1], peramb_ref.shape[-1]
    own2 = 2 * listed // n_cols
    me = lax.axis_index("col")
    row = iota((2 * listed, 2 * listed), 0)
    wanted = ((row // own2) ^ me) * (own2 // 2) + (row % own2) // 2 + (row % 2) * listed
    order = jnp.where(wanted == iota((2 * listed, 2 * listed), 1), 1.0, 0.0).astype(BF16)
    for k in range(products):
        op = op_ref[k, 0]
        onehot = one_hot(column(listed_ref[k : k + 1, :]), 0, eigen)
        real = dot(onehot, sink_ref[0, op, 0])
        imag = dot(onehot, sink_ref[0, op, 1])
        top = jnp.concatenate([real, -imag], axis=1)
        bottom = jnp.concatenate([imag, real], axis=1)
        both = jnp.concatenate([top, bottom], axis=0).astype(BF16)
        rows = dot(order, both).astype(BF16)
        for j in range(n_cols):
            at = (j * products + k) * own2
            left[at : at + own2, :] = rows[j * own2 : (j + 1) * own2]
    for s in range(NS):
        some = peramb_ref[0, :, s * eigen : (s + 1) * eigen, :].reshape(2 * eigen, local_cols)
        mixed = dot(left[...], some).astype(BF16)
        for j in range(n_cols):
            for k in range(products):
                at = (j * products + k) * own2
                outs[j][k, s] = mixed[at : at + own2]


def mix(op_index, listed_rows, sink_ops, peramb, n_cols):
    products, listed = listed_rows.shape
    eigen = sink_ops.shape[-1]
    local_cols = peramb.shape[3]
    own2 = 2 * listed // n_cols
    block = jax.ShapeDtypeStruct((products, NS, own2, local_cols), BF16)
    vmem = pl.BlockSpec(memory_space=pltpu.VMEM)
    return pl.pallas_call(
        mix_kernel,
        in_specs=[pl.BlockSpec(memory_space=pltpu.SMEM), vmem, vmem, vmem],
        out_specs=[vmem] * n_cols,
        out_shape=[block] * n_cols,
        scratch_shapes=[pltpu.VMEM((products * 2 * listed, 2 * eigen), BF16)],
        compiler_params=pltpu.CompilerParams(vmem_limit_bytes=VMEM_LIMIT),
        cost_estimate=pl.CostEstimate(flops=1000, bytes_accessed=1000, transcendentals=0),
        name="mix",
    )(op_index, listed_rows, sink_ops, peramb)


def add_pieces(places, scalars_ref, slot_ref, pieces, products, eigen):
    source_ref, op_ref = scalars_ref
    blocks = eigen // LANES
    nops = slot_ref.shape[0] // blocks // 2
    pair, side = lax.axis_index("tpair"), lax.axis_index("col") % 2
    cols = []
    for k in range(products):
        op = source_ref[0] * nops + op_ref[k, 1]
        cols += [
            column(slot_ref[pl.ds(op * blocks + b, 1), :]) for b in range(blocks)
        ]
    col = jnp.concatenate(cols, axis=0)
    tiles, tables = [], []
    for place, piece in zip(places, pieces):
        height = piece.shape[0]
        first = place
        if isinstance(place, tuple):
            first = (2 * (pair ^ place[0]) + (side ^ place[1])) * height
        tiles.append(one_hot(col, first, height))
        tables.append(piece[...])
    return dot(jnp.concatenate(tiles, axis=1), jnp.concatenate(tables, axis=0))


def assemble_kernel(places, source_ref, op_ref, slot_ref, *refs):
    pieces, out_ref = refs[:-1], refs[-1]
    products, eigen = out_ref.shape[0], out_ref.shape[2]
    total = add_pieces(places, (source_ref, op_ref), slot_ref, pieces, products, eigen)
    total = total.astype(BF16)
    for k in range(products):
        rows = slice(k * eigen, (k + 1) * eigen)
        out_ref[k, :eigen] = total[rows, :eigen]
        out_ref[k, eigen:] = total[rows, eigen:]


def assemble(places, pieces, source, op_index, slots, eigen):
    products = op_index.shape[0]
    vmem = pl.BlockSpec(memory_space=pltpu.VMEM)
    smem = pl.BlockSpec(memory_space=pltpu.SMEM)
    return pl.pallas_call(
        functools.partial(assemble_kernel, places),
        in_specs=[smem, smem] + [vmem] * (1 + len(pieces)),
        out_specs=vmem,
        out_shape=jax.ShapeDtypeStruct((products, 2 * eigen, eigen), BF16),
        compiler_params=pltpu.CompilerParams(vmem_limit_bytes=VMEM_LIMIT),
        cost_estimate=pl.CostEstimate(flops=1000, bytes_accessed=1000, transcendentals=0),
        name="assemble",
    )(source, op_index, slots, *pieces)


def contract_kernel(places, n_cols, source_ref, op_ref, slot_ref, partial_ref, *refs):
    n_pieces = len(places)
    pieces, blocks = refs[:n_pieces], refs[n_pieces : n_pieces + n_cols]
    out_ref, right, done, sems = refs[n_pieces + n_cols :]
    own2, local_cols = blocks[0].shape[2], blocks[0].shape[3]
    products, eigen = right.shape[0], right.shape[2]
    rows = NS * own2
    total = add_pieces(places, (source_ref, op_ref), slot_ref, pieces, products, eigen)
    total = total.astype(BF16)
    for p in range(products):
        some = slice(p * eigen, (p + 1) * eigen)
        right[p, :eigen] = partial_ref[p, :eigen] + total[some, :eigen]
        right[p, eigen:] = partial_ref[p, eigen:] + total[some, eigen:]
    me = lax.axis_index("col")
    per_time = eigen // local_cols
    times = n_cols // per_time
    odd = iota((rows, local_cols), 0) % 2 == 1
    copies = []
    for k in range(products):
        direct, turned = [], []
        for j in range(n_cols):
            x = blocks[j][k].reshape(rows, local_cols)
            wide = x.astype(F32)
            y = jnp.where(odd, pltpu.roll(wide, 1, 0), -pltpu.roll(wide, rows - 1, 0))
            direct.append(x)
            turned.append(y.astype(BF16))
        if per_time == 1:
            lhs = jnp.concatenate(
                [jnp.concatenate(direct, axis=0), jnp.concatenate(turned, axis=0)], axis=1
            )
            result = dot(lhs, right[k])
        else:
            result = []
            for j in range(n_cols):
                first = pl.multiple_of(((me ^ j) % per_time) * local_cols, local_cols)
                second = pl.multiple_of(eigen + first, local_cols)
                part = dot(direct[j], right[k, pl.ds(first, local_cols), :])
                part += dot(turned[j], right[k, pl.ds(second, local_cols), :])
                if j % per_time:
                    result[-1] += part
                else:
                    result.append(part)
            result = jnp.concatenate(result, axis=0)
        result = result.astype(BF16)
        for g in range(times):
            slot = k * times + g
            block = result[g * rows : (g + 1) * rows]
            done[slot] = block.reshape(NS, own2 // 2, 2, eigen)
            at = pl.multiple_of(((me ^ (g * per_time)) // per_time) * eigen, eigen)
            copy = pltpu.make_async_copy(
                done.at[slot], out_ref.at[k, :, :, :, pl.ds(at, eigen)], sems.at[slot]
            )
            copy.start()
            copies.append(copy)
    for copy in copies:
        copy.wait()


def contract(places, pieces, partial, source, op_index, slots, blocks):
    products, _, own2, local_cols = blocks[0].shape
    n_cols = len(blocks)
    eigen = partial.shape[2]
    order = n_cols * local_cols
    times = order // eigen
    vmem = pl.BlockSpec(memory_space=pltpu.VMEM)
    smem = pl.BlockSpec(memory_space=pltpu.SMEM)
    return pl.pallas_call(
        functools.partial(contract_kernel, places, n_cols),
        in_specs=[smem, smem] + [vmem] * (2 + len(pieces) + n_cols),
        out_specs=pl.BlockSpec(memory_space=pl.ANY),
        out_shape=jax.ShapeDtypeStruct((products, NS, own2 // 2, 2, order), BF16),
        scratch_shapes=[
            pltpu.VMEM((products, 2 * eigen, eigen), BF16),
            pltpu.VMEM((products * times, NS, own2 // 2, 2, eigen), BF16),
            pltpu.SemaphoreType.DMA((products * times,)),
        ],
        compiler_params=pltpu.CompilerParams(vmem_limit_bytes=VMEM_LIMIT),
        cost_estimate=pl.CostEstimate(
            flops=4 * products * eigen * NS * own2 * order, bytes_accessed=0, transcendentals=0
        ),
        name="contract",
    )(source, op_index, slots, partial, *pieces, *blocks)


def swap(array, axis, size, mask):
    return lax.ppermute(array, axis, [(i, i ^ mask) for i in range(size)])


def after(array, *others):
    return lax.optimization_barrier((array, *others))[0]


def per_device(peramb, sink_ops, op_table, row_slot, pair_source, op_index, listed_rows):
    n_cols = lax.axis_size("col")
    n_pair = lax.axis_size("tpair")
    rows, _, eigen = op_table.shape
    slots = row_slot.reshape(-1, LANES)

    def across(array, mask):
        return swap(array, "tpair", n_pair, mask)

    def beside(array):
        return swap(array, "col", n_cols, 1)

    def exchange(blocks):
        return [blocks[0]] + [swap(blocks[j], "col", n_cols, j) for j in range(1, n_cols)]

    if n_cols % 2 or n_pair != 8 or rows % 32:
        own = jnp.concatenate([op_table[:, 0], op_table[:, 1]], axis=1)
        whole = lax.all_gather(own, "tpair", axis=0, tiled=True)
        half = whole.shape[0] // 2
        blocks = exchange(mix(op_index, listed_rows, sink_ops, peramb, n_cols))
        partial = assemble([0], [whole[:half]], pair_source, op_index, slots, eigen)
        return contract(
            [half], [whole[half:]], partial, pair_source, op_index, slots, blocks
        )
    half = rows // 2
    own = lax.dynamic_slice_in_dim(op_table, lax.axis_index("col") % 2 * half, half, 0)
    own = jnp.concatenate([own[:, 0], own[:, 1]], axis=1)
    held = {(0, 0): own}
    held[4, 0] = across(own, 4)
    held[2, 0] = across(own, 2)
    held[1, 0] = across(own, 1)
    held[0, 1] = beside(own)
    mixed = mix(op_index, after(listed_rows, held[0, 1]), sink_ops, peramb, n_cols)
    blocks = exchange(mixed)
    near = after(held[2, 0], mixed[0])
    held[3, 0] = across(near, 1)
    held[6, 0] = across(after(own, near), 6)
    held[5, 0] = across(after(held[4, 0], near), 1)
    held[7, 0] = across(held[6, 0], 1)
    for mask in range(1, n_pair):
        held[mask, 1] = beside(held[mask, 0])
    early = [(mask, side) for mask in (0, 1, 2, 3) for side in (0, 1)]
    late = [(mask, side) for mask in (4, 5, 6, 7) for side in (0, 1)]
    partial = assemble(early, [held[p] for p in early], pair_source, op_index, slots, eigen)
    return contract(
        late, [held[p] for p in late], partial, pair_source, op_index, slots, blocks
    )


def solution(mesh):
    in_specs = (
        P("tpair", None, None, "col"),
        P("tpair", None, None, None, None),
        P("tpair", None, None),
        P(),
        P("tpair"),
        P("tpair", None),
        P("tpair", None),
    )
    out_specs = P("tpair", None, "col", None, None)
    return jax.shard_map(
        per_device, mesh=mesh, in_specs=in_specs, out_specs=out_specs, check_vma=False
    )
```

```python
import functools

import jax
import jax.numpy as jnp
from jax import lax
from jax.experimental import pallas as pl
from jax.experimental.pallas import tpu as pltpu
from jax.sharding import PartitionSpec as P

NS = 4
LANES = 128
VMEM_LIMIT = 24 * 1024 * 1024
BF16, F32 = jnp.bfloat16, jnp.float32


def iota(shape, dim):
    return lax.broadcasted_iota(jnp.int32, shape, dim)


def dot(a, b):
    return jnp.dot(a, b, preferred_element_type=F32)


def column(row):
    wide = jnp.broadcast_to(row, (LANES, LANES)).astype(F32)
    return jnp.transpose(wide).astype(jnp.int32)


def one_hot(col, first, width):
    tiles = [
        jnp.where(col - (first + n) == iota((col.shape[0], LANES), 1), 1.0, 0.0)
        for n in range(0, width, LANES)
    ]
    return jnp.concatenate(tiles, axis=1).astype(BF16)


def mix_kernel(op_ref, listed_ref, sink_ref, peramb_ref, *refs):
    outs, (left, held, sems) = refs[:-3], refs[-3:]
    n_cols = len(outs)
    products, listed = listed_ref.shape
    eigen, local_cols = sink_ref.shape[-1], peramb_ref.shape[-1]
    loads = [
        pltpu.make_async_copy(
            peramb_ref.at[0, :, pl.ds(s * eigen, eigen), :], held.at[s], sems.at[s]
        )
        for s in range(NS)
    ]
    for load in loads:
        load.start()
    own2 = 2 * listed // n_cols
    me = lax.axis_index("col")
    row = iota((2 * listed, 2 * listed), 0)
    wanted = ((row // own2) ^ me) * (own2 // 2) + (row % own2) // 2 + (row % 2) * listed
    order = jnp.where(wanted == iota((2 * listed, 2 * listed), 1), 1.0, 0.0).astype(BF16)
    for k in range(products):
        op = op_ref[k, 0]
        onehot = one_hot(column(listed_ref[k : k + 1, :]), 0, eigen)
        real = dot(onehot, sink_ref[0, op, 0])
        imag = dot(onehot, sink_ref[0, op, 1])
        top = jnp.concatenate([real, -imag], axis=1)
        bottom = jnp.concatenate([imag, real], axis=1)
        both = jnp.concatenate([top, bottom], axis=0).astype(BF16)
        rows = dot(order, both).astype(BF16)
        for j in range(n_cols):
            at = (j * products + k) * own2
            left[at : at + own2, :] = rows[j * own2 : (j + 1) * own2]
    for s in range(NS):
        loads[s].wait()
        mixed = dot(left[...], held[s].reshape(2 * eigen, local_cols)).astype(BF16)
        for j in range(n_cols):
            for k in range(products):
                at = (j * products + k) * own2
                outs[j][k, s] = mixed[at : at + own2]


def mix(op_index, listed_rows, sink_ops, peramb, n_cols):
    products, listed = listed_rows.shape
    eigen = sink_ops.shape[-1]
    local_cols = peramb.shape[3]
    own2 = 2 * listed // n_cols
    block = jax.ShapeDtypeStruct((products, NS, own2, local_cols), BF16)
    vmem = pl.BlockSpec(memory_space=pltpu.VMEM)
    return pl.pallas_call(
        mix_kernel,
        in_specs=[
            pl.BlockSpec(memory_space=pltpu.SMEM), vmem, vmem, pl.BlockSpec(memory_space=pltpu.HBM)
        ],
        out_specs=[vmem] * n_cols,
        out_shape=[block] * n_cols,
        scratch_shapes=[
            pltpu.VMEM((products * 2 * listed, 2 * eigen), BF16),
            pltpu.VMEM((NS, 2, eigen, local_cols), BF16),
            pltpu.SemaphoreType.DMA((NS,)),
        ],
        compiler_params=pltpu.CompilerParams(vmem_limit_bytes=VMEM_LIMIT),
        cost_estimate=pl.CostEstimate(flops=1000, bytes_accessed=1000, transcendentals=0),
        name="mix",
    )(op_index, listed_rows, sink_ops, peramb)


def add_pieces(places, scalars_ref, slot_ref, pieces, products, eigen):
    source_ref, op_ref = scalars_ref
    blocks = eigen // LANES
    nops = slot_ref.shape[0] // blocks // 2
    pair, side = lax.axis_index("tpair"), lax.axis_index("col") % 2
    cols = []
    for k in range(products):
        op = source_ref[0] * nops + op_ref[k, 1]
        cols += [
            column(slot_ref[pl.ds(op * blocks + b, 1), :]) for b in range(blocks)
        ]
    col = jnp.concatenate(cols, axis=0)
    tiles, tables = [], []
    for place, piece in zip(places, pieces):
        height = piece.shape[0]
        first = place
        if isinstance(place, tuple):
            first = (2 * (pair ^ place[0]) + (side ^ place[1])) * height
        tiles.append(one_hot(col, first, height))
        tables.append(piece[...])
    return dot(jnp.concatenate(tiles, axis=1), jnp.concatenate(tables, axis=0))


def assemble_kernel(places, source_ref, op_ref, slot_ref, *refs):
    pieces, out_ref = refs[:-1], refs[-1]
    products, eigen = out_ref.shape[0], out_ref.shape[2]
    total = add_pieces(places, (source_ref, op_ref), slot_ref, pieces, products, eigen)
    total = total.astype(BF16)
    for k in range(products):
        rows = slice(k * eigen, (k + 1) * eigen)
        out_ref[k, :eigen] = total[rows, :eigen]
        out_ref[k, eigen:] = total[rows, eigen:]


def assemble(places, pieces, source, op_index, slots, eigen):
    products = op_index.shape[0]
    vmem = pl.BlockSpec(memory_space=pltpu.VMEM)
    smem = pl.BlockSpec(memory_space=pltpu.SMEM)
    return pl.pallas_call(
        functools.partial(assemble_kernel, places),
        in_specs=[smem, smem] + [vmem] * (1 + len(pieces)),
        out_specs=vmem,
        out_shape=jax.ShapeDtypeStruct((products, 2 * eigen, eigen), BF16),
        compiler_params=pltpu.CompilerParams(vmem_limit_bytes=VMEM_LIMIT),
        cost_estimate=pl.CostEstimate(flops=1000, bytes_accessed=1000, transcendentals=0),
        name="assemble",
    )(source, op_index, slots, *pieces)


def contract_kernel(places, n_cols, source_ref, op_ref, slot_ref, partial_ref, *refs):
    n_pieces = len(places)
    pieces, blocks = refs[:n_pieces], refs[n_pieces : n_pieces + n_cols]
    out_ref, right, done, sems = refs[n_pieces + n_cols :]
    own2, local_cols = blocks[0].shape[2], blocks[0].shape[3]
    products, eigen = right.shape[0], right.shape[2]
    rows = NS * own2
    total = add_pieces(places, (source_ref, op_ref), slot_ref, pieces, products, eigen)
    total = total.astype(BF16)
    for p in range(products):
        some = slice(p * eigen, (p + 1) * eigen)
        right[p, :eigen] = partial_ref[p, :eigen] + total[some, :eigen]
        right[p, eigen:] = partial_ref[p, eigen:] + total[some, eigen:]
    me = lax.axis_index("col")
    per_time = eigen // local_cols
    times = n_cols // per_time
    odd = iota((rows, local_cols), 0) % 2 == 1
    copies = []
    for k in range(products):
        direct, turned = [], []
        for j in range(n_cols):
            x = blocks[j][k].reshape(rows, local_cols)
            wide = x.astype(F32)
            y = jnp.where(odd, pltpu.roll(wide, 1, 0), -pltpu.roll(wide, rows - 1, 0))
            direct.append(x)
            turned.append(y.astype(BF16))
        if per_time == 1:
            lhs = jnp.concatenate(
                [jnp.concatenate(direct, axis=0), jnp.concatenate(turned, axis=0)], axis=1
            )
            result = dot(lhs, right[k])
        else:
            result = []
            for j in range(n_cols):
                first = pl.multiple_of(((me ^ j) % per_time) * local_cols, local_cols)
                second = pl.multiple_of(eigen + first, local_cols)
                part = dot(direct[j], right[k, pl.ds(first, local_cols), :])
                part += dot(turned[j], right[k, pl.ds(second, local_cols), :])
                if j % per_time:
                    result[-1] += part
                else:
                    result.append(part)
            result = jnp.concatenate(result, axis=0)
        result = result.astype(BF16)
        for g in range(times):
            slot = k * times + g
            block = result[g * rows : (g + 1) * rows]
            done[slot] = block.reshape(NS, own2 // 2, 2, eigen)
            at = pl.multiple_of(((me ^ (g * per_time)) // per_time) * eigen, eigen)
            copy = pltpu.make_async_copy(
                done.at[slot], out_ref.at[k, :, :, :, pl.ds(at, eigen)], sems.at[slot]
            )
            copy.start()
            copies.append(copy)
    for copy in copies:
        copy.wait()


def contract(places, pieces, partial, source, op_index, slots, blocks):
    products, _, own2, local_cols = blocks[0].shape
    n_cols = len(blocks)
    eigen = partial.shape[2]
    order = n_cols * local_cols
    times = order // eigen
    vmem = pl.BlockSpec(memory_space=pltpu.VMEM)
    smem = pl.BlockSpec(memory_space=pltpu.SMEM)
    return pl.pallas_call(
        functools.partial(contract_kernel, places, n_cols),
        in_specs=[smem, smem] + [vmem] * (2 + len(pieces) + n_cols),
        out_specs=pl.BlockSpec(memory_space=pl.ANY),
        out_shape=jax.ShapeDtypeStruct((products, NS, own2 // 2, 2, order), BF16),
        scratch_shapes=[
            pltpu.VMEM((products, 2 * eigen, eigen), BF16),
            pltpu.VMEM((products * times, NS, own2 // 2, 2, eigen), BF16),
            pltpu.SemaphoreType.DMA((products * times,)),
        ],
        compiler_params=pltpu.CompilerParams(vmem_limit_bytes=VMEM_LIMIT),
        cost_estimate=pl.CostEstimate(
            flops=4 * products * eigen * NS * own2 * order, bytes_accessed=0, transcendentals=0
        ),
        name="contract",
    )(source, op_index, slots, partial, *pieces, *blocks)


def swap(array, axis, size, mask):
    return lax.ppermute(array, axis, [(i, i ^ mask) for i in range(size)])


def after(array, *others):
    return lax.optimization_barrier((array, *others))[0]


def per_device(peramb, sink_ops, op_table, row_slot, pair_source, op_index, listed_rows):
    n_cols = lax.axis_size("col")
    n_pair = lax.axis_size("tpair")
    rows, _, eigen = op_table.shape
    slots = row_slot.reshape(-1, LANES)

    def across(array, mask):
        return swap(array, "tpair", n_pair, mask)

    def beside(array):
        return swap(array, "col", n_cols, 1)

    if n_cols != 4 or n_pair != 8 or rows % 32:
        own = jnp.concatenate([op_table[:, 0], op_table[:, 1]], axis=1)
        whole = lax.all_gather(own, "tpair", axis=0, tiled=True)
        half = whole.shape[0] // 2
        mixed = mix(op_index, listed_rows, sink_ops, peramb, n_cols)
        blocks = [mixed[0]] + [swap(mixed[j], "col", n_cols, j) for j in range(1, n_cols)]
        partial = assemble([0], [whole[:half]], pair_source, op_index, slots, eigen)
        return contract(
            [half], [whole[half:]], partial, pair_source, op_index, slots, blocks
        )
    half = rows // 2
    own = lax.dynamic_slice_in_dim(op_table, lax.axis_index("col") % 2 * half, half, 0)
    own = jnp.concatenate([own[:, 0], own[:, 1]], axis=1)
    held = {(0, 0): own, (0, 1): beside(own)}
    for mask in (4, 2, 1):
        held[mask, 0] = across(own, mask)
    mixed = mix(op_index, after(listed_rows, held[0, 1]), sink_ops, peramb, n_cols)
    cross = swap(mixed[3], "col", n_cols, 2)
    straight = swap(after(mixed[2], cross), "col", n_cols, 2)
    blocks = [mixed[0], beside(mixed[1]), straight, beside(cross)]
    held[3, 0] = across(after(held[2, 0], mixed[0], held[1, 0]), 1)
    held[6, 0] = across(after(own, mixed[0]), 6)
    held[5, 0] = across(after(held[4, 0], held[3, 0]), 1)
    held[6, 1] = beside(held[6, 0])
    held[7, 0] = across(after(held[6, 0], held[6, 1], held[5, 0]), 1)
    for mask in (1, 2, 3, 4, 5):
        held[mask, 1] = beside(held[mask, 0])
    early = [(mask, side) for mask in range(7) for side in (0, 1)]
    partial = assemble(early, [held[p] for p in early], pair_source, op_index, slots, eigen)
    held[7, 1] = beside(after(held[7, 0], partial))
    late = [(7, 0), (7, 1)]
    return contract(
        late, [held[p] for p in late], partial, pair_source, op_index, slots, blocks
    )


def solution(mesh):
    in_specs = (
        P("tpair", None, None, "col"),
        P("tpair", None, None, None, None),
        P("tpair", None, None),
        P(),
        P("tpair"),
        P("tpair", None),
        P("tpair", None),
    )
    out_specs = P("tpair", None, "col", None, None)
    return jax.shard_map(
        per_device, mesh=mesh, in_specs=in_specs, out_specs=out_specs, check_vma=False
    )
```

```python
import functools

import jax
import jax.numpy as jnp
from jax import lax
from jax.experimental import pallas as pl
from jax.experimental.pallas import tpu as pltpu
from jax.sharding import PartitionSpec as P

NS = 4
LANES = 128
VMEM_LIMIT = 24 * 1024 * 1024
BF16, F32 = jnp.bfloat16, jnp.float32


def iota(shape, dim):
    return lax.broadcasted_iota(jnp.int32, shape, dim)


def dot(a, b):
    return jnp.dot(a, b, preferred_element_type=F32)


def column(row):
    wide = jnp.broadcast_to(row, (LANES, LANES)).astype(F32)
    return jnp.transpose(wide).astype(jnp.int32)


def one_hot(col, first, width):
    tiles = [
        jnp.where(col - (first + n) == iota((col.shape[0], LANES), 1), 1.0, 0.0)
        for n in range(0, width, LANES)
    ]
    return jnp.concatenate(tiles, axis=1).astype(BF16)


def mix_kernel(op_ref, listed_ref, sink_ref, peramb_ref, *refs):
    outs, (left, held, sems) = refs[:-3], refs[-3:]
    n_cols = sum(out.shape[0] for out in outs)
    products, listed = listed_ref.shape
    eigen, local_cols = sink_ref.shape[-1], peramb_ref.shape[-1]
    loads = [
        pltpu.make_async_copy(
            peramb_ref.at[0, :, pl.ds(s * eigen, eigen), :], held.at[s], sems.at[s]
        )
        for s in range(NS)
    ]
    for load in loads:
        load.start()
    own2 = 2 * listed // n_cols
    me = lax.axis_index("col")
    row = iota((2 * listed, 2 * listed), 0)
    wanted = ((row // own2) ^ me) * (own2 // 2) + (row % own2) // 2 + (row % 2) * listed
    order = jnp.where(wanted == iota((2 * listed, 2 * listed), 1), 1.0, 0.0).astype(BF16)
    for k in range(products):
        op = op_ref[k, 0]
        onehot = one_hot(column(listed_ref[k : k + 1, :]), 0, eigen)
        real = dot(onehot, sink_ref[0, op, 0])
        imag = dot(onehot, sink_ref[0, op, 1])
        top = jnp.concatenate([real, -imag], axis=1)
        bottom = jnp.concatenate([imag, real], axis=1)
        both = jnp.concatenate([top, bottom], axis=0).astype(BF16)
        rows = dot(order, both).astype(BF16)
        for j in range(n_cols):
            at = (j * products + k) * own2
            left[at : at + own2, :] = rows[j * own2 : (j + 1) * own2]
    for s in range(NS):
        loads[s].wait()
        mixed = dot(left[...], held[s].reshape(2 * eigen, local_cols)).astype(BF16)
        j = 0
        for out in outs:
            for n in range(out.shape[0]):
                for k in range(products):
                    at = (j * products + k) * own2
                    out[n, k, s] = mixed[at : at + own2]
                j += 1


def mix(op_index, listed_rows, sink_ops, peramb, groups):
    products, listed = listed_rows.shape
    eigen = sink_ops.shape[-1]
    local_cols = peramb.shape[3]
    own2 = 2 * listed // sum(groups)
    blocks = [
        jax.ShapeDtypeStruct((group, products, NS, own2, local_cols), BF16) for group in groups
    ]
    vmem = pl.BlockSpec(memory_space=pltpu.VMEM)
    return pl.pallas_call(
        mix_kernel,
        in_specs=[
            pl.BlockSpec(memory_space=pltpu.SMEM), vmem, vmem, pl.BlockSpec(memory_space=pltpu.HBM)
        ],
        out_specs=[vmem] * len(groups),
        out_shape=blocks,
        scratch_shapes=[
            pltpu.VMEM((products * 2 * listed, 2 * eigen), BF16),
            pltpu.VMEM((NS, 2, eigen, local_cols), BF16),
            pltpu.SemaphoreType.DMA((NS,)),
        ],
        compiler_params=pltpu.CompilerParams(vmem_limit_bytes=VMEM_LIMIT),
        cost_estimate=pl.CostEstimate(flops=1000, bytes_accessed=1000, transcendentals=0),
        name="mix",
    )(op_index, listed_rows, sink_ops, pltpu.with_memory_space_constraint(peramb, pltpu.HBM))


def add_pieces(places, scalars_ref, slot_ref, pieces, products, eigen):
    source_ref, op_ref = scalars_ref
    blocks = eigen // LANES
    nops = slot_ref.shape[0] // blocks // 2
    pair, side = lax.axis_index("tpair"), lax.axis_index("col") % 2
    cols = []
    for k in range(products):
        op = source_ref[0] * nops + op_ref[k, 1]
        cols += [
            column(slot_ref[pl.ds(op * blocks + b, 1), :]) for b in range(blocks)
        ]
    col = jnp.concatenate(cols, axis=0)
    tiles, tables = [], []
    for place, piece in zip(places, pieces):
        height = piece.shape[0]
        first = place
        if isinstance(place, tuple):
            first = (2 * (pair ^ place[0]) + (side ^ place[1])) * height
        tiles.append(one_hot(col, first, height))
        tables.append(piece[...])
    return dot(jnp.concatenate(tiles, axis=1), jnp.concatenate(tables, axis=0))


def assemble_kernel(places, source_ref, op_ref, slot_ref, *refs):
    pieces, out_ref = refs[:-1], refs[-1]
    products, eigen = out_ref.shape[0], out_ref.shape[2]
    total = add_pieces(places, (source_ref, op_ref), slot_ref, pieces, products, eigen)
    total = total.astype(BF16)
    for k in range(products):
        rows = slice(k * eigen, (k + 1) * eigen)
        out_ref[k, :eigen] = total[rows, :eigen]
        out_ref[k, eigen:] = total[rows, eigen:]


def assemble(places, pieces, source, op_index, slots, eigen):
    products = op_index.shape[0]
    vmem = pl.BlockSpec(memory_space=pltpu.VMEM)
    smem = pl.BlockSpec(memory_space=pltpu.SMEM)
    return pl.pallas_call(
        functools.partial(assemble_kernel, places),
        in_specs=[smem, smem] + [vmem] * (1 + len(pieces)),
        out_specs=vmem,
        out_shape=jax.ShapeDtypeStruct((products, 2 * eigen, eigen), BF16),
        compiler_params=pltpu.CompilerParams(vmem_limit_bytes=VMEM_LIMIT),
        cost_estimate=pl.CostEstimate(flops=1000, bytes_accessed=1000, transcendentals=0),
        name="assemble",
    )(source, op_index, slots, *pieces)


def contract_kernel(places, n_cols, source_ref, op_ref, slot_ref, partial_ref, *refs):
    n_pieces = len(places)
    pieces, blocks = refs[:n_pieces], refs[n_pieces : n_pieces + n_cols]
    out_ref, right, done, sems = refs[n_pieces + n_cols :]
    own2, local_cols = blocks[0].shape[3], blocks[0].shape[4]
    products, eigen = right.shape[0], right.shape[2]
    rows = NS * own2
    total = add_pieces(places, (source_ref, op_ref), slot_ref, pieces, products, eigen)
    total = total.astype(BF16)
    for p in range(products):
        some = slice(p * eigen, (p + 1) * eigen)
        right[p, :eigen] = partial_ref[p, :eigen] + total[some, :eigen]
        right[p, eigen:] = partial_ref[p, eigen:] + total[some, eigen:]
    me = lax.axis_index("col")
    per_time = eigen // local_cols
    times = n_cols // per_time
    odd = iota((rows, local_cols), 0) % 2 == 1
    copies = []
    for k in range(products):
        direct, turned = [], []
        for j in range(n_cols):
            x = blocks[j][0, k].reshape(rows, local_cols)
            wide = x.astype(F32)
            y = jnp.where(odd, pltpu.roll(wide, 1, 0), -pltpu.roll(wide, rows - 1, 0))
            direct.append(x)
            turned.append(y.astype(BF16))
        if per_time == 1:
            lhs = jnp.concatenate(
                [jnp.concatenate(direct, axis=0), jnp.concatenate(turned, axis=0)], axis=1
            )
            result = dot(lhs, right[k])
        else:
            result = []
            for j in range(n_cols):
                first = pl.multiple_of(((me ^ j) % per_time) * local_cols, local_cols)
                second = pl.multiple_of(eigen + first, local_cols)
                part = dot(direct[j], right[k, pl.ds(first, local_cols), :])
                part += dot(turned[j], right[k, pl.ds(second, local_cols), :])
                if j % per_time:
                    result[-1] += part
                else:
                    result.append(part)
            result = jnp.concatenate(result, axis=0)
        result = result.astype(BF16)
        for g in range(times):
            slot = k * times + g
            block = result[g * rows : (g + 1) * rows]
            done[slot] = block.reshape(NS, own2 // 2, 2, eigen)
            at = pl.multiple_of(((me ^ (g * per_time)) // per_time) * eigen, eigen)
            copy = pltpu.make_async_copy(
                done.at[slot], out_ref.at[k, :, :, :, pl.ds(at, eigen)], sems.at[slot]
            )
            copy.start()
            copies.append(copy)
    for copy in copies:
        copy.wait()


def contract(places, pieces, partial, source, op_index, slots, blocks):
    _, products, _, own2, local_cols = blocks[0].shape
    n_cols = len(blocks)
    eigen = partial.shape[2]
    order = n_cols * local_cols
    times = order // eigen
    vmem = pl.BlockSpec(memory_space=pltpu.VMEM)
    smem = pl.BlockSpec(memory_space=pltpu.SMEM)
    return pl.pallas_call(
        functools.partial(contract_kernel, places, n_cols),
        in_specs=[smem, smem] + [vmem] * (2 + len(pieces) + n_cols),
        out_specs=pl.BlockSpec(memory_space=pl.ANY),
        out_shape=jax.ShapeDtypeStruct((products, NS, own2 // 2, 2, order), BF16),
        scratch_shapes=[
            pltpu.VMEM((products, 2 * eigen, eigen), BF16),
            pltpu.VMEM((products * times, NS, own2 // 2, 2, eigen), BF16),
            pltpu.SemaphoreType.DMA((products * times,)),
        ],
        compiler_params=pltpu.CompilerParams(vmem_limit_bytes=VMEM_LIMIT),
        cost_estimate=pl.CostEstimate(
            flops=4 * products * eigen * NS * own2 * order, bytes_accessed=0, transcendentals=0
        ),
        name="contract",
    )(source, op_index, slots, partial, *pieces, *blocks)


def swap(array, axis, size, mask):
    return lax.ppermute(array, axis, [(i, i ^ mask) for i in range(size)])


def after(array, *others):
    return lax.optimization_barrier((array, *others))[0]


def per_device(peramb, sink_ops, op_table, row_slot, pair_source, op_index, listed_rows):
    n_cols = lax.axis_size("col")
    n_pair = lax.axis_size("tpair")
    rows, _, eigen = op_table.shape
    slots = row_slot.reshape(-1, LANES)

    def across(array, mask):
        return swap(array, "tpair", n_pair, mask)

    def beside(array):
        return swap(array, "col", n_cols, 1)

    if n_cols != 4 or n_pair != 8 or rows % 32:
        own = jnp.concatenate([op_table[:, 0], op_table[:, 1]], axis=1)
        whole = lax.all_gather(own, "tpair", axis=0, tiled=True)
        half = whole.shape[0] // 2
        mixed = mix(op_index, listed_rows, sink_ops, peramb, [1] * n_cols)
        blocks = [mixed[0]] + [swap(mixed[j], "col", n_cols, j) for j in range(1, n_cols)]
        partial = assemble([0], [whole[:half]], pair_source, op_index, slots, eigen)
        return contract(
            [half], [whole[half:]], partial, pair_source, op_index, slots, blocks
        )
    half = rows // 2
    own = lax.dynamic_slice_in_dim(op_table, lax.axis_index("col") % 2 * half, half, 0)
    own = jnp.concatenate([own[:, 0], own[:, 1]], axis=1)
    held = {(0, 0): own, (0, 1): beside(own)}
    for mask in (4, 2, 1):
        held[mask, 0] = across(own, mask)
    mixed = mix(op_index, after(listed_rows, held[0, 1]), sink_ops, peramb, [1, 1, 2])
    crossed = swap(mixed[2], "col", n_cols, 2)
    blocks = [mixed[0], beside(mixed[1]), crossed, beside(crossed[1:])]
    held[3, 0] = across(after(held[2, 0], mixed[0], held[1, 0]), 1)
    held[6, 0] = across(after(own, mixed[0]), 6)
    held[5, 0] = across(after(held[4, 0], held[3, 0]), 1)
    held[6, 1] = beside(held[6, 0])
    held[7, 0] = across(after(held[6, 0], held[6, 1], held[5, 0]), 1)
    for mask in (1, 2, 3, 4, 5):
        held[mask, 1] = beside(held[mask, 0])
    early = [(mask, side) for mask in range(7) for side in (0, 1)]
    partial = assemble(early, [held[p] for p in early], pair_source, op_index, slots, eigen)
    held[7, 1] = beside(after(held[7, 0], partial))
    late = [(7, 0), (7, 1)]
    return contract(
        late, [held[p] for p in late], partial, pair_source, op_index, slots, blocks
    )


def solution(mesh):
    in_specs = (
        P("tpair", None, None, "col"),
        P("tpair", None, None, None, None),
        P("tpair", None, None),
        P(),
        P("tpair"),
        P("tpair", None),
        P("tpair", None),
    )
    out_specs = P("tpair", None, "col", None, None)
    return jax.shard_map(
        per_device, mesh=mesh, in_specs=in_specs, out_specs=out_specs, check_vma=False
    )
```

```python
import functools

import jax
import jax.numpy as jnp
from jax import lax
from jax.experimental import pallas as pl
from jax.experimental.pallas import tpu as pltpu
from jax.sharding import PartitionSpec as P

NS = 4
LANES = 128
VMEM_LIMIT = 24 * 1024 * 1024
BF16, F32 = jnp.bfloat16, jnp.float32


def iota(shape, dim):
    return lax.broadcasted_iota(jnp.int32, shape, dim)


def dot(a, b):
    return jnp.dot(a, b, preferred_element_type=F32)


def column(row):
    wide = jnp.broadcast_to(row, (LANES, LANES)).astype(F32)
    return jnp.transpose(wide).astype(jnp.int32)


def one_hot(col, first, width):
    tiles = [
        jnp.where(col - (first + n) == iota((col.shape[0], LANES), 1), 1.0, 0.0)
        for n in range(0, width, LANES)
    ]
    return jnp.concatenate(tiles, axis=1).astype(BF16)


def mix_kernel(op_ref, listed_ref, sink_ref, peramb_ref, *refs):
    outs, (left, held, sems) = refs[:-3], refs[-3:]
    n_cols = sum(out.shape[0] for out in outs)
    products, listed = listed_ref.shape
    eigen, local_cols = sink_ref.shape[-1], peramb_ref.shape[-1]
    loads = [
        pltpu.make_async_copy(
            peramb_ref.at[0, :, pl.ds(s * eigen, eigen), :], held.at[s], sems.at[s]
        )
        for s in range(NS)
    ]
    for load in loads:
        load.start()
    own2 = 2 * listed // n_cols
    me = lax.axis_index("col")
    row = iota((2 * listed, 2 * listed), 0)
    wanted = ((row // own2) ^ me) * (own2 // 2) + (row % own2) // 2 + (row % 2) * listed
    order = jnp.where(wanted == iota((2 * listed, 2 * listed), 1), 1.0, 0.0).astype(BF16)
    for k in range(products):
        op = op_ref[k, 0]
        onehot = one_hot(column(listed_ref[k : k + 1, :]), 0, eigen)
        real = dot(onehot, sink_ref[0, op, 0])
        imag = dot(onehot, sink_ref[0, op, 1])
        top = jnp.concatenate([real, -imag], axis=1)
        bottom = jnp.concatenate([imag, real], axis=1)
        both = jnp.concatenate([top, bottom], axis=0).astype(BF16)
        rows = dot(order, both).astype(BF16)
        for j in range(n_cols):
            at = (j * products + k) * own2
            left[at : at + own2, :] = rows[j * own2 : (j + 1) * own2]
    for s in range(NS):
        loads[s].wait()
        mixed = dot(left[...], held[s].reshape(2 * eigen, local_cols)).astype(BF16)
        j = 0
        for out in outs:
            for n in range(out.shape[0]):
                for k in range(products):
                    at = (j * products + k) * own2
                    out[n, k, s] = mixed[at : at + own2]
                j += 1


def mix(op_index, listed_rows, sink_ops, peramb, groups):
    products, listed = listed_rows.shape
    eigen = sink_ops.shape[-1]
    local_cols = peramb.shape[3]
    own2 = 2 * listed // sum(groups)
    blocks = [
        jax.ShapeDtypeStruct((group, products, NS, own2, local_cols), BF16) for group in groups
    ]
    vmem = pl.BlockSpec(memory_space=pltpu.VMEM)
    return pl.pallas_call(
        mix_kernel,
        in_specs=[
            pl.BlockSpec(memory_space=pltpu.SMEM), vmem, vmem, pl.BlockSpec(memory_space=pltpu.HBM)
        ],
        out_specs=[vmem] * len(groups),
        out_shape=blocks,
        scratch_shapes=[
            pltpu.VMEM((products * 2 * listed, 2 * eigen), BF16),
            pltpu.VMEM((NS, 2, eigen, local_cols), BF16),
            pltpu.SemaphoreType.DMA((NS,)),
        ],
        compiler_params=pltpu.CompilerParams(vmem_limit_bytes=VMEM_LIMIT),
        cost_estimate=pl.CostEstimate(flops=1000, bytes_accessed=1000, transcendentals=0),
        name="mix",
    )(op_index, listed_rows, sink_ops, pltpu.with_memory_space_constraint(peramb, pltpu.HBM))


def add_pieces(places, scalars_ref, slot_ref, pieces, products, eigen):
    source_ref, op_ref = scalars_ref
    blocks = eigen // LANES
    nops = slot_ref.shape[0] // blocks // 2
    pair, side = lax.axis_index("tpair"), lax.axis_index("col") % 2
    cols = []
    for k in range(products):
        op = source_ref[0] * nops + op_ref[k, 1]
        cols += [
            column(slot_ref[pl.ds(op * blocks + b, 1), :]) for b in range(blocks)
        ]
    col = jnp.concatenate(cols, axis=0)
    tiles, tables = [], []
    for place, piece in zip(places, pieces):
        height = piece.shape[0]
        first = place
        if isinstance(place, tuple):
            first = (2 * (pair ^ place[0]) + (side ^ place[1])) * height
        tiles.append(one_hot(col, first, height))
        tables.append(piece[...])
    return dot(jnp.concatenate(tiles, axis=1), jnp.concatenate(tables, axis=0))


def assemble_kernel(places, source_ref, op_ref, slot_ref, *refs):
    pieces, out_ref = refs[:-1], refs[-1]
    products, eigen = out_ref.shape[0], out_ref.shape[2]
    total = add_pieces(places, (source_ref, op_ref), slot_ref, pieces, products, eigen)
    total = total.astype(BF16)
    for k in range(products):
        rows = slice(k * eigen, (k + 1) * eigen)
        out_ref[k, :eigen] = total[rows, :eigen]
        out_ref[k, eigen:] = total[rows, eigen:]


def assemble(places, pieces, source, op_index, slots, eigen):
    products = op_index.shape[0]
    vmem = pl.BlockSpec(memory_space=pltpu.VMEM)
    smem = pl.BlockSpec(memory_space=pltpu.SMEM)
    return pl.pallas_call(
        functools.partial(assemble_kernel, places),
        in_specs=[smem, smem] + [vmem] * (1 + len(pieces)),
        out_specs=vmem,
        out_shape=jax.ShapeDtypeStruct((products, 2 * eigen, eigen), BF16),
        compiler_params=pltpu.CompilerParams(vmem_limit_bytes=VMEM_LIMIT),
        cost_estimate=pl.CostEstimate(flops=1000, bytes_accessed=1000, transcendentals=0),
        name="assemble",
    )(source, op_index, slots, *pieces)


def contract_kernel(places, n_cols, source_ref, op_ref, slot_ref, partial_ref, *refs):
    n_pieces = len(places)
    pieces, blocks = refs[:n_pieces], refs[n_pieces : n_pieces + n_cols]
    out_ref, right, done, sems = refs[n_pieces + n_cols :]
    own2, local_cols = blocks[0].shape[3], blocks[0].shape[4]
    products, eigen = right.shape[0], right.shape[2]
    rows = NS * own2
    total = add_pieces(places, (source_ref, op_ref), slot_ref, pieces, products, eigen)
    total = total.astype(BF16)
    for p in range(products):
        some = slice(p * eigen, (p + 1) * eigen)
        right[p, :eigen] = partial_ref[p, :eigen] + total[some, :eigen]
        right[p, eigen:] = partial_ref[p, eigen:] + total[some, eigen:]
    me = lax.axis_index("col")
    per_time = eigen // local_cols
    times = n_cols // per_time
    odd = iota((rows, local_cols), 0) % 2 == 1
    copies = []
    for k in range(products):
        direct, turned = [], []
        for j in range(n_cols):
            x = blocks[j][0, k].reshape(rows, local_cols)
            wide = x.astype(F32)
            y = jnp.where(odd, pltpu.roll(wide, 1, 0), -pltpu.roll(wide, rows - 1, 0))
            direct.append(x)
            turned.append(y.astype(BF16))
        if per_time == 1:
            lhs = jnp.concatenate(
                [jnp.concatenate(direct, axis=0), jnp.concatenate(turned, axis=0)], axis=1
            )
            result = dot(lhs, right[k])
        else:
            result = []
            for j in range(n_cols):
                first = pl.multiple_of(((me ^ j) % per_time) * local_cols, local_cols)
                second = pl.multiple_of(eigen + first, local_cols)
                part = dot(direct[j], right[k, pl.ds(first, local_cols), :])
                part += dot(turned[j], right[k, pl.ds(second, local_cols), :])
                if j % per_time:
                    result[-1] += part
                else:
                    result.append(part)
            result = jnp.concatenate(result, axis=0)
        result = result.astype(BF16)
        for g in range(times):
            slot = k * times + g
            block = result[g * rows : (g + 1) * rows]
            done[slot] = block.reshape(NS, own2 // 2, 2, eigen)
            at = pl.multiple_of(((me ^ (g * per_time)) // per_time) * eigen, eigen)
            copy = pltpu.make_async_copy(
                done.at[slot], out_ref.at[k, :, :, :, pl.ds(at, eigen)], sems.at[slot]
            )
            copy.start()
            copies.append(copy)
    for copy in copies:
        copy.wait()


def contract(places, pieces, partial, source, op_index, slots, blocks):
    _, products, _, own2, local_cols = blocks[0].shape
    n_cols = len(blocks)
    eigen = partial.shape[2]
    order = n_cols * local_cols
    times = order // eigen
    vmem = pl.BlockSpec(memory_space=pltpu.VMEM)
    smem = pl.BlockSpec(memory_space=pltpu.SMEM)
    return pl.pallas_call(
        functools.partial(contract_kernel, places, n_cols),
        in_specs=[smem, smem] + [vmem] * (2 + len(pieces) + n_cols),
        out_specs=pl.BlockSpec(memory_space=pl.ANY),
        out_shape=jax.ShapeDtypeStruct((products, NS, own2 // 2, 2, order), BF16),
        scratch_shapes=[
            pltpu.VMEM((products, 2 * eigen, eigen), BF16),
            pltpu.VMEM((products * times, NS, own2 // 2, 2, eigen), BF16),
            pltpu.SemaphoreType.DMA((products * times,)),
        ],
        compiler_params=pltpu.CompilerParams(vmem_limit_bytes=VMEM_LIMIT),
        cost_estimate=pl.CostEstimate(
            flops=4 * products * eigen * NS * own2 * order, bytes_accessed=0, transcendentals=0
        ),
        name="contract",
    )(source, op_index, slots, partial, *pieces, *blocks)


def swap(array, axis, size, mask):
    return lax.ppermute(array, axis, [(i, i ^ mask) for i in range(size)])


def after(array, *others):
    return lax.optimization_barrier((array, *others))[0]


def per_device(peramb, sink_ops, op_table, row_slot, pair_source, op_index, listed_rows):
    n_cols = lax.axis_size("col")
    n_pair = lax.axis_size("tpair")
    rows, _, eigen = op_table.shape
    slots = row_slot.reshape(-1, LANES)

    def across(array, mask):
        return swap(array, "tpair", n_pair, mask)

    def beside(array):
        return swap(array, "col", n_cols, 1)

    if n_cols != 4 or n_pair != 8 or rows % 32:
        own = jnp.concatenate([op_table[:, 0], op_table[:, 1]], axis=1)
        whole = lax.all_gather(own, "tpair", axis=0, tiled=True)
        half = whole.shape[0] // 2
        mixed = mix(op_index, listed_rows, sink_ops, peramb, [1] * n_cols)
        blocks = [mixed[0]] + [swap(mixed[j], "col", n_cols, j) for j in range(1, n_cols)]
        partial = assemble([0], [whole[:half]], pair_source, op_index, slots, eigen)
        return contract(
            [half], [whole[half:]], partial, pair_source, op_index, slots, blocks
        )
    half = rows // 2
    own = lax.dynamic_slice_in_dim(op_table, lax.axis_index("col") % 2 * half, half, 0)
    own = jnp.concatenate([own[:, 0], own[:, 1]], axis=1)
    held = {(0, 0): own}
    for mask in (4, 2, 1):
        held[mask, 0] = across(own, mask)
    mixed = mix(op_index, listed_rows, sink_ops, peramb, [1] * n_cols)
    for mask in (0, 1, 2, 4):
        held[mask, 1] = beside(after(held[mask, 0], mixed[0]))
    cross = swap(mixed[3], "col", n_cols, 2)
    straight = swap(after(mixed[2], cross), "col", n_cols, 2)
    blocks = [mixed[0], beside(mixed[1]), straight, beside(cross)]
    held[3, 0] = across(after(held[2, 0], mixed[0], held[2, 1], held[1, 1]), 1)
    held[6, 0] = across(after(own, mixed[0]), 6)
    held[5, 0] = across(after(held[4, 0], mixed[0], held[4, 1]), 1)
    held[7, 0] = across(after(held[6, 0], held[5, 0]), 1)
    for mask in (3, 5, 6):
        held[mask, 1] = beside(held[mask, 0])
    early = [(mask, side) for mask in range(7) for side in (0, 1)]
    partial = assemble(early, [held[p] for p in early], pair_source, op_index, slots, eigen)
    held[7, 1] = beside(after(held[7, 0], partial))
    late = [(7, 0), (7, 1)]
    return contract(
        late, [held[p] for p in late], partial, pair_source, op_index, slots, blocks
    )


def solution(mesh):
    in_specs = (
        P("tpair", None, None, "col"),
        P("tpair", None, None, None, None),
        P("tpair", None, None),
        P(),
        P("tpair"),
        P("tpair", None),
        P("tpair", None),
    )
    out_specs = P("tpair", None, "col", None, None)
    return jax.shard_map(
        per_device, mesh=mesh, in_specs=in_specs, out_specs=out_specs, check_vma=False
    )
```

```python
import functools

import jax
import jax.numpy as jnp
from jax import lax
from jax.experimental import pallas as pl
from jax.experimental.pallas import tpu as pltpu
from jax.sharding import PartitionSpec as P

NS = 4
LANES = 128
VMEM_LIMIT = 24 * 1024 * 1024
BF16, F32 = jnp.bfloat16, jnp.float32


def iota(shape, dim):
    return lax.broadcasted_iota(jnp.int32, shape, dim)


def dot(a, b):
    return jnp.dot(a, b, preferred_element_type=F32)


def column(row):
    wide = jnp.broadcast_to(row, (LANES, LANES)).astype(F32)
    return jnp.transpose(wide).astype(jnp.int32)


def one_hot(col, first, width):
    tiles = [
        jnp.where(col - (first + n) == iota((col.shape[0], LANES), 1), 1.0, 0.0)
        for n in range(0, width, LANES)
    ]
    return jnp.concatenate(tiles, axis=1).astype(BF16)


def mix_kernel(op_ref, listed_ref, sink_ref, peramb_ref, *refs):
    outs, (left, held, sems) = refs[:-3], refs[-3:]
    n_cols = sum(out.shape[0] for out in outs)
    products, listed = listed_ref.shape
    eigen, local_cols = sink_ref.shape[-1], peramb_ref.shape[-1]
    loads = [
        pltpu.make_async_copy(
            peramb_ref.at[0, :, pl.ds(s * eigen, eigen), :], held.at[s], sems.at[s]
        )
        for s in range(NS)
    ]
    for load in loads:
        load.start()
    own2 = 2 * listed // n_cols
    me = lax.axis_index("col")
    row = iota((2 * listed, 2 * listed), 0)
    wanted = ((row // own2) ^ me) * (own2 // 2) + (row % own2) // 2 + (row % 2) * listed
    order = jnp.where(wanted == iota((2 * listed, 2 * listed), 1), 1.0, 0.0).astype(BF16)
    for k in range(products):
        op = op_ref[k, 0]
        onehot = one_hot(column(listed_ref[k : k + 1, :]), 0, eigen)
        real = dot(onehot, sink_ref[0, op, 0])
        imag = dot(onehot, sink_ref[0, op, 1])
        top = jnp.concatenate([real, -imag], axis=1)
        bottom = jnp.concatenate([imag, real], axis=1)
        both = jnp.concatenate([top, bottom], axis=0).astype(BF16)
        rows = dot(order, both).astype(BF16)
        for j in range(n_cols):
            at = (j * products + k) * own2
            left[at : at + own2, :] = rows[j * own2 : (j + 1) * own2]
    for s in range(NS):
        loads[s].wait()
        mixed = dot(left[...], held[s].reshape(2 * eigen, local_cols)).astype(BF16)
        j = 0
        for out in outs:
            for n in range(out.shape[0]):
                for k in range(products):
                    at = (j * products + k) * own2
                    out[n, k, s] = mixed[at : at + own2]
                j += 1


def mix(op_index, listed_rows, sink_ops, peramb, groups):
    products, listed = listed_rows.shape
    eigen = sink_ops.shape[-1]
    local_cols = peramb.shape[3]
    own2 = 2 * listed // sum(groups)
    blocks = [
        jax.ShapeDtypeStruct((group, products, NS, own2, local_cols), BF16) for group in groups
    ]
    vmem = pl.BlockSpec(memory_space=pltpu.VMEM)
    return pl.pallas_call(
        mix_kernel,
        in_specs=[
            pl.BlockSpec(memory_space=pltpu.SMEM), vmem, vmem, pl.BlockSpec(memory_space=pltpu.HBM)
        ],
        out_specs=[vmem] * len(groups),
        out_shape=blocks,
        scratch_shapes=[
            pltpu.VMEM((products * 2 * listed, 2 * eigen), BF16),
            pltpu.VMEM((NS, 2, eigen, local_cols), BF16),
            pltpu.SemaphoreType.DMA((NS,)),
        ],
        compiler_params=pltpu.CompilerParams(vmem_limit_bytes=VMEM_LIMIT),
        cost_estimate=pl.CostEstimate(flops=1000, bytes_accessed=1000, transcendentals=0),
        name="mix",
    )(op_index, listed_rows, sink_ops, pltpu.with_memory_space_constraint(peramb, pltpu.HBM))


def add_pieces(places, scalars_ref, slot_ref, pieces, products, eigen):
    source_ref, op_ref = scalars_ref
    blocks = eigen // LANES
    nops = slot_ref.shape[0] // blocks // 2
    pair, side = lax.axis_index("tpair"), lax.axis_index("col") % 2
    cols = []
    for k in range(products):
        op = source_ref[0] * nops + op_ref[k, 1]
        cols += [
            column(slot_ref[pl.ds(op * blocks + b, 1), :]) for b in range(blocks)
        ]
    col = jnp.concatenate(cols, axis=0)
    tiles, tables = [], []
    for place, piece in zip(places, pieces):
        height = piece.shape[0]
        first = place
        if isinstance(place, tuple):
            first = (2 * (pair ^ place[0]) + (side ^ place[1])) * height
        tiles.append(one_hot(col, first, height))
        tables.append(piece[...])
    return dot(jnp.concatenate(tiles, axis=1), jnp.concatenate(tables, axis=0))


def assemble_kernel(places, source_ref, op_ref, slot_ref, *refs):
    pieces, out_ref = refs[:-1], refs[-1]
    products, eigen = out_ref.shape[0], out_ref.shape[2]
    total = add_pieces(places, (source_ref, op_ref), slot_ref, pieces, products, eigen)
    total = total.astype(BF16)
    for k in range(products):
        rows = slice(k * eigen, (k + 1) * eigen)
        out_ref[k, :eigen] = total[rows, :eigen]
        out_ref[k, eigen:] = total[rows, eigen:]


def assemble(places, pieces, source, op_index, slots, eigen):
    products = op_index.shape[0]
    vmem = pl.BlockSpec(memory_space=pltpu.VMEM)
    smem = pl.BlockSpec(memory_space=pltpu.SMEM)
    return pl.pallas_call(
        functools.partial(assemble_kernel, places),
        in_specs=[smem, smem] + [vmem] * (1 + len(pieces)),
        out_specs=vmem,
        out_shape=jax.ShapeDtypeStruct((products, 2 * eigen, eigen), BF16),
        compiler_params=pltpu.CompilerParams(vmem_limit_bytes=VMEM_LIMIT),
        cost_estimate=pl.CostEstimate(flops=1000, bytes_accessed=1000, transcendentals=0),
        name="assemble",
    )(source, op_index, slots, *pieces)


def block_rows(parts, k):
    if len(parts) == 1:
        found = [parts[0][0, k]]
    else:
        per = NS // parts[0].shape[2]
        found = [part[0, 0] for part in parts[k * per : (k + 1) * per]]
    return jnp.concatenate([f.reshape(-1, f.shape[-1]) for f in found], axis=0)


def contract_kernel(places, counts, source_ref, op_ref, slot_ref, partial_ref, *refs):
    n_pieces = len(places)
    pieces, refs = refs[:n_pieces], refs[n_pieces:]
    blocks = []
    for count in counts:
        blocks.append(refs[:count])
        refs = refs[count:]
    n_cols = len(blocks)
    out_ref, right, done, sems = refs
    own2, local_cols = blocks[0][0].shape[3:]
    products, eigen = right.shape[0], right.shape[2]
    rows = NS * own2
    total = add_pieces(places, (source_ref, op_ref), slot_ref, pieces, products, eigen)
    total = total.astype(BF16)
    for p in range(products):
        some = slice(p * eigen, (p + 1) * eigen)
        right[p, :eigen] = partial_ref[p, :eigen] + total[some, :eigen]
        right[p, eigen:] = partial_ref[p, eigen:] + total[some, eigen:]
    me = lax.axis_index("col")
    per_time = eigen // local_cols
    times = n_cols // per_time
    odd = iota((rows, local_cols), 0) % 2 == 1
    copies = []
    for k in range(products):
        direct, turned = [], []
        for j in range(n_cols):
            x = block_rows(blocks[j], k)
            wide = x.astype(F32)
            y = jnp.where(odd, pltpu.roll(wide, 1, 0), -pltpu.roll(wide, rows - 1, 0))
            direct.append(x)
            turned.append(y.astype(BF16))
        if per_time == 1:
            lhs = jnp.concatenate(
                [jnp.concatenate(direct, axis=0), jnp.concatenate(turned, axis=0)], axis=1
            )
            result = dot(lhs, right[k])
        else:
            result = []
            for j in range(n_cols):
                first = pl.multiple_of(((me ^ j) % per_time) * local_cols, local_cols)
                second = pl.multiple_of(eigen + first, local_cols)
                part = dot(direct[j], right[k, pl.ds(first, local_cols), :])
                part += dot(turned[j], right[k, pl.ds(second, local_cols), :])
                if j % per_time:
                    result[-1] += part
                else:
                    result.append(part)
            result = jnp.concatenate(result, axis=0)
        result = result.astype(BF16)
        for g in range(times):
            slot = k * times + g
            block = result[g * rows : (g + 1) * rows]
            done[slot] = block.reshape(NS, own2 // 2, 2, eigen)
            at = pl.multiple_of(((me ^ (g * per_time)) // per_time) * eigen, eigen)
            copy = pltpu.make_async_copy(
                done.at[slot], out_ref.at[k, :, :, :, pl.ds(at, eigen)], sems.at[slot]
            )
            copy.start()
            copies.append(copy)
    for copy in copies:
        copy.wait()


def contract(places, pieces, partial, source, op_index, slots, blocks):
    _, products, _, own2, local_cols = blocks[0][0].shape
    n_cols = len(blocks)
    parts = [part for block in blocks for part in block]
    eigen = partial.shape[2]
    order = n_cols * local_cols
    times = order // eigen
    vmem = pl.BlockSpec(memory_space=pltpu.VMEM)
    smem = pl.BlockSpec(memory_space=pltpu.SMEM)
    return pl.pallas_call(
        functools.partial(contract_kernel, places, [len(block) for block in blocks]),
        in_specs=[smem, smem] + [vmem] * (2 + len(pieces) + len(parts)),
        out_specs=pl.BlockSpec(memory_space=pl.ANY),
        out_shape=jax.ShapeDtypeStruct((products, NS, own2 // 2, 2, order), BF16),
        scratch_shapes=[
            pltpu.VMEM((products, 2 * eigen, eigen), BF16),
            pltpu.VMEM((products * times, NS, own2 // 2, 2, eigen), BF16),
            pltpu.SemaphoreType.DMA((products * times,)),
        ],
        compiler_params=pltpu.CompilerParams(vmem_limit_bytes=VMEM_LIMIT),
        cost_estimate=pl.CostEstimate(
            flops=4 * products * eigen * NS * own2 * order, bytes_accessed=0, transcendentals=0
        ),
        name="contract",
    )(source, op_index, slots, partial, *pieces, *parts)


def swap(array, axis, size, mask):
    return lax.ppermute(array, axis, [(i, i ^ mask) for i in range(size)])


def after(array, *others):
    return lax.optimization_barrier((array, *others))[0]


def per_device(peramb, sink_ops, op_table, row_slot, pair_source, op_index, listed_rows):
    n_cols = lax.axis_size("col")
    n_pair = lax.axis_size("tpair")
    rows, _, eigen = op_table.shape
    slots = row_slot.reshape(-1, LANES)

    def across(array, mask):
        return swap(array, "tpair", n_pair, mask)

    def beside(array):
        return swap(array, "col", n_cols, 1)

    if n_cols != 4 or n_pair != 8 or rows % 32:
        own = jnp.concatenate([op_table[:, 0], op_table[:, 1]], axis=1)
        whole = lax.all_gather(own, "tpair", axis=0, tiled=True)
        half = whole.shape[0] // 2
        mixed = mix(op_index, listed_rows, sink_ops, peramb, [1] * n_cols)
        blocks = [[mixed[0]]] + [[swap(mixed[j], "col", n_cols, j)] for j in range(1, n_cols)]
        partial = assemble([0], [whole[:half]], pair_source, op_index, slots, eigen)
        return contract(
            [half], [whole[half:]], partial, pair_source, op_index, slots, blocks
        )
    half = rows // 2
    own = lax.dynamic_slice_in_dim(op_table, lax.axis_index("col") % 2 * half, half, 0)
    own = jnp.concatenate([own[:, 0], own[:, 1]], axis=1)
    held = {(0, 0): own}
    for mask in (4, 2, 1):
        held[mask, 0] = across(own, mask)
    mixed = mix(op_index, listed_rows, sink_ops, peramb, [1, 1, 2])
    crossed = swap(mixed[2], "col", n_cols, 2)
    halves = [
        beside(crossed[1:, k : k + 1, s : s + NS // 2])
        for k in range(mixed[2].shape[1])
        for s in (0, NS // 2)
    ]
    blocks = [[mixed[0]], [beside(mixed[1])], [crossed], halves]
    for mask in (0, 1, 2, 4):
        held[mask, 1] = beside(after(held[mask, 0], mixed[0]))
    held[3, 0] = across(after(held[2, 0], mixed[0], held[1, 0]), 1)
    held[6, 0] = across(after(own, mixed[0]), 6)
    held[6, 1] = beside(held[6, 0])
    held[5, 0] = across(after(held[4, 0], held[4, 1], held[3, 0]), 1)
    held[7, 0] = across(after(held[6, 0], held[6, 1], held[5, 0]), 1)
    for mask in (3, 5):
        held[mask, 1] = beside(held[mask, 0])
    early = [(mask, side) for mask in range(7) for side in (0, 1)]
    partial = assemble(early, [held[p] for p in early], pair_source, op_index, slots, eigen)
    held[7, 1] = beside(after(held[7, 0], partial))
    late = [(7, 0), (7, 1)]
    return contract(
        late, [held[p] for p in late], partial, pair_source, op_index, slots, blocks
    )


def solution(mesh):
    in_specs = (
        P("tpair", None, None, "col"),
        P("tpair", None, None, None, None),
        P("tpair", None, None),
        P(),
        P("tpair"),
        P("tpair", None),
        P("tpair", None),
    )
    out_specs = P("tpair", None, "col", None, None)
    return jax.shard_map(
        per_device, mesh=mesh, in_specs=in_specs, out_specs=out_specs, check_vma=False
    )
```

```python
import functools

import jax
import jax.numpy as jnp
from jax import lax
from jax.experimental import pallas as pl
from jax.experimental.pallas import tpu as pltpu
from jax.sharding import PartitionSpec as P

NS = 4
LANES = 128
VMEM_LIMIT = 24 * 1024 * 1024
BF16, F32 = jnp.bfloat16, jnp.float32


def iota(shape, dim):
    return lax.broadcasted_iota(jnp.int32, shape, dim)


def dot(a, b):
    return jnp.dot(a, b, preferred_element_type=F32)


def column(row):
    wide = jnp.broadcast_to(row, (LANES, LANES)).astype(F32)
    return jnp.transpose(wide).astype(jnp.int32)


def one_hot(col, first, width):
    tiles = [
        jnp.where(col - (first + n) == iota((col.shape[0], LANES), 1), 1.0, 0.0)
        for n in range(0, width, LANES)
    ]
    return jnp.concatenate(tiles, axis=1).astype(BF16)


def mix_kernel(op_ref, listed_ref, sink_ref, peramb_ref, *refs):
    outs, (left, held, sems) = refs[:-3], refs[-3:]
    n_cols = sum(out.shape[0] for out in outs)
    products, listed = listed_ref.shape
    eigen, local_cols = sink_ref.shape[-1], peramb_ref.shape[-1]
    loads = [
        pltpu.make_async_copy(
            peramb_ref.at[0, :, pl.ds(s * eigen, eigen), :], held.at[s], sems.at[s]
        )
        for s in range(NS)
    ]
    for load in loads:
        load.start()
    own2 = 2 * listed // n_cols
    me = lax.axis_index("col")
    row = iota((2 * listed, 2 * listed), 0)
    wanted = ((row // own2) ^ me) * (own2 // 2) + (row % own2) // 2 + (row % 2) * listed
    order = jnp.where(wanted == iota((2 * listed, 2 * listed), 1), 1.0, 0.0).astype(BF16)
    for k in range(products):
        op = op_ref[k, 0]
        onehot = one_hot(column(listed_ref[k : k + 1, :]), 0, eigen)
        real = dot(onehot, sink_ref[0, op, 0])
        imag = dot(onehot, sink_ref[0, op, 1])
        top = jnp.concatenate([real, -imag], axis=1)
        bottom = jnp.concatenate([imag, real], axis=1)
        both = jnp.concatenate([top, bottom], axis=0).astype(BF16)
        rows = dot(order, both).astype(BF16)
        for j in range(n_cols):
            at = (j * products + k) * own2
            left[at : at + own2, :] = rows[j * own2 : (j + 1) * own2]
    for s in range(NS):
        loads[s].wait()
        mixed = dot(left[...], held[s].reshape(2 * eigen, local_cols)).astype(BF16)
        j = 0
        for out in outs:
            for n in range(out.shape[0]):
                for k in range(products):
                    at = (j * products + k) * own2
                    out[n, k, s] = mixed[at : at + own2]
                j += 1


def mix(op_index, listed_rows, sink_ops, peramb, groups):
    products, listed = listed_rows.shape
    eigen = sink_ops.shape[-1]
    local_cols = peramb.shape[3]
    own2 = 2 * listed // sum(groups)
    blocks = [
        jax.ShapeDtypeStruct((group, products, NS, own2, local_cols), BF16) for group in groups
    ]
    vmem = pl.BlockSpec(memory_space=pltpu.VMEM)
    return pl.pallas_call(
        mix_kernel,
        in_specs=[
            pl.BlockSpec(memory_space=pltpu.SMEM), vmem, vmem, pl.BlockSpec(memory_space=pltpu.HBM)
        ],
        out_specs=[vmem] * len(groups),
        out_shape=blocks,
        scratch_shapes=[
            pltpu.VMEM((products * 2 * listed, 2 * eigen), BF16),
            pltpu.VMEM((NS, 2, eigen, local_cols), BF16),
            pltpu.SemaphoreType.DMA((NS,)),
        ],
        compiler_params=pltpu.CompilerParams(vmem_limit_bytes=VMEM_LIMIT),
        cost_estimate=pl.CostEstimate(flops=1000, bytes_accessed=1000, transcendentals=0),
        name="mix",
    )(op_index, listed_rows, sink_ops, pltpu.with_memory_space_constraint(peramb, pltpu.HBM))


def add_pieces(places, scalars_ref, slot_ref, pieces, products, eigen):
    source_ref, op_ref = scalars_ref
    blocks = eigen // LANES
    nops = slot_ref.shape[0] // blocks // 2
    pair, side = lax.axis_index("tpair"), lax.axis_index("col") % 2
    cols = []
    for k in range(products):
        op = source_ref[0] * nops + op_ref[k, 1]
        cols += [
            column(slot_ref[pl.ds(op * blocks + b, 1), :]) for b in range(blocks)
        ]
    col = jnp.concatenate(cols, axis=0)
    tiles, tables = [], []
    for place, parts in zip(places, pieces):
        height = sum(part.shape[0] for part in parts)
        first = place
        if isinstance(place, tuple):
            first = (2 * (pair ^ place[0]) + (side ^ place[1])) * height
        tiles.append(one_hot(col, first, height))
        tables += [part[...] for part in parts]
    return dot(jnp.concatenate(tiles, axis=1), jnp.concatenate(tables, axis=0))


def grouped(counts, refs):
    groups = []
    for count in counts:
        groups.append(refs[:count])
        refs = refs[count:]
    return groups, refs


def assemble_kernel(places, counts, source_ref, op_ref, slot_ref, *refs):
    pieces, (out_ref,) = grouped(counts, refs)
    products, eigen = out_ref.shape[0], out_ref.shape[2]
    total = add_pieces(places, (source_ref, op_ref), slot_ref, pieces, products, eigen)
    total = total.astype(BF16)
    for k in range(products):
        rows = slice(k * eigen, (k + 1) * eigen)
        out_ref[k, :eigen] = total[rows, :eigen]
        out_ref[k, eigen:] = total[rows, eigen:]


def assemble(places, pieces, source, op_index, slots, eigen):
    products = op_index.shape[0]
    vmem = pl.BlockSpec(memory_space=pltpu.VMEM)
    smem = pl.BlockSpec(memory_space=pltpu.SMEM)
    return pl.pallas_call(
        functools.partial(assemble_kernel, places, [len(group) for group in pieces]),
        in_specs=[smem, smem] + [vmem] * (1 + sum(len(group) for group in pieces)),
        out_specs=vmem,
        out_shape=jax.ShapeDtypeStruct((products, 2 * eigen, eigen), BF16),
        compiler_params=pltpu.CompilerParams(vmem_limit_bytes=VMEM_LIMIT),
        cost_estimate=pl.CostEstimate(flops=1000, bytes_accessed=1000, transcendentals=0),
        name="assemble",
    )(source, op_index, slots, *[part for group in pieces for part in group])


def block_rows(parts, k):
    if len(parts) == 1:
        found = [parts[0][0, k]]
    else:
        per = NS // parts[0].shape[2]
        found = [part[0, 0] for part in parts[k * per : (k + 1) * per]]
    return jnp.concatenate([f.reshape(-1, f.shape[-1]) for f in found], axis=0)


def contract_kernel(places, counts, source_ref, op_ref, slot_ref, partial_ref, *refs):
    groups, (out_ref, right, done, sems) = grouped(counts, refs)
    pieces, blocks = groups[: len(places)], groups[len(places) :]
    n_cols = len(blocks)
    own2, local_cols = blocks[0][0].shape[3:]
    products, eigen = right.shape[0], right.shape[2]
    rows = NS * own2
    total = add_pieces(places, (source_ref, op_ref), slot_ref, pieces, products, eigen)
    total = total.astype(BF16)
    for p in range(products):
        some = slice(p * eigen, (p + 1) * eigen)
        right[p, :eigen] = partial_ref[p, :eigen] + total[some, :eigen]
        right[p, eigen:] = partial_ref[p, eigen:] + total[some, eigen:]
    me = lax.axis_index("col")
    per_time = eigen // local_cols
    times = n_cols // per_time
    odd = iota((rows, local_cols), 0) % 2 == 1
    copies = []
    for k in range(products):
        direct, turned = [], []
        for j in range(n_cols):
            x = block_rows(blocks[j], k)
            wide = x.astype(F32)
            y = jnp.where(odd, pltpu.roll(wide, 1, 0), -pltpu.roll(wide, rows - 1, 0))
            direct.append(x)
            turned.append(y.astype(BF16))
        if per_time == 1:
            lhs = jnp.concatenate(
                [jnp.concatenate(direct, axis=0), jnp.concatenate(turned, axis=0)], axis=1
            )
            result = dot(lhs, right[k])
        else:
            result = []
            for j in range(n_cols):
                first = pl.multiple_of(((me ^ j) % per_time) * local_cols, local_cols)
                second = pl.multiple_of(eigen + first, local_cols)
                part = dot(direct[j], right[k, pl.ds(first, local_cols), :])
                part += dot(turned[j], right[k, pl.ds(second, local_cols), :])
                if j % per_time:
                    result[-1] += part
                else:
                    result.append(part)
            result = jnp.concatenate(result, axis=0)
        result = result.astype(BF16)
        for g in range(times):
            slot = k * times + g
            block = result[g * rows : (g + 1) * rows]
            done[slot] = block.reshape(NS, own2 // 2, 2, eigen)
            at = pl.multiple_of(((me ^ (g * per_time)) // per_time) * eigen, eigen)
            copy = pltpu.make_async_copy(
                done.at[slot], out_ref.at[k, :, :, :, pl.ds(at, eigen)], sems.at[slot]
            )
            copy.start()
            copies.append(copy)
    for copy in copies:
        copy.wait()


def contract(places, pieces, partial, source, op_index, slots, blocks):
    _, products, _, own2, local_cols = blocks[0][0].shape
    n_cols = len(blocks)
    groups = pieces + blocks
    parts = [part for group in groups for part in group]
    eigen = partial.shape[2]
    order = n_cols * local_cols
    times = order // eigen
    vmem = pl.BlockSpec(memory_space=pltpu.VMEM)
    smem = pl.BlockSpec(memory_space=pltpu.SMEM)
    return pl.pallas_call(
        functools.partial(contract_kernel, places, [len(group) for group in groups]),
        in_specs=[smem, smem] + [vmem] * (2 + len(parts)),
        out_specs=pl.BlockSpec(memory_space=pl.ANY),
        out_shape=jax.ShapeDtypeStruct((products, NS, own2 // 2, 2, order), BF16),
        scratch_shapes=[
            pltpu.VMEM((products, 2 * eigen, eigen), BF16),
            pltpu.VMEM((products * times, NS, own2 // 2, 2, eigen), BF16),
            pltpu.SemaphoreType.DMA((products * times,)),
        ],
        compiler_params=pltpu.CompilerParams(vmem_limit_bytes=VMEM_LIMIT),
        cost_estimate=pl.CostEstimate(
            flops=4 * products * eigen * NS * own2 * order, bytes_accessed=0, transcendentals=0
        ),
        name="contract",
    )(source, op_index, slots, partial, *parts)


def swap(array, axis, size, mask):
    return lax.ppermute(array, axis, [(i, i ^ mask) for i in range(size)])


def after(array, *others):
    return lax.optimization_barrier((array, *others))[0]


def per_device(peramb, sink_ops, op_table, row_slot, pair_source, op_index, listed_rows):
    n_cols = lax.axis_size("col")
    n_pair = lax.axis_size("tpair")
    rows, _, eigen = op_table.shape
    slots = row_slot.reshape(-1, LANES)

    def across(array, mask):
        return swap(array, "tpair", n_pair, mask)

    def beside(array):
        return swap(array, "col", n_cols, 1)

    if n_cols != 4 or n_pair != 8 or rows % 32:
        own = jnp.concatenate([op_table[:, 0], op_table[:, 1]], axis=1)
        whole = lax.all_gather(own, "tpair", axis=0, tiled=True)
        half = whole.shape[0] // 2
        mixed = mix(op_index, listed_rows, sink_ops, peramb, [1] * n_cols)
        blocks = [[mixed[0]]] + [[swap(mixed[j], "col", n_cols, j)] for j in range(1, n_cols)]
        partial = assemble([0], [[whole[:half]]], pair_source, op_index, slots, eigen)
        return contract(
            [half], [[whole[half:]]], partial, pair_source, op_index, slots, blocks
        )
    half = rows // 2
    own = lax.dynamic_slice_in_dim(op_table, lax.axis_index("col") % 2 * half, half, 0)
    own = jnp.concatenate([own[:, 0], own[:, 1]], axis=1)
    held = {(0, 0): own}
    for mask in (4, 2, 1):
        held[mask, 0] = across(own, mask)
    mixed = mix(op_index, listed_rows, sink_ops, peramb, [1, 1, 2])
    crossed = swap(mixed[2], "col", n_cols, 2)
    halves = [beside(crossed[1:, k : k + 1]) for k in range(mixed[2].shape[1])]
    blocks = [[mixed[0]], [beside(mixed[1])], [crossed], halves]
    for mask in (0, 1, 2, 4):
        held[mask, 1] = beside(after(held[mask, 0], mixed[0]))
    held[3, 0] = across(after(held[2, 0], mixed[0], held[1, 0]), 1)
    held[6, 0] = across(after(own, mixed[0]), 6)
    held[6, 1] = beside(held[6, 0])
    held[5, 0] = across(after(held[4, 0], held[4, 1], held[3, 0]), 1)
    held[7, 0] = across(after(held[6, 0], held[5, 0]), 1)
    for mask in (3, 5):
        held[mask, 1] = beside(held[mask, 0])
    early = [(mask, side) for mask in range(7) for side in (0, 1)]
    held = {p: pieces if isinstance(pieces, list) else [pieces] for p, pieces in held.items()}
    partial = assemble(early, [held[p] for p in early], pair_source, op_index, slots, eigen)
    held[7, 1] = [beside(after(held[7, 0][0], partial))]
    late = [(7, 0), (7, 1)]
    return contract(
        late, [held[p] for p in late], partial, pair_source, op_index, slots, blocks
    )


def solution(mesh):
    in_specs = (
        P("tpair", None, None, "col"),
        P("tpair", None, None, None, None),
        P("tpair", None, None),
        P(),
        P("tpair"),
        P("tpair", None),
        P("tpair", None),
    )
    out_specs = P("tpair", None, "col", None, None)
    return jax.shard_map(
        per_device, mesh=mesh, in_specs=in_specs, out_specs=out_specs, check_vma=False
    )
```

```python
import functools

import jax
import jax.numpy as jnp
from jax import lax
from jax.experimental import pallas as pl
from jax.experimental.pallas import tpu as pltpu
from jax.sharding import PartitionSpec as P

NS = 4
LANES = 128
VMEM_LIMIT = 24 * 1024 * 1024
BF16, F32 = jnp.bfloat16, jnp.float32


def iota(shape, dim):
    return lax.broadcasted_iota(jnp.int32, shape, dim)


def dot(a, b):
    return jnp.dot(a, b, preferred_element_type=F32)


def column(row):
    wide = jnp.broadcast_to(row, (LANES, LANES)).astype(F32)
    return jnp.transpose(wide).astype(jnp.int32)


def one_hot(col, first, width):
    tiles = [
        jnp.where(col - (first + n) == iota((col.shape[0], LANES), 1), 1.0, 0.0)
        for n in range(0, width, LANES)
    ]
    return jnp.concatenate(tiles, axis=1).astype(BF16)


def mix_kernel(op_ref, listed_ref, sink_ref, peramb_ref, *refs):
    outs, (left, held, sems) = refs[:-3], refs[-3:]
    n_cols = sum(out.shape[0] for out in outs)
    products, listed = listed_ref.shape
    eigen, local_cols = sink_ref.shape[-1], peramb_ref.shape[-1]
    loads = [
        pltpu.make_async_copy(
            peramb_ref.at[0, :, pl.ds(s * eigen, eigen), :], held.at[s], sems.at[s]
        )
        for s in range(NS)
    ]
    for load in loads:
        load.start()
    own2 = 2 * listed // n_cols
    me = lax.axis_index("col")
    row = iota((2 * listed, 2 * listed), 0)
    wanted = ((row // own2) ^ me) * (own2 // 2) + (row % own2) // 2 + (row % 2) * listed
    order = jnp.where(wanted == iota((2 * listed, 2 * listed), 1), 1.0, 0.0).astype(BF16)
    for k in range(products):
        op = op_ref[k, 0]
        onehot = one_hot(column(listed_ref[k : k + 1, :]), 0, eigen)
        real = dot(onehot, sink_ref[0, op, 0])
        imag = dot(onehot, sink_ref[0, op, 1])
        top = jnp.concatenate([real, -imag], axis=1)
        bottom = jnp.concatenate([imag, real], axis=1)
        both = jnp.concatenate([top, bottom], axis=0).astype(BF16)
        rows = dot(order, both).astype(BF16)
        for j in range(n_cols):
            at = (j * products + k) * own2
            left[at : at + own2, :] = rows[j * own2 : (j + 1) * own2]
    for s in range(NS):
        loads[s].wait()
        mixed = dot(left[...], held[s].reshape(2 * eigen, local_cols)).astype(BF16)
        j = 0
        for out in outs:
            for n in range(out.shape[0]):
                for k in range(products):
                    at = (j * products + k) * own2
                    out[n, k, s] = mixed[at : at + own2]
                j += 1


def mix(op_index, listed_rows, sink_ops, peramb, groups):
    products, listed = listed_rows.shape
    eigen = sink_ops.shape[-1]
    local_cols = peramb.shape[3]
    own2 = 2 * listed // sum(groups)
    blocks = [
        jax.ShapeDtypeStruct((group, products, NS, own2, local_cols), BF16) for group in groups
    ]
    vmem = pl.BlockSpec(memory_space=pltpu.VMEM)
    return pl.pallas_call(
        mix_kernel,
        in_specs=[
            pl.BlockSpec(memory_space=pltpu.SMEM), vmem, vmem, pl.BlockSpec(memory_space=pltpu.HBM)
        ],
        out_specs=[vmem] * len(groups),
        out_shape=blocks,
        scratch_shapes=[
            pltpu.VMEM((products * 2 * listed, 2 * eigen), BF16),
            pltpu.VMEM((NS, 2, eigen, local_cols), BF16),
            pltpu.SemaphoreType.DMA((NS,)),
        ],
        compiler_params=pltpu.CompilerParams(vmem_limit_bytes=VMEM_LIMIT),
        cost_estimate=pl.CostEstimate(flops=1000, bytes_accessed=1000, transcendentals=0),
        name="mix",
    )(op_index, listed_rows, sink_ops, pltpu.with_memory_space_constraint(peramb, pltpu.HBM))


def add_pieces(places, scalars_ref, slot_ref, pieces, products, eigen):
    source_ref, op_ref = scalars_ref
    blocks = eigen // LANES
    nops = slot_ref.shape[0] // blocks // 2
    pair, side = lax.axis_index("tpair"), lax.axis_index("col") % 2
    cols = []
    for k in products:
        op = source_ref[0] * nops + op_ref[k, 1]
        cols += [
            column(slot_ref[pl.ds(op * blocks + b, 1), :]) for b in range(blocks)
        ]
    col = jnp.concatenate(cols, axis=0)
    tiles, tables = [], []
    for place, parts in zip(places, pieces):
        height = sum(part.shape[0] for part in parts)
        first = place
        if isinstance(place, tuple):
            first = (2 * (pair ^ place[0]) + (side ^ place[1])) * height
        tiles.append(one_hot(col, first, height))
        tables += [part[...] for part in parts]
    return dot(jnp.concatenate(tiles, axis=1), jnp.concatenate(tables, axis=0))


def grouped(counts, refs):
    groups = []
    for count in counts:
        groups.append(refs[:count])
        refs = refs[count:]
    return groups, refs


def assemble_kernel(places, counts, source_ref, op_ref, slot_ref, *refs):
    pieces, (out_ref,) = grouped(counts, refs)
    products, eigen = out_ref.shape[0], out_ref.shape[2]
    total = add_pieces(places, (source_ref, op_ref), slot_ref, pieces, range(products), eigen)
    total = total.astype(BF16)
    for k in range(products):
        rows = slice(k * eigen, (k + 1) * eigen)
        out_ref[k, :eigen] = total[rows, :eigen]
        out_ref[k, eigen:] = total[rows, eigen:]


def assemble(places, pieces, source, op_index, slots, eigen):
    products = op_index.shape[0]
    vmem = pl.BlockSpec(memory_space=pltpu.VMEM)
    smem = pl.BlockSpec(memory_space=pltpu.SMEM)
    return pl.pallas_call(
        functools.partial(assemble_kernel, places, [len(group) for group in pieces]),
        in_specs=[smem, smem] + [vmem] * (1 + sum(len(group) for group in pieces)),
        out_specs=vmem,
        out_shape=jax.ShapeDtypeStruct((products, 2 * eigen, eigen), BF16),
        compiler_params=pltpu.CompilerParams(vmem_limit_bytes=VMEM_LIMIT),
        cost_estimate=pl.CostEstimate(flops=1000, bytes_accessed=1000, transcendentals=0),
        name="assemble",
    )(source, op_index, slots, *[part for group in pieces for part in group])


def block_rows(parts, k):
    if len(parts) == 1:
        found = [parts[0][0, k]]
    else:
        per = NS // parts[0].shape[2]
        found = [part[0, 0] for part in parts[k * per : (k + 1) * per]]
    return jnp.concatenate([f.reshape(-1, f.shape[-1]) for f in found], axis=0)


def times_right(blocks, masks, right, k):
    eigen = right.shape[2]
    local_cols = blocks[0][0].shape[4]
    me = lax.axis_index("col")
    per_time = eigen // local_cols
    direct = [block_rows(parts, k) for parts in blocks]
    rows = direct[0].shape[0]
    odd = iota((rows, local_cols), 0) % 2 == 1
    turned = []
    for x in direct:
        wide = x.astype(F32)
        y = jnp.where(odd, pltpu.roll(wide, 1, 0), -pltpu.roll(wide, rows - 1, 0))
        turned.append(y.astype(BF16))
    if per_time == 1:
        lhs = jnp.concatenate(
            [jnp.concatenate(direct, axis=0), jnp.concatenate(turned, axis=0)], axis=1
        )
        whole = dot(lhs, right[k]).astype(BF16)
        results = [whole[n * rows : (n + 1) * rows] for n in range(len(masks))]
    else:
        results = []
        for n, mask in enumerate(masks):
            first = pl.multiple_of(((me ^ mask) % per_time) * local_cols, local_cols)
            second = pl.multiple_of(eigen + first, local_cols)
            part = dot(direct[n], right[k, pl.ds(first, local_cols), :])
            part += dot(turned[n], right[k, pl.ds(second, local_cols), :])
            if n % per_time:
                results[-1] += part
            else:
                results.append(part)
        results = [result.astype(BF16) for result in results]
    times = [(me ^ mask) // per_time for mask in masks[::per_time]]
    return list(zip(times, results))


def near_kernel(places, masks, counts, source_ref, op_ref, slot_ref, partial_ref, *refs):
    groups, (right, done) = grouped(counts, refs)
    pieces, blocks = groups[: len(places)], groups[len(places) :]
    products, eigen = right.shape[0], right.shape[2]
    scalars = (source_ref, op_ref)
    for k in range(products):
        total = add_pieces(places, scalars, slot_ref, pieces, [k], eigen).astype(BF16)
        right[k, :eigen] = partial_ref[k, :eigen] + total[:, :eigen]
        right[k, eigen:] = partial_ref[k, eigen:] + total[:, eigen:]
    for k in range(products):
        for n, (_, result) in enumerate(times_right(blocks, masks, right, k)):
            done[k, n] = result.reshape(done.shape[2:])


def far_kernel(near_masks, masks, counts, right, near_ref, *refs):
    blocks, (out_ref, done, near_sems, sems) = grouped(counts, refs)
    products, eigen = right.shape[0], right.shape[2]
    near_times, times = near_ref.shape[1], done.shape[1]
    per_time = len(masks) // times
    me = lax.axis_index("col")

    def send(source, k, time, sem):
        at = pl.multiple_of(time * eigen, eigen)
        copy = pltpu.make_async_copy(source, out_ref.at[k, :, :, :, pl.ds(at, eigen)], sem)
        copy.start()
        return copy

    copies = []
    for k in range(products):
        for n in range(near_times):
            time = (me ^ near_masks[n * per_time]) // per_time
            copies.append(send(near_ref.at[k, n], k, time, near_sems.at[k, n]))
    for k in range(products):
        for n, (time, result) in enumerate(times_right(blocks, masks, right, k)):
            done[k, n] = result.reshape(done.shape[2:])
            copies.append(send(done.at[k, n], k, time, sems.at[k, n]))
    for copy in copies:
        copy.wait()


def flat(groups):
    return [part for group in groups for part in group]


def contract(places, pieces, partial, source, op_index, slots, blocks):
    _, products, _, own2, local_cols = blocks[0][0].shape
    n_cols = len(blocks)
    eigen = partial.shape[2]
    times = n_cols * local_cols // eigen
    near = n_cols // 2
    near_masks, far_masks = list(range(near)), list(range(near, n_cols))
    vmem = pl.BlockSpec(memory_space=pltpu.VMEM)
    smem = pl.BlockSpec(memory_space=pltpu.SMEM)
    params = pltpu.CompilerParams(vmem_limit_bytes=VMEM_LIMIT)
    cost = pl.CostEstimate(
        flops=2 * products * eigen * NS * own2 * n_cols * local_cols,
        bytes_accessed=1000,
        transcendentals=0,
    )
    half = (products, times // 2, NS, own2 // 2, 2, eigen)
    groups = pieces + blocks[:near]
    right, done = pl.pallas_call(
        functools.partial(near_kernel, places, near_masks, [len(g) for g in groups]),
        in_specs=[smem, smem] + [vmem] * (2 + len(flat(groups))),
        out_specs=[vmem, vmem],
        out_shape=[
            jax.ShapeDtypeStruct((products, 2 * eigen, eigen), BF16),
            jax.ShapeDtypeStruct(half, BF16),
        ],
        compiler_params=params,
        cost_estimate=cost,
        name="near",
    )(source, op_index, slots, partial, *flat(groups))
    groups = blocks[near:]
    return pl.pallas_call(
        functools.partial(far_kernel, near_masks, far_masks, [len(g) for g in groups]),
        in_specs=[vmem] * (2 + len(flat(groups))),
        out_specs=pl.BlockSpec(memory_space=pl.ANY),
        out_shape=jax.ShapeDtypeStruct((products, NS, own2 // 2, 2, times * eigen), BF16),
        scratch_shapes=[
            pltpu.VMEM(half, BF16),
            pltpu.SemaphoreType.DMA(half[:2]),
            pltpu.SemaphoreType.DMA(half[:2]),
        ],
        compiler_params=params,
        cost_estimate=cost,
        name="far",
    )(right, done, *flat(groups))


def swap(array, axis, size, mask):
    return lax.ppermute(array, axis, [(i, i ^ mask) for i in range(size)])


def after(array, *others):
    return lax.optimization_barrier((array, *others))[0]


def per_device(peramb, sink_ops, op_table, row_slot, pair_source, op_index, listed_rows):
    n_cols = lax.axis_size("col")
    n_pair = lax.axis_size("tpair")
    rows, _, eigen = op_table.shape
    slots = row_slot.reshape(-1, LANES)

    def across(array, mask):
        return swap(array, "tpair", n_pair, mask)

    def beside(array):
        return swap(array, "col", n_cols, 1)

    if n_cols != 4 or n_pair != 8 or rows % 32:
        own = jnp.concatenate([op_table[:, 0], op_table[:, 1]], axis=1)
        whole = lax.all_gather(own, "tpair", axis=0, tiled=True)
        half = whole.shape[0] // 2
        mixed = mix(op_index, listed_rows, sink_ops, peramb, [1] * n_cols)
        blocks = [[mixed[0]]] + [[swap(mixed[j], "col", n_cols, j)] for j in range(1, n_cols)]
        partial = assemble([0], [[whole[:half]]], pair_source, op_index, slots, eigen)
        return contract(
            [half], [[whole[half:]]], partial, pair_source, op_index, slots, blocks
        )
    half = rows // 2
    own = lax.dynamic_slice_in_dim(op_table, lax.axis_index("col") % 2 * half, half, 0)
    own = jnp.concatenate([own[:, 0], own[:, 1]], axis=1)
    held = {(0, 0): own, (0, 1): beside(own)}
    for mask in (2, 4):
        held[mask, 0] = across(own, mask)
    held[1, 0] = across(after(own, held[0, 1]), 1)
    mixed = mix(op_index, listed_rows, sink_ops, peramb, [1, 1, 2])
    crossed = swap(mixed[2], "col", n_cols, 2)
    halves = [beside(crossed[1:, k : k + 1]) for k in range(mixed[2].shape[1])]
    beside_me = beside(mixed[1])
    blocks = [[mixed[0]], [beside_me], [crossed], halves]
    for mask in (1, 2, 4):
        held[mask, 1] = beside(after(held[mask, 0], mixed[0]))
    held[3, 0] = across(after(held[2, 0], mixed[0], held[1, 0]), 1)
    held[6, 0] = across(after(own, mixed[0]), 6)
    held[6, 1] = beside(held[6, 0])
    held[5, 0] = across(
        after(held[4, 0], held[4, 1], held[3, 0], held[1, 1], beside_me), 1
    )
    held[7, 0] = across(after(held[6, 0], held[5, 0]), 1)
    for mask in (3, 5):
        held[mask, 1] = beside(held[mask, 0])
    early = [(mask, side) for mask in range(7) for side in (0, 1)]
    held = {p: pieces if isinstance(pieces, list) else [pieces] for p, pieces in held.items()}
    partial = assemble(early, [held[p] for p in early], pair_source, op_index, slots, eigen)
    held[7, 1] = [beside(after(held[7, 0][0], partial))]
    late = [(7, 0), (7, 1)]
    return contract(
        late, [held[p] for p in late], partial, pair_source, op_index, slots, blocks
    )


def solution(mesh):
    in_specs = (
        P("tpair", None, None, "col"),
        P("tpair", None, None, None, None),
        P("tpair", None, None),
        P(),
        P("tpair"),
        P("tpair", None),
        P("tpair", None),
    )
    out_specs = P("tpair", None, "col", None, None)
    return jax.shard_map(
        per_device, mesh=mesh, in_specs=in_specs, out_specs=out_specs, check_vma=False
    )
```

```python
import functools

import jax
import jax.numpy as jnp
from jax import lax
from jax.experimental import pallas as pl
from jax.experimental.pallas import tpu as pltpu
from jax.sharding import PartitionSpec as P

NS = 4
LANES = 128
VMEM_LIMIT = 24 * 1024 * 1024
BF16, F32 = jnp.bfloat16, jnp.float32


def iota(shape, dim):
    return lax.broadcasted_iota(jnp.int32, shape, dim)


def dot(a, b):
    return jnp.dot(a, b, preferred_element_type=F32)


def column(row):
    wide = jnp.broadcast_to(row, (LANES, LANES)).astype(F32)
    return jnp.transpose(wide).astype(jnp.int32)


def one_hot(col, first, width):
    tiles = [
        jnp.where(col - (first + n) == iota((col.shape[0], LANES), 1), 1.0, 0.0)
        for n in range(0, width, LANES)
    ]
    return jnp.concatenate(tiles, axis=1).astype(BF16)


def mix_kernel(op_ref, listed_ref, sink_ref, peramb_ref, *refs):
    outs, (left, held, sems) = refs[:-3], refs[-3:]
    n_cols = sum(out.shape[0] for out in outs)
    products, listed = listed_ref.shape
    eigen, local_cols = sink_ref.shape[-1], peramb_ref.shape[-1]
    loads = [
        pltpu.make_async_copy(
            peramb_ref.at[0, :, pl.ds(s * eigen, eigen), :], held.at[s], sems.at[s]
        )
        for s in range(NS)
    ]
    for load in loads:
        load.start()
    own2 = 2 * listed // n_cols
    me = lax.axis_index("col")
    row = iota((2 * listed, 2 * listed), 0)
    wanted = ((row // own2) ^ me) * (own2 // 2) + (row % own2) // 2 + (row % 2) * listed
    order = jnp.where(wanted == iota((2 * listed, 2 * listed), 1), 1.0, 0.0).astype(BF16)
    for k in range(products):
        op = op_ref[k, 0]
        onehot = one_hot(column(listed_ref[k : k + 1, :]), 0, eigen)
        real = dot(onehot, sink_ref[0, op, 0])
        imag = dot(onehot, sink_ref[0, op, 1])
        top = jnp.concatenate([real, -imag], axis=1)
        bottom = jnp.concatenate([imag, real], axis=1)
        both = jnp.concatenate([top, bottom], axis=0).astype(BF16)
        rows = dot(order, both).astype(BF16)
        for j in range(n_cols):
            at = (j * products + k) * own2
            left[at : at + own2, :] = rows[j * own2 : (j + 1) * own2]
    for s in range(NS):
        loads[s].wait()
        mixed = dot(left[...], held[s].reshape(2 * eigen, local_cols)).astype(BF16)
        j = 0
        for out in outs:
            for n in range(out.shape[0]):
                for k in range(products):
                    at = (j * products + k) * own2
                    out[n, k, s] = mixed[at : at + own2]
                j += 1


def mix(op_index, listed_rows, sink_ops, peramb, groups):
    products, listed = listed_rows.shape
    eigen = sink_ops.shape[-1]
    local_cols = peramb.shape[3]
    own2 = 2 * listed // sum(groups)
    blocks = [
        jax.ShapeDtypeStruct((group, products, NS, own2, local_cols), BF16) for group in groups
    ]
    vmem = pl.BlockSpec(memory_space=pltpu.VMEM)
    return pl.pallas_call(
        mix_kernel,
        in_specs=[
            pl.BlockSpec(memory_space=pltpu.SMEM), vmem, vmem, pl.BlockSpec(memory_space=pltpu.HBM)
        ],
        out_specs=[vmem] * len(groups),
        out_shape=blocks,
        scratch_shapes=[
            pltpu.VMEM((products * 2 * listed, 2 * eigen), BF16),
            pltpu.VMEM((NS, 2, eigen, local_cols), BF16),
            pltpu.SemaphoreType.DMA((NS,)),
        ],
        compiler_params=pltpu.CompilerParams(vmem_limit_bytes=VMEM_LIMIT),
        cost_estimate=pl.CostEstimate(flops=1000, bytes_accessed=1000, transcendentals=0),
        name="mix",
    )(op_index, listed_rows, sink_ops, pltpu.with_memory_space_constraint(peramb, pltpu.HBM))


def add_pieces(places, scalars_ref, slot_ref, pieces, products, eigen):
    source_ref, op_ref = scalars_ref
    blocks = eigen // LANES
    nops = slot_ref.shape[0] // blocks // 2
    pair, side = lax.axis_index("tpair"), lax.axis_index("col") % 2
    cols = []
    for k in products:
        op = source_ref[0] * nops + op_ref[k, 1]
        cols += [
            column(slot_ref[pl.ds(op * blocks + b, 1), :]) for b in range(blocks)
        ]
    col = jnp.concatenate(cols, axis=0)
    tiles, tables = [], []
    for owners, parts in zip(places, pieces):
        height = sum(part.shape[0] for part in parts) // len(owners)
        for owner in owners:
            first = owner
            if isinstance(owner, tuple):
                first = (2 * (pair ^ owner[0]) + (side ^ owner[1])) * height
            tiles.append(one_hot(col, first, height))
        tables += [part[...] for part in parts]
    return dot(jnp.concatenate(tiles, axis=1), jnp.concatenate(tables, axis=0))


def grouped(counts, refs):
    groups = []
    for count in counts:
        groups.append(refs[:count])
        refs = refs[count:]
    return groups, refs


def assemble_kernel(places, counts, source_ref, op_ref, slot_ref, *refs):
    pieces, (out_ref,) = grouped(counts, refs)
    products, eigen = out_ref.shape[0], out_ref.shape[2]
    total = add_pieces(places, (source_ref, op_ref), slot_ref, pieces, range(products), eigen)
    total = total.astype(BF16)
    for k in range(products):
        rows = slice(k * eigen, (k + 1) * eigen)
        out_ref[k, :eigen] = total[rows, :eigen]
        out_ref[k, eigen:] = total[rows, eigen:]


def assemble(places, pieces, source, op_index, slots, eigen):
    products = op_index.shape[0]
    vmem = pl.BlockSpec(memory_space=pltpu.VMEM)
    smem = pl.BlockSpec(memory_space=pltpu.SMEM)
    return pl.pallas_call(
        functools.partial(assemble_kernel, places, [len(group) for group in pieces]),
        in_specs=[smem, smem] + [vmem] * (1 + sum(len(group) for group in pieces)),
        out_specs=vmem,
        out_shape=jax.ShapeDtypeStruct((products, 2 * eigen, eigen), BF16),
        compiler_params=pltpu.CompilerParams(vmem_limit_bytes=VMEM_LIMIT),
        cost_estimate=pl.CostEstimate(flops=1000, bytes_accessed=1000, transcendentals=0),
        name="assemble",
    )(source, op_index, slots, *[part for group in pieces for part in group])


def block_rows(parts, k):
    if len(parts) == 1:
        found = [parts[0][0, k]]
    else:
        per = NS // parts[0].shape[2]
        found = [part[0, 0] for part in parts[k * per : (k + 1) * per]]
    return jnp.concatenate([f.reshape(-1, f.shape[-1]) for f in found], axis=0)


def times_right(blocks, masks, right, k):
    eigen = right.shape[2]
    local_cols = blocks[0][0].shape[4]
    me = lax.axis_index("col")
    per_time = eigen // local_cols
    direct = [block_rows(parts, k) for parts in blocks]
    rows = direct[0].shape[0]
    odd = iota((rows, local_cols), 0) % 2 == 1
    turned = []
    for x in direct:
        wide = x.astype(F32)
        y = jnp.where(odd, pltpu.roll(wide, 1, 0), -pltpu.roll(wide, rows - 1, 0))
        turned.append(y.astype(BF16))
    if per_time == 1:
        lhs = jnp.concatenate(
            [jnp.concatenate(direct, axis=0), jnp.concatenate(turned, axis=0)], axis=1
        )
        whole = dot(lhs, right[k]).astype(BF16)
        results = [whole[n * rows : (n + 1) * rows] for n in range(len(masks))]
    else:
        results = []
        for n, mask in enumerate(masks):
            first = pl.multiple_of(((me ^ mask) % per_time) * local_cols, local_cols)
            second = pl.multiple_of(eigen + first, local_cols)
            part = dot(direct[n], right[k, pl.ds(first, local_cols), :])
            part += dot(turned[n], right[k, pl.ds(second, local_cols), :])
            if n % per_time:
                results[-1] += part
            else:
                results.append(part)
        results = [result.astype(BF16) for result in results]
    times = [(me ^ mask) // per_time for mask in masks[::per_time]]
    return list(zip(times, results))


def near_kernel(places, masks, counts, source_ref, op_ref, slot_ref, partial_ref, *refs):
    groups, (right, done) = grouped(counts, refs)
    pieces, blocks = groups[: len(places)], groups[len(places) :]
    products, eigen = right.shape[0], right.shape[2]
    scalars = (source_ref, op_ref)
    for k in range(products):
        total = add_pieces(places, scalars, slot_ref, pieces, [k], eigen).astype(BF16)
        right[k, :eigen] = partial_ref[k, :eigen] + total[:, :eigen]
        right[k, eigen:] = partial_ref[k, eigen:] + total[:, eigen:]
    for k in range(products):
        for n, (_, result) in enumerate(times_right(blocks, masks, right, k)):
            done[k, n] = result.reshape(done.shape[2:])


def far_kernel(near_masks, masks, counts, right, near_ref, *refs):
    blocks, (out_ref, done, near_sems, sems) = grouped(counts, refs)
    products, eigen = right.shape[0], right.shape[2]
    near_times, times = near_ref.shape[1], done.shape[1]
    per_time = len(masks) // times
    me = lax.axis_index("col")

    def send(source, k, time, sem):
        at = pl.multiple_of(time * eigen, eigen)
        copy = pltpu.make_async_copy(source, out_ref.at[k, :, :, :, pl.ds(at, eigen)], sem)
        copy.start()
        return copy

    copies = []
    for k in range(products):
        for n in range(near_times):
            time = (me ^ near_masks[n * per_time]) // per_time
            copies.append(send(near_ref.at[k, n], k, time, near_sems.at[k, n]))
    for k in range(products):
        for n, (time, result) in enumerate(times_right(blocks, masks, right, k)):
            done[k, n] = result.reshape(done.shape[2:])
            copies.append(send(done.at[k, n], k, time, sems.at[k, n]))
    for copy in copies:
        copy.wait()


def flat(groups):
    return [part for group in groups for part in group]


def contract(places, pieces, partial, source, op_index, slots, blocks):
    _, products, _, own2, local_cols = blocks[0][0].shape
    n_cols = len(blocks)
    eigen = partial.shape[2]
    times = n_cols * local_cols // eigen
    near = n_cols // 2
    near_masks, far_masks = list(range(near)), list(range(near, n_cols))
    vmem = pl.BlockSpec(memory_space=pltpu.VMEM)
    smem = pl.BlockSpec(memory_space=pltpu.SMEM)
    params = pltpu.CompilerParams(vmem_limit_bytes=VMEM_LIMIT)
    cost = pl.CostEstimate(
        flops=2 * products * eigen * NS * own2 * n_cols * local_cols,
        bytes_accessed=1000,
        transcendentals=0,
    )
    half = (products, times // 2, NS, own2 // 2, 2, eigen)
    groups = pieces + blocks[:near]
    right, done = pl.pallas_call(
        functools.partial(near_kernel, places, near_masks, [len(g) for g in groups]),
        in_specs=[smem, smem] + [vmem] * (2 + len(flat(groups))),
        out_specs=[vmem, vmem],
        out_shape=[
            jax.ShapeDtypeStruct((products, 2 * eigen, eigen), BF16),
            jax.ShapeDtypeStruct(half, BF16),
        ],
        compiler_params=params,
        cost_estimate=cost,
        name="near",
    )(source, op_index, slots, partial, *flat(groups))
    groups = blocks[near:]
    return pl.pallas_call(
        functools.partial(far_kernel, near_masks, far_masks, [len(g) for g in groups]),
        in_specs=[vmem] * (2 + len(flat(groups))),
        out_specs=pl.BlockSpec(memory_space=pl.ANY),
        out_shape=jax.ShapeDtypeStruct((products, NS, own2 // 2, 2, times * eigen), BF16),
        scratch_shapes=[
            pltpu.VMEM(half, BF16),
            pltpu.SemaphoreType.DMA(half[:2]),
            pltpu.SemaphoreType.DMA(half[:2]),
        ],
        compiler_params=params,
        cost_estimate=cost,
        name="far",
    )(right, done, *flat(groups))


def swap(array, axis, size, mask):
    return lax.ppermute(array, axis, [(i, i ^ mask) for i in range(size)])


def after(array, *others):
    return lax.optimization_barrier((array, *others))[0]


def per_device(peramb, sink_ops, op_table, row_slot, pair_source, op_index, listed_rows):
    n_cols = lax.axis_size("col")
    n_pair = lax.axis_size("tpair")
    rows, _, eigen = op_table.shape
    slots = row_slot.reshape(-1, LANES)

    def across(array, mask):
        return swap(array, "tpair", n_pair, mask)

    def beside(array):
        return swap(array, "col", n_cols, 1)

    if n_cols != 4 or n_pair != 8 or rows % 32:
        own = jnp.concatenate([op_table[:, 0], op_table[:, 1]], axis=1)
        whole = lax.all_gather(own, "tpair", axis=0, tiled=True)
        half = whole.shape[0] // 2
        mixed = mix(op_index, listed_rows, sink_ops, peramb, [1] * n_cols)
        blocks = [[mixed[0]]] + [[swap(mixed[j], "col", n_cols, j)] for j in range(1, n_cols)]
        partial = assemble([[0]], [[whole[:half]]], pair_source, op_index, slots, eigen)
        return contract(
            [[half]], [[whole[half:]]], partial, pair_source, op_index, slots, blocks
        )
    half = rows // 2
    own = lax.dynamic_slice_in_dim(op_table, lax.axis_index("col") % 2 * half, half, 0)
    own = jnp.concatenate([own[:, 0], own[:, 1]], axis=1)
    beside_own = beside(own)
    z2 = across(own, 4)
    z1 = across(own, 2)
    x0 = across(after(own, beside_own), 1)
    mixed = mix(op_index, listed_rows, sink_ops, peramb, [1, 1, 2])
    crossed = swap(mixed[2], "col", n_cols, 2)
    beside_mixed = beside(mixed[1])
    blocks = [[mixed[0]], [beside_mixed], [crossed], [beside(crossed[1:])]]
    beside_x0 = beside(after(x0, mixed[0]))
    z3 = across(after(own, mixed[0]), 6)
    z12 = after(jnp.concatenate([z1, z2]), mixed[0], x0)
    x12 = across(z12, 1)
    x3 = across(after(z3, x12, beside_x0, beside_mixed), 1)
    early = [
        ([(0, 0)], own), ([(0, 1)], beside_own),
        ([(1, 0)], x0), ([(1, 1)], beside_x0),
        ([(2, 0), (4, 0)], z12), ([(2, 1), (4, 1)], beside(z12)),
        ([(6, 0)], z3), ([(6, 1)], beside(z3)),
        ([(3, 0), (5, 0)], x12), ([(3, 1), (5, 1)], beside(x12)),
    ]
    places, pieces = [p for p, _ in early], [[piece] for _, piece in early]
    partial = assemble(places, pieces, pair_source, op_index, slots, eigen)
    late = [[x3], [beside(after(x3, partial))]]
    places = [[(7, 0)], [(7, 1)]]
    return contract(places, late, partial, pair_source, op_index, slots, blocks)


def solution(mesh):
    in_specs = (
        P("tpair", None, None, "col"),
        P("tpair", None, None, None, None),
        P("tpair", None, None),
        P(),
        P("tpair"),
        P("tpair", None),
        P("tpair", None),
    )
    out_specs = P("tpair", None, "col", None, None)
    return jax.shard_map(
        per_device, mesh=mesh, in_specs=in_specs, out_specs=out_specs, check_vma=False
    )
```

```python
import functools

import jax
import jax.numpy as jnp
from jax import lax
from jax.experimental import pallas as pl
from jax.experimental.pallas import tpu as pltpu
from jax.sharding import PartitionSpec as P

NS = 4
LANES = 128
VMEM_LIMIT = 24 * 1024 * 1024
BF16, F32 = jnp.bfloat16, jnp.float32


def iota(shape, dim):
    return lax.broadcasted_iota(jnp.int32, shape, dim)


def dot(a, b):
    return jnp.dot(a, b, preferred_element_type=F32)


def column(row):
    wide = jnp.broadcast_to(row, (LANES, LANES)).astype(F32)
    return jnp.transpose(wide).astype(jnp.int32)


def one_hot(col, first, width):
    tiles = [
        jnp.where(col - (first + n) == iota((col.shape[0], LANES), 1), 1.0, 0.0)
        for n in range(0, width, LANES)
    ]
    return jnp.concatenate(tiles, axis=1).astype(BF16)


def mix_kernel(op_ref, listed_ref, sink_ref, peramb_ref, *refs):
    outs, (left, held, sems) = refs[:-3], refs[-3:]
    n_cols = sum(out.shape[0] for out in outs)
    products, listed = listed_ref.shape
    eigen, local_cols = sink_ref.shape[-1], peramb_ref.shape[-1]
    loads = [
        pltpu.make_async_copy(
            peramb_ref.at[0, :, pl.ds(s * eigen, eigen), :], held.at[s], sems.at[s]
        )
        for s in range(NS)
    ]
    for load in loads:
        load.start()
    own2 = 2 * listed // n_cols
    me = lax.axis_index("col")
    row = iota((2 * listed, 2 * listed), 0)
    wanted = ((row // own2) ^ me) * (own2 // 2) + (row % own2) // 2 + (row % 2) * listed
    order = jnp.where(wanted == iota((2 * listed, 2 * listed), 1), 1.0, 0.0).astype(BF16)
    for k in range(products):
        op = op_ref[k, 0]
        onehot = one_hot(column(listed_ref[k : k + 1, :]), 0, eigen)
        real = dot(onehot, sink_ref[0, op, 0])
        imag = dot(onehot, sink_ref[0, op, 1])
        top = jnp.concatenate([real, -imag], axis=1)
        bottom = jnp.concatenate([imag, real], axis=1)
        both = jnp.concatenate([top, bottom], axis=0).astype(BF16)
        rows = dot(order, both).astype(BF16)
        for j in range(n_cols):
            at = (j * products + k) * own2
            left[at : at + own2, :] = rows[j * own2 : (j + 1) * own2]
    for s in range(NS):
        loads[s].wait()
        mixed = dot(left[...], held[s].reshape(2 * eigen, local_cols)).astype(BF16)
        j = 0
        for out in outs:
            for n in range(out.shape[0]):
                for k in range(products):
                    at = (j * products + k) * own2
                    out[n, k, s] = mixed[at : at + own2]
                j += 1


def mix(op_index, listed_rows, sink_ops, peramb, groups):
    products, listed = listed_rows.shape
    eigen = sink_ops.shape[-1]
    local_cols = peramb.shape[3]
    own2 = 2 * listed // sum(groups)
    blocks = [
        jax.ShapeDtypeStruct((group, products, NS, own2, local_cols), BF16) for group in groups
    ]
    vmem = pl.BlockSpec(memory_space=pltpu.VMEM)
    return pl.pallas_call(
        mix_kernel,
        in_specs=[
            pl.BlockSpec(memory_space=pltpu.SMEM), vmem, vmem, pl.BlockSpec(memory_space=pltpu.HBM)
        ],
        out_specs=[vmem] * len(groups),
        out_shape=blocks,
        scratch_shapes=[
            pltpu.VMEM((products * 2 * listed, 2 * eigen), BF16),
            pltpu.VMEM((NS, 2, eigen, local_cols), BF16),
            pltpu.SemaphoreType.DMA((NS,)),
        ],
        compiler_params=pltpu.CompilerParams(vmem_limit_bytes=VMEM_LIMIT),
        cost_estimate=pl.CostEstimate(flops=1000, bytes_accessed=1000, transcendentals=0),
        name="mix",
    )(op_index, listed_rows, sink_ops, pltpu.with_memory_space_constraint(peramb, pltpu.HBM))


def add_pieces(places, scalars_ref, slot_ref, pieces, products, eigen):
    source_ref, op_ref = scalars_ref
    blocks = eigen // LANES
    nops = slot_ref.shape[0] // blocks // 2
    pair, side = lax.axis_index("tpair"), lax.axis_index("col") % 2
    cols = []
    for k in products:
        op = source_ref[0] * nops + op_ref[k, 1]
        cols += [
            column(slot_ref[pl.ds(op * blocks + b, 1), :]) for b in range(blocks)
        ]
    col = jnp.concatenate(cols, axis=0)
    tiles, tables = [], []
    for owners, parts in zip(places, pieces):
        height = sum(part.shape[0] for part in parts) // len(owners)
        for owner in owners:
            first = owner
            if isinstance(owner, tuple):
                first = (2 * (pair ^ owner[0]) + (side ^ owner[1])) * height
            tiles.append(one_hot(col, first, height))
        tables += [part[...] for part in parts]
    return dot(jnp.concatenate(tiles, axis=1), jnp.concatenate(tables, axis=0))


def grouped(counts, refs):
    groups = []
    for count in counts:
        groups.append(refs[:count])
        refs = refs[count:]
    return groups, refs


def assemble_kernel(places, counts, source_ref, op_ref, slot_ref, *refs):
    pieces, (out_ref,) = grouped(counts, refs)
    products, eigen = out_ref.shape[0], out_ref.shape[2]
    total = add_pieces(places, (source_ref, op_ref), slot_ref, pieces, range(products), eigen)
    total = total.astype(BF16)
    for k in range(products):
        rows = slice(k * eigen, (k + 1) * eigen)
        out_ref[k, :eigen] = total[rows, :eigen]
        out_ref[k, eigen:] = total[rows, eigen:]


def assemble(places, pieces, source, op_index, slots, eigen):
    products = op_index.shape[0]
    vmem = pl.BlockSpec(memory_space=pltpu.VMEM)
    smem = pl.BlockSpec(memory_space=pltpu.SMEM)
    return pl.pallas_call(
        functools.partial(assemble_kernel, places, [len(group) for group in pieces]),
        in_specs=[smem, smem] + [vmem] * (1 + sum(len(group) for group in pieces)),
        out_specs=vmem,
        out_shape=jax.ShapeDtypeStruct((products, 2 * eigen, eigen), BF16),
        compiler_params=pltpu.CompilerParams(vmem_limit_bytes=VMEM_LIMIT),
        cost_estimate=pl.CostEstimate(flops=1000, bytes_accessed=1000, transcendentals=0),
        name="assemble",
    )(source, op_index, slots, *[part for group in pieces for part in group])


def block_rows(parts, k):
    found = [part[0, k] for part in parts]
    return jnp.concatenate([f.reshape(-1, f.shape[-1]) for f in found], axis=0)


def times_right(blocks, masks, right, k):
    eigen = right.shape[2]
    local_cols = blocks[0][0].shape[4]
    me = lax.axis_index("col")
    per_time = eigen // local_cols
    direct = [block_rows(parts, k) for parts in blocks]
    rows = direct[0].shape[0]
    odd = iota((rows, local_cols), 0) % 2 == 1
    turned = []
    for x in direct:
        wide = x.astype(F32)
        y = jnp.where(odd, pltpu.roll(wide, 1, 0), -pltpu.roll(wide, rows - 1, 0))
        turned.append(y.astype(BF16))
    if per_time == 1:
        lhs = jnp.concatenate(
            [jnp.concatenate(direct, axis=0), jnp.concatenate(turned, axis=0)], axis=1
        )
        whole = dot(lhs, right[k]).astype(BF16)
        results = [whole[n * rows : (n + 1) * rows] for n in range(len(masks))]
    else:
        results = []
        for n, mask in enumerate(masks):
            first = pl.multiple_of(((me ^ mask) % per_time) * local_cols, local_cols)
            second = pl.multiple_of(eigen + first, local_cols)
            part = dot(direct[n], right[k, pl.ds(first, local_cols), :])
            part += dot(turned[n], right[k, pl.ds(second, local_cols), :])
            if n % per_time:
                results[-1] += part
            else:
                results.append(part)
        results = [result.astype(BF16) for result in results]
    times = [(me ^ mask) // per_time for mask in masks[::per_time]]
    return list(zip(times, results))


def near_kernel(places, masks, counts, source_ref, op_ref, slot_ref, partial_ref, *refs):
    groups, (right, done) = grouped(counts, refs)
    pieces, blocks = groups[: len(places)], groups[len(places) :]
    products, eigen = right.shape[0], right.shape[2]
    scalars = (source_ref, op_ref)
    for k in range(products):
        total = add_pieces(places, scalars, slot_ref, pieces, [k], eigen).astype(BF16)
        right[k, :eigen] = partial_ref[k, :eigen] + total[:, :eigen]
        right[k, eigen:] = partial_ref[k, eigen:] + total[:, eigen:]
    for k in range(products):
        for n, (_, result) in enumerate(times_right(blocks, masks, right, k)):
            done[k, n] = result.reshape(done.shape[2:])


def far_kernel(near_masks, masks, counts, right, near_ref, *refs):
    blocks, (out_ref, done, near_sems, sems) = grouped(counts, refs)
    products, eigen = right.shape[0], right.shape[2]
    near_times, times = near_ref.shape[1], done.shape[1]
    per_time = len(masks) // times
    me = lax.axis_index("col")

    def send(source, k, time, sem):
        at = pl.multiple_of(time * eigen, eigen)
        copy = pltpu.make_async_copy(source, out_ref.at[k, :, :, :, pl.ds(at, eigen)], sem)
        copy.start()
        return copy

    copies = []
    for k in range(products):
        for n in range(near_times):
            time = (me ^ near_masks[n * per_time]) // per_time
            copies.append(send(near_ref.at[k, n], k, time, near_sems.at[k, n]))
    for k in range(products):
        for n, (time, result) in enumerate(times_right(blocks, masks, right, k)):
            done[k, n] = result.reshape(done.shape[2:])
            copies.append(send(done.at[k, n], k, time, sems.at[k, n]))
    for copy in copies:
        copy.wait()


def flat(groups):
    return [part for group in groups for part in group]


def contract(places, pieces, partial, source, op_index, slots, blocks):
    _, products, _, own2, local_cols = blocks[0][0].shape
    n_cols = len(blocks)
    eigen = partial.shape[2]
    times = n_cols * local_cols // eigen
    near = n_cols // 2
    near_masks, far_masks = list(range(near)), list(range(near, n_cols))
    vmem = pl.BlockSpec(memory_space=pltpu.VMEM)
    smem = pl.BlockSpec(memory_space=pltpu.SMEM)
    params = pltpu.CompilerParams(vmem_limit_bytes=VMEM_LIMIT)
    cost = pl.CostEstimate(flops=1000 * 10**6, bytes_accessed=1000, transcendentals=0)
    half = (products, times // 2, NS, own2 // 2, 2, eigen)
    groups = pieces + blocks[:near]
    right, done = pl.pallas_call(
        functools.partial(near_kernel, places, near_masks, [len(g) for g in groups]),
        in_specs=[smem, smem] + [vmem] * (2 + len(flat(groups))),
        out_specs=[vmem, vmem],
        out_shape=[
            jax.ShapeDtypeStruct((products, 2 * eigen, eigen), BF16),
            jax.ShapeDtypeStruct(half, BF16),
        ],
        compiler_params=params,
        cost_estimate=cost,
        name="near",
    )(source, op_index, slots, partial, *flat(groups))
    groups = blocks[near:]
    return pl.pallas_call(
        functools.partial(far_kernel, near_masks, far_masks, [len(g) for g in groups]),
        in_specs=[vmem] * (2 + len(flat(groups))),
        out_specs=pl.BlockSpec(memory_space=pl.ANY),
        out_shape=jax.ShapeDtypeStruct((products, NS, own2 // 2, 2, times * eigen), BF16),
        scratch_shapes=[
            pltpu.VMEM(half, BF16),
            pltpu.SemaphoreType.DMA(half[:2]),
            pltpu.SemaphoreType.DMA(half[:2]),
        ],
        compiler_params=params,
        cost_estimate=cost,
        name="far",
    )(right, done, *flat(groups))


def swap(array, axis, size, mask):
    return lax.ppermute(array, axis, [(i, i ^ mask) for i in range(size)])


def after(array, *others):
    return lax.optimization_barrier((array, *others))[0]


def per_device(peramb, sink_ops, op_table, row_slot, pair_source, op_index, listed_rows):
    n_cols = lax.axis_size("col")
    n_pair = lax.axis_size("tpair")
    rows, _, eigen = op_table.shape
    slots = row_slot.reshape(-1, LANES)

    def across(array, mask):
        return swap(array, "tpair", n_pair, mask)

    def beside(array):
        return swap(array, "col", n_cols, 1)

    if n_cols != 4 or n_pair != 8 or rows % 32:
        own = jnp.concatenate([op_table[:, 0], op_table[:, 1]], axis=1)
        whole = lax.all_gather(own, "tpair", axis=0, tiled=True)
        half = whole.shape[0] // 2
        mixed = mix(op_index, listed_rows, sink_ops, peramb, [1] * n_cols)
        blocks = [[mixed[0]]] + [[swap(mixed[j], "col", n_cols, j)] for j in range(1, n_cols)]
        partial = assemble([[0]], [[whole[:half]]], pair_source, op_index, slots, eigen)
        return contract(
            [[half]], [[whole[half:]]], partial, pair_source, op_index, slots, blocks
        )
    half = rows // 2
    own = lax.dynamic_slice_in_dim(op_table, lax.axis_index("col") % 2 * half, half, 0)
    own = jnp.concatenate([own[:, 0], own[:, 1]], axis=1)
    beside_own = beside(own)
    z1 = across(own, 2)
    z2 = across(own, 4)
    x0 = across(own, 1)
    mixed = mix(op_index, listed_rows, sink_ops, peramb, [1, 1, 2])
    crossed = swap(mixed[2], "col", n_cols, 2)
    beside_mixed = beside(mixed[1])
    beside_x0 = beside(after(x0, mixed[0]))
    z3 = across(after(own, mixed[0]), 6)
    z12 = after(jnp.concatenate([z1, after(z2, x0)]), mixed[0])
    x12 = across(z12, 1)
    x3 = across(after(z3, x12, beside_x0, beside_mixed), 1)
    early = [
        ([(0, 0)], own), ([(0, 1)], beside_own),
        ([(1, 0)], x0), ([(1, 1)], beside_x0),
        ([(2, 0), (4, 0)], z12), ([(2, 1), (4, 1)], beside(z12)),
        ([(6, 0)], z3), ([(6, 1)], beside(z3)),
        ([(3, 0), (5, 0)], x12),
    ]
    places, pieces = [p for p, _ in early], [[piece] for _, piece in early]
    partial = assemble(places, pieces, pair_source, op_index, slots, eigen)
    spins = [crossed[1:, :, : NS - 1], crossed[1:, :, NS - 1 :]]
    over = [beside(after(some, partial)) for some in spins]
    blocks = [[mixed[0]], [beside_mixed], [crossed], over]
    late = [[x3], [beside(after(x3, partial))], [beside(x12)]]
    places = [[(7, 0)], [(7, 1)], [(3, 1), (5, 1)]]
    return contract(places, late, partial, pair_source, op_index, slots, blocks)


def solution(mesh):
    in_specs = (
        P("tpair", None, None, "col"),
        P("tpair", None, None, None, None),
        P("tpair", None, None),
        P(),
        P("tpair"),
        P("tpair", None),
        P("tpair", None),
    )
    out_specs = P("tpair", None, "col", None, None)
    return jax.shard_map(
        per_device, mesh=mesh, in_specs=in_specs, out_specs=out_specs, check_vma=False
    )
```

```python
import functools

import jax
import jax.numpy as jnp
from jax import lax
from jax.experimental import pallas as pl
from jax.experimental.pallas import tpu as pltpu
from jax.sharding import PartitionSpec as P

NS = 4
LANES = 128
VMEM_LIMIT = 24 * 1024 * 1024
BF16, F32 = jnp.bfloat16, jnp.float32


def iota(shape, dim):
    return lax.broadcasted_iota(jnp.int32, shape, dim)


def dot(a, b):
    return jnp.dot(a, b, preferred_element_type=F32)


def column(row):
    wide = jnp.broadcast_to(row, (LANES, LANES)).astype(F32)
    return jnp.transpose(wide).astype(jnp.int32)


def one_hot(col, first, width):
    tiles = [
        jnp.where(col - (first + n) == iota((col.shape[0], LANES), 1), 1.0, 0.0)
        for n in range(0, width, LANES)
    ]
    return jnp.concatenate(tiles, axis=1).astype(BF16)


def mix_kernel(op_ref, listed_ref, sink_ref, peramb_ref, *refs):
    outs, (left, held, sems) = refs[:-3], refs[-3:]
    n_cols = sum(out.shape[0] for out in outs)
    products, listed = listed_ref.shape
    eigen, local_cols = sink_ref.shape[-1], peramb_ref.shape[-1]
    loads = [
        pltpu.make_async_copy(
            peramb_ref.at[0, :, pl.ds(s * eigen, eigen), :], held.at[s], sems.at[s]
        )
        for s in range(NS)
    ]
    for load in loads:
        load.start()
    own2 = 2 * listed // n_cols
    me = lax.axis_index("col")
    row = iota((2 * listed, 2 * listed), 0)
    wanted = ((row // own2) ^ me) * (own2 // 2) + (row % own2) // 2 + (row % 2) * listed
    order = jnp.where(wanted == iota((2 * listed, 2 * listed), 1), 1.0, 0.0).astype(BF16)
    for k in range(products):
        op = op_ref[k, 0]
        onehot = one_hot(column(listed_ref[k : k + 1, :]), 0, eigen)
        real = dot(onehot, sink_ref[0, op, 0])
        imag = dot(onehot, sink_ref[0, op, 1])
        top = jnp.concatenate([real, -imag], axis=1)
        bottom = jnp.concatenate([imag, real], axis=1)
        both = jnp.concatenate([top, bottom], axis=0).astype(BF16)
        rows = dot(order, both).astype(BF16)
        for j in range(n_cols):
            at = (j * products + k) * own2
            left[at : at + own2, :] = rows[j * own2 : (j + 1) * own2]
    for s in range(NS):
        loads[s].wait()
        mixed = dot(left[...], held[s].reshape(2 * eigen, local_cols)).astype(BF16)
        j = 0
        for out in outs:
            for n in range(out.shape[0]):
                for k in range(products):
                    at = (j * products + k) * own2
                    out[n, k, s] = mixed[at : at + own2]
                j += 1


def mix(op_index, listed_rows, sink_ops, peramb, groups):
    products, listed = listed_rows.shape
    eigen = sink_ops.shape[-1]
    local_cols = peramb.shape[3]
    own2 = 2 * listed // sum(groups)
    blocks = [
        jax.ShapeDtypeStruct((group, products, NS, own2, local_cols), BF16) for group in groups
    ]
    vmem = pl.BlockSpec(memory_space=pltpu.VMEM)
    return pl.pallas_call(
        mix_kernel,
        in_specs=[
            pl.BlockSpec(memory_space=pltpu.SMEM), vmem, vmem, pl.BlockSpec(memory_space=pltpu.HBM)
        ],
        out_specs=[vmem] * len(groups),
        out_shape=blocks,
        scratch_shapes=[
            pltpu.VMEM((products * 2 * listed, 2 * eigen), BF16),
            pltpu.VMEM((NS, 2, eigen, local_cols), BF16),
            pltpu.SemaphoreType.DMA((NS,)),
        ],
        compiler_params=pltpu.CompilerParams(vmem_limit_bytes=VMEM_LIMIT),
        cost_estimate=pl.CostEstimate(flops=1000, bytes_accessed=1000, transcendentals=0),
        name="mix",
    )(op_index, listed_rows, sink_ops, pltpu.with_memory_space_constraint(peramb, pltpu.HBM))


def add_pieces(places, scalars_ref, slot_ref, pieces, products, eigen):
    source_ref, op_ref = scalars_ref
    blocks = eigen // LANES
    nops = slot_ref.shape[0] // blocks // 2
    pair, side = lax.axis_index("tpair"), lax.axis_index("col") % 2
    cols = []
    for k in products:
        op = source_ref[0] * nops + op_ref[k, 1]
        cols += [
            column(slot_ref[pl.ds(op * blocks + b, 1), :]) for b in range(blocks)
        ]
    col = jnp.concatenate(cols, axis=0)
    tiles, tables = [], []
    for owners, parts in zip(places, pieces):
        height = sum(part.shape[0] for part in parts) // len(owners)
        for owner in owners:
            first = owner
            if isinstance(owner, tuple):
                first = (2 * (pair ^ owner[0]) + (side ^ owner[1])) * height
            tiles.append(one_hot(col, first, height))
        tables += [part[...] for part in parts]
    return dot(jnp.concatenate(tiles, axis=1), jnp.concatenate(tables, axis=0))


def grouped(counts, refs):
    groups = []
    for count in counts:
        groups.append(refs[:count])
        refs = refs[count:]
    return groups, refs


def assemble_kernel(places, counts, source_ref, op_ref, slot_ref, *refs):
    pieces, (out_ref,) = grouped(counts, refs)
    products, eigen = out_ref.shape[0], out_ref.shape[2]
    total = add_pieces(places, (source_ref, op_ref), slot_ref, pieces, range(products), eigen)
    total = total.astype(BF16)
    for k in range(products):
        rows = slice(k * eigen, (k + 1) * eigen)
        out_ref[k, :eigen] = total[rows, :eigen]
        out_ref[k, eigen:] = total[rows, eigen:]


def assemble(places, pieces, source, op_index, slots, eigen):
    products = op_index.shape[0]
    vmem = pl.BlockSpec(memory_space=pltpu.VMEM)
    smem = pl.BlockSpec(memory_space=pltpu.SMEM)
    return pl.pallas_call(
        functools.partial(assemble_kernel, places, [len(group) for group in pieces]),
        in_specs=[smem, smem] + [vmem] * (1 + sum(len(group) for group in pieces)),
        out_specs=vmem,
        out_shape=jax.ShapeDtypeStruct((products, 2 * eigen, eigen), BF16),
        compiler_params=pltpu.CompilerParams(vmem_limit_bytes=VMEM_LIMIT),
        cost_estimate=pl.CostEstimate(flops=1000, bytes_accessed=1000, transcendentals=0),
        name="assemble",
    )(source, op_index, slots, *[part for group in pieces for part in group])


def block_rows(parts, k):
    found = [part[0, k] for part in parts]
    return jnp.concatenate([f.reshape(-1, f.shape[-1]) for f in found], axis=0)


def times_right(blocks, masks, right, k):
    eigen = right.shape[2]
    local_cols = blocks[0][0].shape[4]
    me = lax.axis_index("col")
    per_time = eigen // local_cols
    direct = [block_rows(parts, k) for parts in blocks]
    rows = direct[0].shape[0]
    odd = iota((rows, local_cols), 0) % 2 == 1
    turned = []
    for x in direct:
        wide = x.astype(F32)
        y = jnp.where(odd, pltpu.roll(wide, 1, 0), -pltpu.roll(wide, rows - 1, 0))
        turned.append(y.astype(BF16))
    if per_time == 1:
        lhs = jnp.concatenate(
            [jnp.concatenate(direct, axis=0), jnp.concatenate(turned, axis=0)], axis=1
        )
        whole = dot(lhs, right[k]).astype(BF16)
        results = [whole[n * rows : (n + 1) * rows] for n in range(len(masks))]
    else:
        results = []
        for n, mask in enumerate(masks):
            first = pl.multiple_of(((me ^ mask) % per_time) * local_cols, local_cols)
            second = pl.multiple_of(eigen + first, local_cols)
            part = dot(direct[n], right[k, pl.ds(first, local_cols), :])
            part += dot(turned[n], right[k, pl.ds(second, local_cols), :])
            if n % per_time:
                results[-1] += part
            else:
                results.append(part)
        results = [result.astype(BF16) for result in results]
    times = [(me ^ mask) // per_time for mask in masks[::per_time]]
    return list(zip(times, results))


def near_kernel(places, masks, counts, source_ref, op_ref, slot_ref, partial_ref, *refs):
    groups, (right, done) = grouped(counts, refs)
    pieces, blocks = groups[: len(places)], groups[len(places) :]
    products, eigen = right.shape[0], right.shape[2]
    scalars = (source_ref, op_ref)
    for k in range(products):
        total = add_pieces(places, scalars, slot_ref, pieces, [k], eigen).astype(BF16)
        right[k, :eigen] = partial_ref[k, :eigen] + total[:, :eigen]
        right[k, eigen:] = partial_ref[k, eigen:] + total[:, eigen:]
    for k in range(products):
        for n, (_, result) in enumerate(times_right(blocks, masks, right, k)):
            done[k, n] = result.reshape(done.shape[2:])


def far_kernel(near_masks, masks, counts, right, near_ref, *refs):
    blocks, (out_ref, done, near_sems, sems) = grouped(counts, refs)
    products, eigen = right.shape[0], right.shape[2]
    near_times, times = near_ref.shape[1], done.shape[1]
    per_time = len(masks) // times
    me = lax.axis_index("col")

    def send(source, k, time, sem):
        at = pl.multiple_of(time * eigen, eigen)
        copy = pltpu.make_async_copy(source, out_ref.at[k, :, :, :, pl.ds(at, eigen)], sem)
        copy.start()
        return copy

    copies = []
    for k in range(products):
        for n in range(near_times):
            time = (me ^ near_masks[n * per_time]) // per_time
            copies.append(send(near_ref.at[k, n], k, time, near_sems.at[k, n]))
    for k in range(products):
        for n, (time, result) in enumerate(times_right(blocks, masks, right, k)):
            done[k, n] = result.reshape(done.shape[2:])
            copies.append(send(done.at[k, n], k, time, sems.at[k, n]))
    for copy in copies:
        copy.wait()


def flat(groups):
    return [part for group in groups for part in group]


def contract(places, pieces, partial, source, op_index, slots, blocks):
    _, products, _, own2, local_cols = blocks[0][0].shape
    n_cols = len(blocks)
    eigen = partial.shape[2]
    times = n_cols * local_cols // eigen
    near = n_cols // 2
    near_masks, far_masks = list(range(near)), list(range(near, n_cols))
    vmem = pl.BlockSpec(memory_space=pltpu.VMEM)
    smem = pl.BlockSpec(memory_space=pltpu.SMEM)
    params = pltpu.CompilerParams(vmem_limit_bytes=VMEM_LIMIT)
    cost = pl.CostEstimate(flops=1000 * 10**6, bytes_accessed=1000, transcendentals=0)
    half = (products, times // 2, NS, own2 // 2, 2, eigen)
    groups = pieces + blocks[:near]
    right, done = pl.pallas_call(
        functools.partial(near_kernel, places, near_masks, [len(g) for g in groups]),
        in_specs=[smem, smem] + [vmem] * (2 + len(flat(groups))),
        out_specs=[vmem, vmem],
        out_shape=[
            jax.ShapeDtypeStruct((products, 2 * eigen, eigen), BF16),
            jax.ShapeDtypeStruct(half, BF16),
        ],
        compiler_params=params,
        cost_estimate=cost,
        name="near",
    )(source, op_index, slots, partial, *flat(groups))
    groups = blocks[near:]
    return pl.pallas_call(
        functools.partial(far_kernel, near_masks, far_masks, [len(g) for g in groups]),
        in_specs=[vmem] * (2 + len(flat(groups))),
        out_specs=pl.BlockSpec(memory_space=pl.ANY),
        out_shape=jax.ShapeDtypeStruct((products, NS, own2 // 2, 2, times * eigen), BF16),
        scratch_shapes=[
            pltpu.VMEM(half, BF16),
            pltpu.SemaphoreType.DMA(half[:2]),
            pltpu.SemaphoreType.DMA(half[:2]),
        ],
        compiler_params=params,
        cost_estimate=cost,
        name="far",
    )(right, done, *flat(groups))


def swap(array, axis, size, mask):
    return lax.ppermute(array, axis, [(i, i ^ mask) for i in range(size)])


def after(array, *others):
    return lax.optimization_barrier((array, *others))[0]


def per_device(peramb, sink_ops, op_table, row_slot, pair_source, op_index, listed_rows):
    n_cols = lax.axis_size("col")
    n_pair = lax.axis_size("tpair")
    rows, _, eigen = op_table.shape
    slots = row_slot.reshape(-1, LANES)

    def across(array, mask):
        return swap(array, "tpair", n_pair, mask)

    def beside(array):
        return swap(array, "col", n_cols, 1)

    if n_cols != 4 or n_pair != 8 or rows % 32:
        own = jnp.concatenate([op_table[:, 0], op_table[:, 1]], axis=1)
        whole = lax.all_gather(own, "tpair", axis=0, tiled=True)
        half = whole.shape[0] // 2
        mixed = mix(op_index, listed_rows, sink_ops, peramb, [1] * n_cols)
        blocks = [[mixed[0]]] + [[swap(mixed[j], "col", n_cols, j)] for j in range(1, n_cols)]
        partial = assemble([[0]], [[whole[:half]]], pair_source, op_index, slots, eigen)
        return contract(
            [[half]], [[whole[half:]]], partial, pair_source, op_index, slots, blocks
        )
    half = rows // 2
    own = lax.dynamic_slice_in_dim(op_table, lax.axis_index("col") % 2 * half, half, 0)
    own = jnp.concatenate([own[:, 0], own[:, 1]], axis=1)
    beside_own = beside(own)
    z1 = across(own, 2)
    z2 = across(own, 4)
    x0 = across(own, 1)
    mixed = mix(op_index, listed_rows, sink_ops, peramb, [1, 1, 2])
    crossed = swap(mixed[2], "col", n_cols, 2)
    beside_mixed = beside(mixed[1])
    beside_x0 = beside(after(x0, mixed[0]))
    z12 = after(jnp.concatenate([z1, after(z2, x0)]), mixed[0])
    z3 = across(after(own, z12), 6)
    x12 = across(z12, 1)
    x3 = across(after(z3, x12, beside_x0, beside_mixed), 1)
    early = [
        ([(0, 0)], own), ([(0, 1)], beside_own),
        ([(1, 0)], x0), ([(1, 1)], beside_x0),
        ([(2, 0), (4, 0)], z12), ([(2, 1), (4, 1)], beside(z12)),
        ([(6, 0)], z3), ([(6, 1)], beside(z3)),
        ([(3, 0), (5, 0)], x12),
    ]
    places, pieces = [p for p, _ in early], [[piece] for _, piece in early]
    partial = assemble(places, pieces, pair_source, op_index, slots, eigen)
    spins = [crossed[1:, :, : NS - 1], crossed[1:, :, NS - 1 :]]
    over = [beside(after(some, partial)) for some in spins]
    blocks = [[mixed[0]], [beside_mixed], [crossed], over]
    late = [[x3], [beside(after(x3, partial))], [beside(x12)]]
    places = [[(7, 0)], [(7, 1)], [(3, 1), (5, 1)]]
    return contract(places, late, partial, pair_source, op_index, slots, blocks)


def solution(mesh):
    in_specs = (
        P("tpair", None, None, "col"),
        P("tpair", None, None, None, None),
        P("tpair", None, None),
        P(),
        P("tpair"),
        P("tpair", None),
        P("tpair", None),
    )
    out_specs = P("tpair", None, "col", None, None)
    return jax.shard_map(
        per_device, mesh=mesh, in_specs=in_specs, out_specs=out_specs, check_vma=False
    )
```

```python
import functools

import jax
import jax.numpy as jnp
from jax import lax
from jax.experimental import pallas as pl
from jax.experimental.pallas import tpu as pltpu
from jax.sharding import PartitionSpec as P

NS = 4
LANES = 128
VMEM_LIMIT = 24 * 1024 * 1024
BF16, F32 = jnp.bfloat16, jnp.float32


def iota(shape, dim):
    return lax.broadcasted_iota(jnp.int32, shape, dim)


def dot(a, b):
    return jnp.dot(a, b, preferred_element_type=F32)


def column(row):
    wide = jnp.broadcast_to(row, (LANES, LANES)).astype(F32)
    return jnp.transpose(wide).astype(jnp.int32)


def one_hot(col, first, width):
    tiles = [
        jnp.where(col - (first + n) == iota((col.shape[0], LANES), 1), 1.0, 0.0)
        for n in range(0, width, LANES)
    ]
    return jnp.concatenate(tiles, axis=1).astype(BF16)


def mix_kernel(op_ref, listed_ref, sink_ref, peramb_ref, *refs):
    outs, (left, sink, held, sink_sem, sems) = refs[:-5], refs[-5:]
    n_cols = sum(out.shape[0] for out in outs)
    products, listed = listed_ref.shape
    eigen, local_cols = sink_ref.shape[-1], peramb_ref.shape[-1]
    fetch = pltpu.make_async_copy(sink_ref.at[0], sink, sink_sem)
    fetch.start()
    loads = [
        pltpu.make_async_copy(
            peramb_ref.at[0, :, pl.ds(s * eigen, eigen), :], held.at[s], sems.at[s]
        )
        for s in range(NS)
    ]
    for load in loads:
        load.start()
    own2 = 2 * listed // n_cols
    me = lax.axis_index("col")
    row = iota((2 * listed, 2 * listed), 0)
    wanted = ((row // own2) ^ me) * (own2 // 2) + (row % own2) // 2 + (row % 2) * listed
    order = jnp.where(wanted == iota((2 * listed, 2 * listed), 1), 1.0, 0.0).astype(BF16)
    onehots = [one_hot(column(listed_ref[k : k + 1, :]), 0, eigen) for k in range(products)]
    fetch.wait()
    for k in range(products):
        op = op_ref[k, 0]
        real = dot(onehots[k], sink[op, 0])
        imag = dot(onehots[k], sink[op, 1])
        top = jnp.concatenate([real, -imag], axis=1)
        bottom = jnp.concatenate([imag, real], axis=1)
        both = jnp.concatenate([top, bottom], axis=0).astype(BF16)
        rows = dot(order, both).astype(BF16)
        for j in range(n_cols):
            at = (j * products + k) * own2
            left[at : at + own2, :] = rows[j * own2 : (j + 1) * own2]
    for s in range(NS):
        loads[s].wait()
        mixed = dot(left[...], held[s].reshape(2 * eigen, local_cols)).astype(BF16)
        j = 0
        for out in outs:
            for n in range(out.shape[0]):
                for k in range(products):
                    at = (j * products + k) * own2
                    out[n, k, s] = mixed[at : at + own2]
                j += 1


def mix(op_index, listed_rows, sink_ops, peramb, groups):
    products, listed = listed_rows.shape
    eigen = sink_ops.shape[-1]
    local_cols = peramb.shape[3]
    own2 = 2 * listed // sum(groups)
    blocks = [
        jax.ShapeDtypeStruct((group, products, NS, own2, local_cols), BF16) for group in groups
    ]
    vmem = pl.BlockSpec(memory_space=pltpu.VMEM)
    return pl.pallas_call(
        mix_kernel,
        in_specs=[
            pl.BlockSpec(memory_space=pltpu.SMEM),
            vmem,
            pl.BlockSpec(memory_space=pltpu.HBM),
            pl.BlockSpec(memory_space=pltpu.HBM),
        ],
        out_specs=[vmem] * len(groups),
        out_shape=blocks,
        scratch_shapes=[
            pltpu.VMEM((products * 2 * listed, 2 * eigen), BF16),
            pltpu.VMEM(sink_ops.shape[1:], BF16),
            pltpu.VMEM((NS, 2, eigen, local_cols), BF16),
            pltpu.SemaphoreType.DMA,
            pltpu.SemaphoreType.DMA((NS,)),
        ],
        compiler_params=pltpu.CompilerParams(vmem_limit_bytes=VMEM_LIMIT),
        cost_estimate=pl.CostEstimate(flops=1000, bytes_accessed=1000, transcendentals=0),
        name="mix",
    )(
        op_index,
        listed_rows,
        pltpu.with_memory_space_constraint(sink_ops, pltpu.HBM),
        pltpu.with_memory_space_constraint(peramb, pltpu.HBM),
    )


def add_pieces(places, scalars_ref, slot_ref, pieces, products, eigen):
    source_ref, op_ref = scalars_ref
    blocks = eigen // LANES
    nops = slot_ref.shape[0] // blocks // 2
    pair, side = lax.axis_index("tpair"), lax.axis_index("col") % 2
    cols = []
    for k in products:
        op = source_ref[0] * nops + op_ref[k, 1]
        cols += [
            column(slot_ref[pl.ds(op * blocks + b, 1), :]) for b in range(blocks)
        ]
    col = jnp.concatenate(cols, axis=0)
    tiles, tables = [], []
    for owners, parts in zip(places, pieces):
        height = sum(part.shape[0] for part in parts) // len(owners)
        for owner in owners:
            first = owner
            if isinstance(owner, tuple):
                first = (2 * (pair ^ owner[0]) + (side ^ owner[1])) * height
            tiles.append(one_hot(col, first, height))
        tables += [part[...] for part in parts]
    return dot(jnp.concatenate(tiles, axis=1), jnp.concatenate(tables, axis=0))


def flat(groups):
    return [part for group in groups for part in group]


def grouped(counts, refs):
    groups = []
    for count in counts:
        groups.append(refs[:count])
        refs = refs[count:]
    return groups, refs


def assemble_kernel(places, counts, source_ref, op_ref, slot_ref, *refs):
    pieces, (*earlier, out_ref) = grouped(counts, refs)
    products, eigen = out_ref.shape[0], out_ref.shape[2]
    for k in range(products):
        total = add_pieces(places, (source_ref, op_ref), slot_ref, pieces, [k], eigen)
        total = total.astype(BF16)
        real, imag = total[:, :eigen], total[:, eigen:]
        if earlier:
            real += earlier[0][k, :eigen]
            imag += earlier[0][k, eigen:]
        out_ref[k, :eigen] = real
        out_ref[k, eigen:] = imag


def assemble(places, pieces, source, op_index, slots, eigen, *earlier):
    products = op_index.shape[0]
    vmem = pl.BlockSpec(memory_space=pltpu.VMEM)
    smem = pl.BlockSpec(memory_space=pltpu.SMEM)
    inputs = [*flat(pieces), *earlier]
    return pl.pallas_call(
        functools.partial(assemble_kernel, places, [len(group) for group in pieces]),
        in_specs=[smem, smem] + [vmem] * (1 + len(inputs)),
        out_specs=vmem,
        out_shape=jax.ShapeDtypeStruct((products, 2 * eigen, eigen), BF16),
        compiler_params=pltpu.CompilerParams(vmem_limit_bytes=VMEM_LIMIT),
        cost_estimate=pl.CostEstimate(flops=1000, bytes_accessed=1000, transcendentals=0),
        name="assemble",
    )(source, op_index, slots, *inputs)


def block_rows(parts, k):
    found = [part[0, k] for part in parts]
    return jnp.concatenate([f.reshape(-1, f.shape[-1]) for f in found], axis=0)


def times_right(blocks, masks, right, k):
    eigen = right.shape[2]
    local_cols = blocks[0][0].shape[4]
    me = lax.axis_index("col")
    per_time = eigen // local_cols
    direct = [block_rows(parts, k) for parts in blocks]
    rows = direct[0].shape[0]
    odd = iota((rows, local_cols), 0) % 2 == 1
    turned = []
    for x in direct:
        wide = x.astype(F32)
        y = jnp.where(odd, pltpu.roll(wide, 1, 0), -pltpu.roll(wide, rows - 1, 0))
        turned.append(y.astype(BF16))
    if per_time == 1:
        lhs = jnp.concatenate(
            [jnp.concatenate(direct, axis=0), jnp.concatenate(turned, axis=0)], axis=1
        )
        whole = dot(lhs, right[k]).astype(BF16)
        results = [whole[n * rows : (n + 1) * rows] for n in range(len(masks))]
    else:
        results = []
        for n, mask in enumerate(masks):
            first = pl.multiple_of(((me ^ mask) % per_time) * local_cols, local_cols)
            second = pl.multiple_of(eigen + first, local_cols)
            part = dot(direct[n], right[k, pl.ds(first, local_cols), :])
            part += dot(turned[n], right[k, pl.ds(second, local_cols), :])
            if n % per_time:
                results[-1] += part
            else:
                results.append(part)
        results = [result.astype(BF16) for result in results]
    times = [(me ^ mask) // per_time for mask in masks[::per_time]]
    return list(zip(times, results))


def near_kernel(places, masks, counts, source_ref, op_ref, slot_ref, partial_ref, *refs):
    groups, (right, done) = grouped(counts, refs)
    pieces, blocks = groups[: len(places)], groups[len(places) :]
    products, eigen = right.shape[0], right.shape[2]
    scalars = (source_ref, op_ref)
    for k in range(products):
        total = add_pieces(places, scalars, slot_ref, pieces, [k], eigen).astype(BF16)
        right[k, :eigen] = partial_ref[k, :eigen] + total[:, :eigen]
        right[k, eigen:] = partial_ref[k, eigen:] + total[:, eigen:]
    for k in range(products):
        for n, (_, result) in enumerate(times_right(blocks, masks, right, k)):
            done[k, n] = result.reshape(done.shape[2:])


def far_kernel(near_masks, masks, counts, right, near_ref, *refs):
    blocks, (out_ref, done, near_sems, sems) = grouped(counts, refs)
    products, eigen = right.shape[0], right.shape[2]
    near_times, times = near_ref.shape[1], done.shape[1]
    per_time = len(masks) // times
    me = lax.axis_index("col")

    def send(source, k, time, sem):
        at = pl.multiple_of(time * eigen, eigen)
        copy = pltpu.make_async_copy(source, out_ref.at[k, :, :, :, pl.ds(at, eigen)], sem)
        copy.start()
        return copy

    copies = []
    for k in range(products):
        for n in range(near_times):
            time = (me ^ near_masks[n * per_time]) // per_time
            copies.append(send(near_ref.at[k, n], k, time, near_sems.at[k, n]))
    for k in range(products):
        for n, (time, result) in enumerate(times_right(blocks, masks, right, k)):
            done[k, n] = result.reshape(done.shape[2:])
            copies.append(send(done.at[k, n], k, time, sems.at[k, n]))
    for copy in copies:
        copy.wait()


def contract(places, pieces, partial, source, op_index, slots, blocks):
    _, products, _, own2, local_cols = blocks[0][0].shape
    n_cols = len(blocks)
    eigen = partial.shape[2]
    times = n_cols * local_cols // eigen
    near = n_cols // 2
    near_masks, far_masks = list(range(near)), list(range(near, n_cols))
    vmem = pl.BlockSpec(memory_space=pltpu.VMEM)
    smem = pl.BlockSpec(memory_space=pltpu.SMEM)
    params = pltpu.CompilerParams(vmem_limit_bytes=VMEM_LIMIT)
    cost = pl.CostEstimate(flops=1000 * 10**6, bytes_accessed=1000, transcendentals=0)
    half = (products, times // 2, NS, own2 // 2, 2, eigen)
    groups = pieces + blocks[:near]
    right, done = pl.pallas_call(
        functools.partial(near_kernel, places, near_masks, [len(g) for g in groups]),
        in_specs=[smem, smem] + [vmem] * (2 + len(flat(groups))),
        out_specs=[vmem, vmem],
        out_shape=[
            jax.ShapeDtypeStruct((products, 2 * eigen, eigen), BF16),
            jax.ShapeDtypeStruct(half, BF16),
        ],
        compiler_params=params,
        cost_estimate=cost,
        name="near",
    )(source, op_index, slots, partial, *flat(groups))
    groups = blocks[near:]
    return pl.pallas_call(
        functools.partial(far_kernel, near_masks, far_masks, [len(g) for g in groups]),
        in_specs=[vmem] * (2 + len(flat(groups))),
        out_specs=pl.BlockSpec(memory_space=pl.ANY),
        out_shape=jax.ShapeDtypeStruct((products, NS, own2 // 2, 2, times * eigen), BF16),
        scratch_shapes=[
            pltpu.VMEM(half, BF16),
            pltpu.SemaphoreType.DMA(half[:2]),
            pltpu.SemaphoreType.DMA(half[:2]),
        ],
        compiler_params=params,
        cost_estimate=cost,
        name="far",
    )(right, done, *flat(groups))


def swap(array, axis, size, mask):
    return lax.ppermute(array, axis, [(i, i ^ mask) for i in range(size)])


def after(array, *others):
    return lax.optimization_barrier((array, *others))[0]


def per_device(peramb, sink_ops, op_table, row_slot, pair_source, op_index, listed_rows):
    n_cols = lax.axis_size("col")
    n_pair = lax.axis_size("tpair")
    rows, _, eigen = op_table.shape
    slots = row_slot.reshape(-1, LANES)

    def across(array, mask):
        return swap(array, "tpair", n_pair, mask)

    def beside(array):
        return swap(array, "col", n_cols, 1)

    if n_cols != 4 or n_pair != 8 or rows % 32:
        own = jnp.concatenate([op_table[:, 0], op_table[:, 1]], axis=1)
        whole = lax.all_gather(own, "tpair", axis=0, tiled=True)
        half = whole.shape[0] // 2
        mixed = mix(op_index, listed_rows, sink_ops, peramb, [1] * n_cols)
        blocks = [[mixed[0]]] + [[swap(mixed[j], "col", n_cols, j)] for j in range(1, n_cols)]
        partial = assemble([[0]], [[whole[:half]]], pair_source, op_index, slots, eigen)
        return contract(
            [[half]], [[whole[half:]]], partial, pair_source, op_index, slots, blocks
        )
    half = rows // 2
    own = lax.dynamic_slice_in_dim(op_table, lax.axis_index("col") % 2 * half, half, 0)
    own = jnp.concatenate([own[:, 0], own[:, 1]], axis=1)
    beside_own = beside(own)
    z1 = across(own, 2)
    z2 = across(own, 4)
    x0 = across(own, 1)
    mixed = mix(op_index, listed_rows, sink_ops, peramb, [1, 1, 2])
    crossed = swap(mixed[2], "col", n_cols, 2)
    beside_mixed = beside(mixed[1])
    beside_x0 = beside(after(x0, mixed[0]))
    z12 = after(jnp.concatenate([z1, after(z2, x0)]), mixed[0])
    z3 = across(after(own, z12, beside_x0), 6)
    x12 = across(z12, 1)
    x3 = across(after(z3, x12, beside_x0, beside_mixed), 1)
    early = [
        ([(0, 0)], own), ([(0, 1)], beside_own),
        ([(1, 0)], x0), ([(1, 1)], beside_x0),
        ([(2, 0), (4, 0)], z12), ([(2, 1), (4, 1)], beside(z12)),
        ([(6, 0)], z3), ([(6, 1)], beside(z3)),
        ([(3, 0), (5, 0)], x12),
    ]
    places, pieces = [p for p, _ in early], [[piece] for _, piece in early]
    partial = assemble(places, pieces, pair_source, op_index, slots, eigen)
    spins = [crossed[1:, :, : NS - 1], crossed[1:, :, NS - 1 :]]
    over = [beside(after(some, partial)) for some in spins]
    blocks = [[mixed[0]], [beside_mixed], [crossed], over]
    last = beside(after(x3, partial))
    places, late = [[(7, 0)], [(3, 1), (5, 1)]], [[x3], [beside(x12)]]
    most = assemble(places, late, pair_source, op_index, slots, eigen, partial)
    return contract([[(7, 1)]], [[last]], most, pair_source, op_index, slots, blocks)


def solution(mesh):
    in_specs = (
        P("tpair", None, None, "col"),
        P("tpair", None, None, None, None),
        P("tpair", None, None),
        P(),
        P("tpair"),
        P("tpair", None),
        P("tpair", None),
    )
    out_specs = P("tpair", None, "col", None, None)
    return jax.shard_map(
        per_device, mesh=mesh, in_specs=in_specs, out_specs=out_specs, check_vma=False
    )
```

```python
import functools

import jax
import jax.numpy as jnp
from jax import lax
from jax.experimental import pallas as pl
from jax.experimental.pallas import tpu as pltpu
from jax.sharding import PartitionSpec as P

NS = 4
LANES = 128
VMEM_LIMIT = 24 * 1024 * 1024
BF16, F32 = jnp.bfloat16, jnp.float32


def iota(shape, dim):
    return lax.broadcasted_iota(jnp.int32, shape, dim)


def dot(a, b):
    return jnp.dot(a, b, preferred_element_type=F32)


def column(row):
    wide = jnp.broadcast_to(row, (LANES, LANES)).astype(F32)
    return jnp.transpose(wide).astype(jnp.int32)


def one_hot(col, first, width):
    tiles = [
        jnp.where(col - (first + n) == iota((col.shape[0], LANES), 1), 1.0, 0.0)
        for n in range(0, width, LANES)
    ]
    return jnp.concatenate(tiles, axis=1).astype(BF16)


def mix_kernel(op_ref, listed_ref, sink_ref, peramb_ref, *refs):
    outs, (left, held, sems) = refs[:-3], refs[-3:]
    n_cols = sum(out.shape[0] for out in outs)
    products, listed = listed_ref.shape
    eigen, local_cols = sink_ref.shape[-1], peramb_ref.shape[-1]
    loads = [
        pltpu.make_async_copy(
            peramb_ref.at[0, :, pl.ds(s * eigen, eigen), :], held.at[s], sems.at[s]
        )
        for s in range(NS)
    ]
    for load in loads[:2]:
        load.start()
    own2 = 2 * listed // n_cols
    me = lax.axis_index("col")
    row = iota((2 * listed, 2 * listed), 0)
    wanted = ((row // own2) ^ me) * (own2 // 2) + (row % own2) // 2 + (row % 2) * listed
    order = jnp.where(wanted == iota((2 * listed, 2 * listed), 1), 1.0, 0.0).astype(BF16)
    for k in range(products):
        op = op_ref[k, 0]
        onehot = one_hot(column(listed_ref[k : k + 1, :]), 0, eigen)
        real = dot(onehot, sink_ref[0, op, 0])
        imag = dot(onehot, sink_ref[0, op, 1])
        top = jnp.concatenate([real, -imag], axis=1)
        bottom = jnp.concatenate([imag, real], axis=1)
        both = jnp.concatenate([top, bottom], axis=0).astype(BF16)
        rows = dot(order, both).astype(BF16)
        for j in range(n_cols):
            at = (j * products + k) * own2
            left[at : at + own2, :] = rows[j * own2 : (j + 1) * own2]
    for s in range(NS):
        loads[s].wait()
        if s + 2 < NS:
            loads[s + 2].start()
        mixed = dot(left[...], held[s].reshape(2 * eigen, local_cols)).astype(BF16)
        j = 0
        for out in outs:
            for n in range(out.shape[0]):
                for k in range(products):
                    at = (j * products + k) * own2
                    out[n, k, s] = mixed[at : at + own2]
                j += 1


def mix(op_index, listed_rows, sink_ops, peramb, groups):
    products, listed = listed_rows.shape
    eigen = sink_ops.shape[-1]
    local_cols = peramb.shape[3]
    own2 = 2 * listed // sum(groups)
    blocks = [
        jax.ShapeDtypeStruct((group, products, NS, own2, local_cols), BF16) for group in groups
    ]
    vmem = pl.BlockSpec(memory_space=pltpu.VMEM)
    return pl.pallas_call(
        mix_kernel,
        in_specs=[
            pl.BlockSpec(memory_space=pltpu.SMEM), vmem, vmem, pl.BlockSpec(memory_space=pltpu.HBM)
        ],
        out_specs=[vmem] * len(groups),
        out_shape=blocks,
        scratch_shapes=[
            pltpu.VMEM((products * 2 * listed, 2 * eigen), BF16),
            pltpu.VMEM((NS, 2, eigen, local_cols), BF16),
            pltpu.SemaphoreType.DMA((NS,)),
        ],
        compiler_params=pltpu.CompilerParams(vmem_limit_bytes=VMEM_LIMIT),
        cost_estimate=pl.CostEstimate(flops=1000, bytes_accessed=1000, transcendentals=0),
        name="mix",
    )(op_index, listed_rows, sink_ops, pltpu.with_memory_space_constraint(peramb, pltpu.HBM))


def add_pieces(places, scalars_ref, slot_ref, pieces, products, eigen):
    source_ref, op_ref = scalars_ref
    blocks = eigen // LANES
    nops = slot_ref.shape[0] // blocks // 2
    pair, side = lax.axis_index("tpair"), lax.axis_index("col") % 2
    cols = []
    for k in products:
        op = source_ref[0] * nops + op_ref[k, 1]
        cols += [
            column(slot_ref[pl.ds(op * blocks + b, 1), :]) for b in range(blocks)
        ]
    col = jnp.concatenate(cols, axis=0)
    tiles, tables = [], []
    for owners, parts in zip(places, pieces):
        height = sum(part.shape[0] for part in parts) // len(owners)
        for owner in owners:
            first = owner
            if isinstance(owner, tuple):
                first = (2 * (pair ^ owner[0]) + (side ^ owner[1])) * height
            tiles.append(one_hot(col, first, height))
        tables += [part[...] for part in parts]
    return dot(jnp.concatenate(tiles, axis=1), jnp.concatenate(tables, axis=0))


def flat(groups):
    return [part for group in groups for part in group]


def grouped(counts, refs):
    groups = []
    for count in counts:
        groups.append(refs[:count])
        refs = refs[count:]
    return groups, refs


def assemble_kernel(places, counts, source_ref, op_ref, slot_ref, *refs):
    pieces, (*earlier, out_ref) = grouped(counts, refs)
    products, eigen = out_ref.shape[0], out_ref.shape[2]
    for k in range(products):
        total = add_pieces(places, (source_ref, op_ref), slot_ref, pieces, [k], eigen)
        total = total.astype(BF16)
        real, imag = total[:, :eigen], total[:, eigen:]
        if earlier:
            real += earlier[0][k, :eigen]
            imag += earlier[0][k, eigen:]
        out_ref[k, :eigen] = real
        out_ref[k, eigen:] = imag


def assemble(places, pieces, source, op_index, slots, eigen, *earlier):
    products = op_index.shape[0]
    vmem = pl.BlockSpec(memory_space=pltpu.VMEM)
    smem = pl.BlockSpec(memory_space=pltpu.SMEM)
    inputs = [*flat(pieces), *earlier]
    return pl.pallas_call(
        functools.partial(assemble_kernel, places, [len(group) for group in pieces]),
        in_specs=[smem, smem] + [vmem] * (1 + len(inputs)),
        out_specs=vmem,
        out_shape=jax.ShapeDtypeStruct((products, 2 * eigen, eigen), BF16),
        compiler_params=pltpu.CompilerParams(vmem_limit_bytes=VMEM_LIMIT),
        cost_estimate=pl.CostEstimate(flops=1000, bytes_accessed=1000, transcendentals=0),
        name="assemble",
    )(source, op_index, slots, *inputs)


def block_rows(parts, k):
    found = [part[0, k] for part in parts]
    return jnp.concatenate([f.reshape(-1, f.shape[-1]) for f in found], axis=0)


def times_right(blocks, masks, right, k):
    eigen = right.shape[2]
    local_cols = blocks[0][0].shape[4]
    me = lax.axis_index("col")
    per_time = eigen // local_cols
    direct = [block_rows(parts, k) for parts in blocks]
    rows = direct[0].shape[0]
    odd = iota((rows, local_cols), 0) % 2 == 1
    turned = []
    for x in direct:
        wide = x.astype(F32)
        y = jnp.where(odd, pltpu.roll(wide, 1, 0), -pltpu.roll(wide, rows - 1, 0))
        turned.append(y.astype(BF16))
    if per_time == 1:
        lhs = jnp.concatenate(
            [jnp.concatenate(direct, axis=0), jnp.concatenate(turned, axis=0)], axis=1
        )
        whole = dot(lhs, right[k]).astype(BF16)
        results = [whole[n * rows : (n + 1) * rows] for n in range(len(masks))]
    else:
        results = []
        for n, mask in enumerate(masks):
            first = pl.multiple_of(((me ^ mask) % per_time) * local_cols, local_cols)
            second = pl.multiple_of(eigen + first, local_cols)
            part = dot(direct[n], right[k, pl.ds(first, local_cols), :])
            part += dot(turned[n], right[k, pl.ds(second, local_cols), :])
            if n % per_time:
                results[-1] += part
            else:
                results.append(part)
        results = [result.astype(BF16) for result in results]
    times = [(me ^ mask) // per_time for mask in masks[::per_time]]
    return list(zip(times, results))


def near_kernel(places, masks, counts, source_ref, op_ref, slot_ref, partial_ref, *refs):
    groups, (right, done) = grouped(counts, refs)
    pieces, blocks = groups[: len(places)], groups[len(places) :]
    products, eigen = right.shape[0], right.shape[2]
    scalars = (source_ref, op_ref)
    for k in range(products):
        total = add_pieces(places, scalars, slot_ref, pieces, [k], eigen).astype(BF16)
        right[k, :eigen] = partial_ref[k, :eigen] + total[:, :eigen]
        right[k, eigen:] = partial_ref[k, eigen:] + total[:, eigen:]
    for k in range(products):
        for n, (_, result) in enumerate(times_right(blocks, masks, right, k)):
            done[k, n] = result.reshape(done.shape[2:])


def far_kernel(near_masks, masks, counts, right, near_ref, *refs):
    blocks, (out_ref, done, near_sems, sems) = grouped(counts, refs)
    products, eigen = right.shape[0], right.shape[2]
    near_times, times = near_ref.shape[1], done.shape[1]
    per_time = len(masks) // times
    me = lax.axis_index("col")

    def send(source, k, time, sem):
        at = pl.multiple_of(time * eigen, eigen)
        copy = pltpu.make_async_copy(source, out_ref.at[k, :, :, :, pl.ds(at, eigen)], sem)
        copy.start()
        return copy

    copies = []
    for k in range(products):
        for n in range(near_times):
            time = (me ^ near_masks[n * per_time]) // per_time
            copies.append(send(near_ref.at[k, n], k, time, near_sems.at[k, n]))
    for k in range(products):
        for n, (time, result) in enumerate(times_right(blocks, masks, right, k)):
            done[k, n] = result.reshape(done.shape[2:])
            copies.append(send(done.at[k, n], k, time, sems.at[k, n]))
    for copy in copies:
        copy.wait()


def contract(places, pieces, partial, source, op_index, slots, blocks):
    _, products, _, own2, local_cols = blocks[0][0].shape
    n_cols = len(blocks)
    eigen = partial.shape[2]
    times = n_cols * local_cols // eigen
    near = n_cols // 2
    near_masks, far_masks = list(range(near)), list(range(near, n_cols))
    vmem = pl.BlockSpec(memory_space=pltpu.VMEM)
    smem = pl.BlockSpec(memory_space=pltpu.SMEM)
    params = pltpu.CompilerParams(vmem_limit_bytes=VMEM_LIMIT)
    cost = pl.CostEstimate(flops=1000 * 10**6, bytes_accessed=1000, transcendentals=0)
    half = (products, times // 2, NS, own2 // 2, 2, eigen)
    groups = pieces + blocks[:near]
    right, done = pl.pallas_call(
        functools.partial(near_kernel, places, near_masks, [len(g) for g in groups]),
        in_specs=[smem, smem] + [vmem] * (2 + len(flat(groups))),
        out_specs=[vmem, vmem],
        out_shape=[
            jax.ShapeDtypeStruct((products, 2 * eigen, eigen), BF16),
            jax.ShapeDtypeStruct(half, BF16),
        ],
        compiler_params=params,
        cost_estimate=cost,
        name="near",
    )(source, op_index, slots, partial, *flat(groups))
    groups = blocks[near:]
    return pl.pallas_call(
        functools.partial(far_kernel, near_masks, far_masks, [len(g) for g in groups]),
        in_specs=[vmem] * (2 + len(flat(groups))),
        out_specs=pl.BlockSpec(memory_space=pl.ANY),
        out_shape=jax.ShapeDtypeStruct((products, NS, own2 // 2, 2, times * eigen), BF16),
        scratch_shapes=[
            pltpu.VMEM(half, BF16),
            pltpu.SemaphoreType.DMA(half[:2]),
            pltpu.SemaphoreType.DMA(half[:2]),
        ],
        compiler_params=params,
        cost_estimate=cost,
        name="far",
    )(right, done, *flat(groups))


def swap(array, axis, size, mask):
    return lax.ppermute(array, axis, [(i, i ^ mask) for i in range(size)])


def after(array, *others):
    return lax.optimization_barrier((array, *others))[0]


def per_device(peramb, sink_ops, op_table, row_slot, pair_source, op_index, listed_rows):
    n_cols = lax.axis_size("col")
    n_pair = lax.axis_size("tpair")
    rows, _, eigen = op_table.shape
    slots = row_slot.reshape(-1, LANES)

    def across(array, mask):
        return swap(array, "tpair", n_pair, mask)

    def beside(array):
        return swap(array, "col", n_cols, 1)

    if n_cols != 4 or n_pair != 8 or rows % 32:
        own = jnp.concatenate([op_table[:, 0], op_table[:, 1]], axis=1)
        whole = lax.all_gather(own, "tpair", axis=0, tiled=True)
        half = whole.shape[0] // 2
        mixed = mix(op_index, listed_rows, sink_ops, peramb, [1] * n_cols)
        blocks = [[mixed[0]]] + [[swap(mixed[j], "col", n_cols, j)] for j in range(1, n_cols)]
        partial = assemble([[0]], [[whole[:half]]], pair_source, op_index, slots, eigen)
        return contract(
            [[half]], [[whole[half:]]], partial, pair_source, op_index, slots, blocks
        )
    half = rows // 2
    own = lax.dynamic_slice_in_dim(op_table, lax.axis_index("col") % 2 * half, half, 0)
    own = jnp.concatenate([own[:, 0], own[:, 1]], axis=1)
    beside_own = beside(own)
    z1 = across(own, 2)
    z2 = across(own, 4)
    x0 = across(own, 1)
    mixed = mix(op_index, listed_rows, sink_ops, peramb, [1, 1, 2])
    crossed = swap(mixed[2], "col", n_cols, 2)
    beside_mixed = beside(mixed[1])
    beside_x0 = beside(after(x0, mixed[0]))
    z12 = after(jnp.concatenate([z1, after(z2, x0)]), mixed[0])
    z3 = across(after(own, z12, beside_x0), 6)
    x12 = across(z12, 1)
    spread = [
        ([(0, 0)], own), ([(0, 1)], beside_own),
        ([(1, 0)], x0), ([(1, 1)], beside_x0),
        ([(2, 0), (4, 0)], z12), ([(2, 1), (4, 1)], beside(z12)),
    ]

    def add(found, *earlier):
        places, pieces = [p for p, _ in found], [[piece] for _, piece in found]
        return assemble(places, pieces, pair_source, op_index, slots, eigen, *earlier)

    first = add(spread)
    x3 = across(after(z3, x12, first, beside_mixed), 1)
    spread = [([(6, 0)], z3), ([(6, 1)], beside(z3)), ([(3, 0), (5, 0)], x12)]
    second = add(spread, first)
    spins = [crossed[1:, :, : NS - 1], crossed[1:, :, NS - 1 :]]
    over = [beside(after(some, second)) for some in spins]
    blocks = [[mixed[0]], [beside_mixed], [crossed], over]
    last = beside(after(x3, second))
    third = add([([(3, 1), (5, 1)], beside(x12))], second)
    late, places = [[x3], [last]], [[(7, 0)], [(7, 1)]]
    return contract(places, late, third, pair_source, op_index, slots, blocks)


def solution(mesh):
    in_specs = (
        P("tpair", None, None, "col"),
        P("tpair", None, None, None, None),
        P("tpair", None, None),
        P(),
        P("tpair"),
        P("tpair", None),
        P("tpair", None),
    )
    out_specs = P("tpair", None, "col", None, None)
    return jax.shard_map(
        per_device, mesh=mesh, in_specs=in_specs, out_specs=out_specs, check_vma=False
    )
```

```python
import functools

import jax
import jax.numpy as jnp
from jax import lax
from jax.experimental import pallas as pl
from jax.experimental.pallas import tpu as pltpu
from jax.sharding import PartitionSpec as P

NS = 4
LANES = 128
VMEM_LIMIT = 24 * 1024 * 1024
BF16, F32 = jnp.bfloat16, jnp.float32


def iota(shape, dim):
    return lax.broadcasted_iota(jnp.int32, shape, dim)


def dot(a, b):
    return jnp.dot(a, b, preferred_element_type=F32)


def column(row):
    wide = jnp.broadcast_to(row, (LANES, LANES)).astype(F32)
    return jnp.transpose(wide).astype(jnp.int32)


def one_hot(col, first, width):
    tiles = [
        jnp.where(col - (first + n) == iota((col.shape[0], LANES), 1), 1.0, 0.0)
        for n in range(0, width, LANES)
    ]
    return jnp.concatenate(tiles, axis=1).astype(BF16)


def mix_kernel(op_ref, listed_ref, sink_ref, peramb_ref, *refs):
    outs, (left, held, sems) = refs[:-3], refs[-3:]
    n_cols = sum(out.shape[0] for out in outs)
    products, listed = listed_ref.shape
    eigen, local_cols = sink_ref.shape[-1], peramb_ref.shape[-1]
    loads = [
        pltpu.make_async_copy(
            peramb_ref.at[0, :, pl.ds(s * eigen, eigen), :], held.at[s], sems.at[s]
        )
        for s in range(NS)
    ]
    for load in loads:
        load.start()
    own2 = 2 * listed // n_cols
    me = lax.axis_index("col")
    row = iota((2 * listed, 2 * listed), 0)
    wanted = ((row // own2) ^ me) * (own2 // 2) + (row % own2) // 2 + (row % 2) * listed
    order = jnp.where(wanted == iota((2 * listed, 2 * listed), 1), 1.0, 0.0).astype(BF16)
    for k in range(products):
        op = op_ref[k, 0]
        onehot = one_hot(column(listed_ref[k : k + 1, :]), 0, eigen)
        real = dot(onehot, sink_ref[0, op, 0])
        imag = dot(onehot, sink_ref[0, op, 1])
        top = jnp.concatenate([real, -imag], axis=1)
        bottom = jnp.concatenate([imag, real], axis=1)
        both = jnp.concatenate([top, bottom], axis=0).astype(BF16)
        rows = dot(order, both).astype(BF16)
        for j in range(n_cols):
            at = (j * products + k) * own2
            left[at : at + own2, :] = rows[j * own2 : (j + 1) * own2]
    for s in range(NS):
        loads[s].wait()
        mixed = dot(left[...], held[s].reshape(2 * eigen, local_cols)).astype(BF16)
        j = 0
        for out in outs:
            for n in range(out.shape[0]):
                for k in range(products):
                    at = (j * products + k) * own2
                    out[n, k, s] = mixed[at : at + own2]
                j += 1


def mix(op_index, listed_rows, sink_ops, peramb, groups):
    products, listed = listed_rows.shape
    eigen = sink_ops.shape[-1]
    local_cols = peramb.shape[3]
    own2 = 2 * listed // sum(groups)
    blocks = [
        jax.ShapeDtypeStruct((group, products, NS, own2, local_cols), BF16) for group in groups
    ]
    vmem = pl.BlockSpec(memory_space=pltpu.VMEM)
    return pl.pallas_call(
        mix_kernel,
        in_specs=[
            pl.BlockSpec(memory_space=pltpu.SMEM), vmem, vmem, pl.BlockSpec(memory_space=pltpu.HBM)
        ],
        out_specs=[vmem] * len(groups),
        out_shape=blocks,
        scratch_shapes=[
            pltpu.VMEM((products * 2 * listed, 2 * eigen), BF16),
            pltpu.VMEM((NS, 2, eigen, local_cols), BF16),
            pltpu.SemaphoreType.DMA((NS,)),
        ],
        compiler_params=pltpu.CompilerParams(vmem_limit_bytes=VMEM_LIMIT),
        cost_estimate=pl.CostEstimate(flops=1000, bytes_accessed=1000, transcendentals=0),
        name="mix",
    )(op_index, listed_rows, sink_ops, pltpu.with_memory_space_constraint(peramb, pltpu.HBM))


def add_pieces(places, scalars_ref, slot_ref, pieces, products, eigen):
    source_ref, op_ref = scalars_ref
    blocks = eigen // LANES
    nops = slot_ref.shape[0] // blocks // 2
    pair, side = lax.axis_index("tpair"), lax.axis_index("col") % 2
    cols = []
    for k in products:
        op = source_ref[0] * nops + op_ref[k, 1]
        cols += [
            column(slot_ref[pl.ds(op * blocks + b, 1), :]) for b in range(blocks)
        ]
    col = jnp.concatenate(cols, axis=0)
    tiles, tables = [], []
    for owners, parts in zip(places, pieces):
        height = sum(part.shape[0] for part in parts) // len(owners)
        for owner in owners:
            first = owner
            if isinstance(owner, tuple):
                first = (2 * (pair ^ owner[0]) + (side ^ owner[1])) * height
            tiles.append(one_hot(col, first, height))
        tables += [part[...] for part in parts]
    return dot(jnp.concatenate(tiles, axis=1), jnp.concatenate(tables, axis=0))


def grouped(counts, refs):
    groups = []
    for count in counts:
        groups.append(refs[:count])
        refs = refs[count:]
    return groups, refs


def assemble_kernel(places, counts, source_ref, op_ref, slot_ref, *refs):
    pieces, (out_ref,) = grouped(counts, refs)
    products, eigen = out_ref.shape[0], out_ref.shape[2]
    total = add_pieces(places, (source_ref, op_ref), slot_ref, pieces, range(products), eigen)
    total = total.astype(BF16)
    for k in range(products):
        rows = slice(k * eigen, (k + 1) * eigen)
        out_ref[k, :eigen] = total[rows, :eigen]
        out_ref[k, eigen:] = total[rows, eigen:]


def assemble(places, pieces, source, op_index, slots, eigen):
    products = op_index.shape[0]
    vmem = pl.BlockSpec(memory_space=pltpu.VMEM)
    smem = pl.BlockSpec(memory_space=pltpu.SMEM)
    return pl.pallas_call(
        functools.partial(assemble_kernel, places, [len(group) for group in pieces]),
        in_specs=[smem, smem] + [vmem] * (1 + sum(len(group) for group in pieces)),
        out_specs=vmem,
        out_shape=jax.ShapeDtypeStruct((products, 2 * eigen, eigen), BF16),
        compiler_params=pltpu.CompilerParams(vmem_limit_bytes=VMEM_LIMIT),
        cost_estimate=pl.CostEstimate(flops=1000, bytes_accessed=1000, transcendentals=0),
        name="assemble",
    )(source, op_index, slots, *[part for group in pieces for part in group])


def block_rows(parts, k):
    found = [part[0, k] for part in parts]
    return jnp.concatenate([f.reshape(-1, f.shape[-1]) for f in found], axis=0)


def times_right(blocks, masks, right, k):
    eigen = right.shape[2]
    local_cols = blocks[0][0].shape[4]
    me = lax.axis_index("col")
    per_time = eigen // local_cols
    direct = [block_rows(parts, k) for parts in blocks]
    rows = direct[0].shape[0]
    row, other = iota((rows, rows), 0), iota((rows, rows), 1)
    signs = jnp.where(row % 2 == 1, 1.0, -1.0)
    turn = jnp.where(other == row + 1 - 2 * (row % 2), signs, 0.0).astype(BF16)
    turned = [dot(turn, x).astype(BF16) for x in direct]
    if per_time == 1:
        lhs = jnp.concatenate(
            [jnp.concatenate(direct, axis=0), jnp.concatenate(turned, axis=0)], axis=1
        )
        whole = dot(lhs, right[k]).astype(BF16)
        results = [whole[n * rows : (n + 1) * rows] for n in range(len(masks))]
    else:
        results = []
        for n, mask in enumerate(masks):
            first = pl.multiple_of(((me ^ mask) % per_time) * local_cols, local_cols)
            second = pl.multiple_of(eigen + first, local_cols)
            part = dot(direct[n], right[k, pl.ds(first, local_cols), :])
            part += dot(turned[n], right[k, pl.ds(second, local_cols), :])
            if n % per_time:
                results[-1] += part
            else:
                results.append(part)
        results = [result.astype(BF16) for result in results]
    times = [(me ^ mask) // per_time for mask in masks[::per_time]]
    return list(zip(times, results))


def near_kernel(places, masks, counts, source_ref, op_ref, slot_ref, partial_ref, *refs):
    groups, (right, done) = grouped(counts, refs)
    pieces, blocks = groups[: len(places)], groups[len(places) :]
    products, eigen = right.shape[0], right.shape[2]
    scalars = (source_ref, op_ref)
    for k in range(products):
        total = add_pieces(places, scalars, slot_ref, pieces, [k], eigen).astype(BF16)
        right[k, :eigen] = partial_ref[k, :eigen] + total[:, :eigen]
        right[k, eigen:] = partial_ref[k, eigen:] + total[:, eigen:]
    for k in range(products):
        for n, (_, result) in enumerate(times_right(blocks, masks, right, k)):
            done[k, n] = result.reshape(done.shape[2:])


def far_kernel(near_masks, masks, counts, right, near_ref, *refs):
    blocks, (out_ref, done, near_sems, sems) = grouped(counts, refs)
    products, eigen = right.shape[0], right.shape[2]
    near_times, times = near_ref.shape[1], done.shape[1]
    per_time = len(masks) // times
    me = lax.axis_index("col")

    def send(source, k, time, sem):
        at = pl.multiple_of(time * eigen, eigen)
        copy = pltpu.make_async_copy(source, out_ref.at[k, :, :, :, pl.ds(at, eigen)], sem)
        copy.start()
        return copy

    copies = []
    for k in range(products):
        for n in range(near_times):
            time = (me ^ near_masks[n * per_time]) // per_time
            copies.append(send(near_ref.at[k, n], k, time, near_sems.at[k, n]))
    for k in range(products):
        for n, (time, result) in enumerate(times_right(blocks, masks, right, k)):
            done[k, n] = result.reshape(done.shape[2:])
            copies.append(send(done.at[k, n], k, time, sems.at[k, n]))
    for copy in copies:
        copy.wait()


def flat(groups):
    return [part for group in groups for part in group]


def contract(places, pieces, partial, source, op_index, slots, blocks):
    _, products, _, own2, local_cols = blocks[0][0].shape
    n_cols = len(blocks)
    eigen = partial.shape[2]
    times = n_cols * local_cols // eigen
    near = n_cols // 2
    near_masks, far_masks = list(range(near)), list(range(near, n_cols))
    vmem = pl.BlockSpec(memory_space=pltpu.VMEM)
    smem = pl.BlockSpec(memory_space=pltpu.SMEM)
    params = pltpu.CompilerParams(vmem_limit_bytes=VMEM_LIMIT)
    cost = pl.CostEstimate(flops=1000 * 10**6, bytes_accessed=1000, transcendentals=0)
    half = (products, times // 2, NS, own2 // 2, 2, eigen)
    groups = pieces + blocks[:near]
    right, done = pl.pallas_call(
        functools.partial(near_kernel, places, near_masks, [len(g) for g in groups]),
        in_specs=[smem, smem] + [vmem] * (2 + len(flat(groups))),
        out_specs=[vmem, vmem],
        out_shape=[
            jax.ShapeDtypeStruct((products, 2 * eigen, eigen), BF16),
            jax.ShapeDtypeStruct(half, BF16),
        ],
        compiler_params=params,
        cost_estimate=cost,
        name="near",
    )(source, op_index, slots, partial, *flat(groups))
    groups = blocks[near:]
    return pl.pallas_call(
        functools.partial(far_kernel, near_masks, far_masks, [len(g) for g in groups]),
        in_specs=[vmem] * (2 + len(flat(groups))),
        out_specs=pl.BlockSpec(memory_space=pl.ANY),
        out_shape=jax.ShapeDtypeStruct((products, NS, own2 // 2, 2, times * eigen), BF16),
        scratch_shapes=[
            pltpu.VMEM(half, BF16),
            pltpu.SemaphoreType.DMA(half[:2]),
            pltpu.SemaphoreType.DMA(half[:2]),
        ],
        compiler_params=params,
        cost_estimate=cost,
        name="far",
    )(right, done, *flat(groups))


def swap(array, axis, size, mask):
    return lax.ppermute(array, axis, [(i, i ^ mask) for i in range(size)])


def after(array, *others):
    return lax.optimization_barrier((array, *others))[0]


def per_device(peramb, sink_ops, op_table, row_slot, pair_source, op_index, listed_rows):
    n_cols = lax.axis_size("col")
    n_pair = lax.axis_size("tpair")
    rows, _, eigen = op_table.shape
    slots = row_slot.reshape(-1, LANES)

    def across(array, mask):
        return swap(array, "tpair", n_pair, mask)

    def beside(array):
        return swap(array, "col", n_cols, 1)

    if n_cols != 4 or n_pair != 8 or rows % 32:
        own = jnp.concatenate([op_table[:, 0], op_table[:, 1]], axis=1)
        whole = lax.all_gather(own, "tpair", axis=0, tiled=True)
        half = whole.shape[0] // 2
        mixed = mix(op_index, listed_rows, sink_ops, peramb, [1] * n_cols)
        blocks = [[mixed[0]]] + [[swap(mixed[j], "col", n_cols, j)] for j in range(1, n_cols)]
        partial = assemble([[0]], [[whole[:half]]], pair_source, op_index, slots, eigen)
        return contract(
            [[half]], [[whole[half:]]], partial, pair_source, op_index, slots, blocks
        )
    half = rows // 2
    own = lax.dynamic_slice_in_dim(op_table, lax.axis_index("col") % 2 * half, half, 0)
    own = jnp.concatenate([own[:, 0], own[:, 1]], axis=1)
    beside_own = beside(own)
    z1 = across(own, 2)
    z2 = across(own, 4)
    x0 = across(own, 1)
    mixed = mix(op_index, listed_rows, sink_ops, peramb, [1, 1, 2])
    crossed = swap(mixed[2], "col", n_cols, 2)
    beside_mixed = beside(mixed[1])
    beside_x0 = beside(after(x0, mixed[0]))
    z12 = after(jnp.concatenate([z1, after(z2, x0)]), mixed[0])
    z3 = across(after(own, z12), 6)
    x12 = across(z12, 1)
    x3 = across(after(z3, x12, beside_x0, beside_mixed), 1)
    early = [
        ([(0, 0)], own), ([(0, 1)], beside_own),
        ([(1, 0)], x0), ([(1, 1)], beside_x0),
        ([(2, 0), (4, 0)], z12), ([(2, 1), (4, 1)], beside(z12)),
        ([(6, 0)], z3), ([(6, 1)], beside(z3)),
        ([(3, 0), (5, 0)], x12),
    ]
    places, pieces = [p for p, _ in early], [[piece] for _, piece in early]
    partial = assemble(places, pieces, pair_source, op_index, slots, eigen)
    spins = [crossed[1:, :, : NS - 1], crossed[1:, :, NS - 1 :]]
    over = [beside(after(some, partial)) for some in spins]
    blocks = [[mixed[0]], [beside_mixed], [crossed], over]
    late = [[x3], [beside(after(x3, partial))], [beside(x12)]]
    places = [[(7, 0)], [(7, 1)], [(3, 1), (5, 1)]]
    return contract(places, late, partial, pair_source, op_index, slots, blocks)


def solution(mesh):
    in_specs = (
        P("tpair", None, None, "col"),
        P("tpair", None, None, None, None),
        P("tpair", None, None),
        P(),
        P("tpair"),
        P("tpair", None),
        P("tpair", None),
    )
    out_specs = P("tpair", None, "col", None, None)
    return jax.shard_map(
        per_device, mesh=mesh, in_specs=in_specs, out_specs=out_specs, check_vma=False
    )
```

```python
import functools

import jax
import jax.numpy as jnp
from jax import lax
from jax.experimental import pallas as pl
from jax.experimental.pallas import tpu as pltpu
from jax.sharding import PartitionSpec as P

NS = 4
LANES = 128
VMEM_LIMIT = 24 * 1024 * 1024
BF16, F32 = jnp.bfloat16, jnp.float32


def iota(shape, dim):
    return lax.broadcasted_iota(jnp.int32, shape, dim)


def dot(a, b):
    return jnp.dot(a, b, preferred_element_type=F32)


def column(row):
    wide = jnp.broadcast_to(row, (LANES, LANES)).astype(F32)
    return jnp.transpose(wide).astype(jnp.int32)


def one_hot(col, first, width):
    tiles = [
        jnp.where(col - (first + n) == iota((col.shape[0], LANES), 1), 1.0, 0.0)
        for n in range(0, width, LANES)
    ]
    return jnp.concatenate(tiles, axis=1).astype(BF16)


def mix_kernel(op_ref, listed_ref, sink_ref, peramb_ref, *refs):
    outs, (left, held, sems) = refs[:-3], refs[-3:]
    n_cols = sum(out.shape[0] for out in outs)
    products, listed = listed_ref.shape
    eigen, local_cols = sink_ref.shape[-1], peramb_ref.shape[-1]
    loads = [
        pltpu.make_async_copy(
            peramb_ref.at[0, :, pl.ds(s * eigen, eigen), :], held.at[s], sems.at[s]
        )
        for s in range(NS)
    ]
    for load in loads[:2]:
        load.start()
    own2 = 2 * listed // n_cols
    me = lax.axis_index("col")
    row = iota((2 * listed, 2 * listed), 0)
    wanted = ((row // own2) ^ me) * (own2 // 2) + (row % own2) // 2 + (row % 2) * listed
    order = jnp.where(wanted == iota((2 * listed, 2 * listed), 1), 1.0, 0.0).astype(BF16)
    for k in range(products):
        op = op_ref[k, 0]
        onehot = one_hot(column(listed_ref[k : k + 1, :]), 0, eigen)
        real = dot(onehot, sink_ref[0, op, 0])
        imag = dot(onehot, sink_ref[0, op, 1])
        top = jnp.concatenate([real, -imag], axis=1)
        bottom = jnp.concatenate([imag, real], axis=1)
        both = jnp.concatenate([top, bottom], axis=0).astype(BF16)
        rows = dot(order, both).astype(BF16)
        for j in range(n_cols):
            at = (j * products + k) * own2
            left[at : at + own2, :] = rows[j * own2 : (j + 1) * own2]
    for s in range(NS):
        loads[s].wait()
        if s + 2 < NS:
            loads[s + 2].start()
        mixed = dot(left[...], held[s].reshape(2 * eigen, local_cols)).astype(BF16)
        j = 0
        for out in outs:
            for n in range(out.shape[0]):
                for k in range(products):
                    at = (j * products + k) * own2
                    out[n, k, s] = mixed[at : at + own2]
                j += 1


def mix(op_index, listed_rows, sink_ops, peramb, groups):
    products, listed = listed_rows.shape
    eigen = sink_ops.shape[-1]
    local_cols = peramb.shape[3]
    own2 = 2 * listed // sum(groups)
    blocks = [
        jax.ShapeDtypeStruct((group, products, NS, own2, local_cols), BF16) for group in groups
    ]
    vmem = pl.BlockSpec(memory_space=pltpu.VMEM)
    return pl.pallas_call(
        mix_kernel,
        in_specs=[
            pl.BlockSpec(memory_space=pltpu.SMEM), vmem, vmem, pl.BlockSpec(memory_space=pltpu.HBM)
        ],
        out_specs=[vmem] * len(groups),
        out_shape=blocks,
        scratch_shapes=[
            pltpu.VMEM((products * 2 * listed, 2 * eigen), BF16),
            pltpu.VMEM((NS, 2, eigen, local_cols), BF16),
            pltpu.SemaphoreType.DMA((NS,)),
        ],
        compiler_params=pltpu.CompilerParams(vmem_limit_bytes=VMEM_LIMIT),
        cost_estimate=pl.CostEstimate(flops=1000, bytes_accessed=1000, transcendentals=0),
        name="mix",
    )(op_index, listed_rows, sink_ops, pltpu.with_memory_space_constraint(peramb, pltpu.HBM))


def add_pieces(places, scalars_ref, slot_ref, pieces, products, eigen):
    source_ref, op_ref = scalars_ref
    blocks = eigen // LANES
    nops = slot_ref.shape[0] // blocks // 2
    pair, side = lax.axis_index("tpair"), lax.axis_index("col") % 2
    cols = []
    for k in products:
        op = source_ref[0] * nops + op_ref[k, 1]
        cols += [
            column(slot_ref[pl.ds(op * blocks + b, 1), :]) for b in range(blocks)
        ]
    col = jnp.concatenate(cols, axis=0)
    tiles, tables = [], []
    for owners, parts in zip(places, pieces):
        height = sum(part.shape[0] for part in parts) // len(owners)
        for owner in owners:
            first = owner
            if isinstance(owner, tuple):
                first = (2 * (pair ^ owner[0]) + (side ^ owner[1])) * height
            tiles.append(one_hot(col, first, height))
        tables += [part[...] for part in parts]
    return dot(jnp.concatenate(tiles, axis=1), jnp.concatenate(tables, axis=0))


def flat(groups):
    return [part for group in groups for part in group]


def grouped(counts, refs):
    groups = []
    for count in counts:
        groups.append(refs[:count])
        refs = refs[count:]
    return groups, refs


def assemble_kernel(places, counts, source_ref, op_ref, slot_ref, *refs):
    pieces, (*earlier, out_ref) = grouped(counts, refs)
    products, eigen = out_ref.shape[0], out_ref.shape[2]
    for k in range(products):
        total = add_pieces(places, (source_ref, op_ref), slot_ref, pieces, [k], eigen)
        total = total.astype(BF16)
        real, imag = total[:, :eigen], total[:, eigen:]
        if earlier:
            real += earlier[0][k, :eigen]
            imag += earlier[0][k, eigen:]
        out_ref[k, :eigen] = real
        out_ref[k, eigen:] = imag


def assemble(places, pieces, source, op_index, slots, eigen, *earlier):
    products = op_index.shape[0]
    vmem = pl.BlockSpec(memory_space=pltpu.VMEM)
    smem = pl.BlockSpec(memory_space=pltpu.SMEM)
    inputs = [*flat(pieces), *earlier]
    return pl.pallas_call(
        functools.partial(assemble_kernel, places, [len(group) for group in pieces]),
        in_specs=[smem, smem] + [vmem] * (1 + len(inputs)),
        out_specs=vmem,
        out_shape=jax.ShapeDtypeStruct((products, 2 * eigen, eigen), BF16),
        compiler_params=pltpu.CompilerParams(vmem_limit_bytes=VMEM_LIMIT),
        cost_estimate=pl.CostEstimate(flops=1000, bytes_accessed=1000, transcendentals=0),
        name="assemble",
    )(source, op_index, slots, *inputs)


def block_rows(parts, k):
    found = [part[0, k] for part in parts]
    return jnp.concatenate([f.reshape(-1, f.shape[-1]) for f in found], axis=0)


def times_right(blocks, masks, right, k):
    eigen = right.shape[2]
    local_cols = blocks[0][0].shape[4]
    me = lax.axis_index("col")
    per_time = eigen // local_cols
    direct = [block_rows(parts, k) for parts in blocks]
    rows = direct[0].shape[0]
    odd = iota((rows, local_cols), 0) % 2 == 1
    turned = []
    for x in direct:
        wide = x.astype(F32)
        y = jnp.where(odd, pltpu.roll(wide, 1, 0), -pltpu.roll(wide, rows - 1, 0))
        turned.append(y.astype(BF16))
    if per_time == 1:
        lhs = jnp.concatenate(
            [jnp.concatenate(direct, axis=0), jnp.concatenate(turned, axis=0)], axis=1
        )
        whole = dot(lhs, right[k]).astype(BF16)
        results = [whole[n * rows : (n + 1) * rows] for n in range(len(masks))]
    else:
        results = []
        for n, mask in enumerate(masks):
            first = pl.multiple_of(((me ^ mask) % per_time) * local_cols, local_cols)
            second = pl.multiple_of(eigen + first, local_cols)
            part = dot(direct[n], right[k, pl.ds(first, local_cols), :])
            part += dot(turned[n], right[k, pl.ds(second, local_cols), :])
            if n % per_time:
                results[-1] += part
            else:
                results.append(part)
        results = [result.astype(BF16) for result in results]
    times = [(me ^ mask) // per_time for mask in masks[::per_time]]
    return list(zip(times, results))


def near_kernel(places, masks, counts, source_ref, op_ref, slot_ref, partial_ref, *refs):
    groups, (right, done) = grouped(counts, refs)
    pieces, blocks = groups[: len(places)], groups[len(places) :]
    products, eigen = right.shape[0], right.shape[2]
    scalars = (source_ref, op_ref)
    for k in range(products):
        total = add_pieces(places, scalars, slot_ref, pieces, [k], eigen).astype(BF16)
        right[k, :eigen] = partial_ref[k, :eigen] + total[:, :eigen]
        right[k, eigen:] = partial_ref[k, eigen:] + total[:, eigen:]
    for k in range(products):
        for n, (_, result) in enumerate(times_right(blocks, masks, right, k)):
            done[k, n] = result.reshape(done.shape[2:])


def far_kernel(near_masks, masks, counts, right, near_ref, *refs):
    blocks, (out_ref, done, near_sems, sems) = grouped(counts, refs)
    products, eigen = right.shape[0], right.shape[2]
    near_times, times = near_ref.shape[1], done.shape[1]
    per_time = len(masks) // times
    me = lax.axis_index("col")

    def send(source, k, time, sem):
        at = pl.multiple_of(time * eigen, eigen)
        copy = pltpu.make_async_copy(source, out_ref.at[k, :, :, :, pl.ds(at, eigen)], sem)
        copy.start()
        return copy

    copies = []
    for k in range(products):
        for n in range(near_times):
            time = (me ^ near_masks[n * per_time]) // per_time
            copies.append(send(near_ref.at[k, n], k, time, near_sems.at[k, n]))
    for k in range(products):
        for n, (time, result) in enumerate(times_right(blocks, masks, right, k)):
            done[k, n] = result.reshape(done.shape[2:])
            copies.append(send(done.at[k, n], k, time, sems.at[k, n]))
    for copy in copies:
        copy.wait()


def contract(places, pieces, partial, source, op_index, slots, blocks):
    _, products, _, own2, local_cols = blocks[0][0].shape
    n_cols = len(blocks)
    eigen = partial.shape[2]
    times = n_cols * local_cols // eigen
    near = n_cols // 2
    near_masks, far_masks = list(range(near)), list(range(near, n_cols))
    vmem = pl.BlockSpec(memory_space=pltpu.VMEM)
    smem = pl.BlockSpec(memory_space=pltpu.SMEM)
    params = pltpu.CompilerParams(vmem_limit_bytes=VMEM_LIMIT)
    cost = pl.CostEstimate(flops=3000 * 10**6, bytes_accessed=1000, transcendentals=0)
    half = (products, times // 2, NS, own2 // 2, 2, eigen)
    groups = pieces + blocks[:near]
    right, done = pl.pallas_call(
        functools.partial(near_kernel, places, near_masks, [len(g) for g in groups]),
        in_specs=[smem, smem] + [vmem] * (2 + len(flat(groups))),
        out_specs=[vmem, vmem],
        out_shape=[
            jax.ShapeDtypeStruct((products, 2 * eigen, eigen), BF16),
            jax.ShapeDtypeStruct(half, BF16),
        ],
        compiler_params=params,
        cost_estimate=cost,
        name="near",
    )(source, op_index, slots, partial, *flat(groups))
    groups = blocks[near:]
    return pl.pallas_call(
        functools.partial(far_kernel, near_masks, far_masks, [len(g) for g in groups]),
        in_specs=[vmem] * (2 + len(flat(groups))),
        out_specs=pl.BlockSpec(memory_space=pl.ANY),
        out_shape=jax.ShapeDtypeStruct((products, NS, own2 // 2, 2, times * eigen), BF16),
        scratch_shapes=[
            pltpu.VMEM(half, BF16),
            pltpu.SemaphoreType.DMA(half[:2]),
            pltpu.SemaphoreType.DMA(half[:2]),
        ],
        compiler_params=params,
        cost_estimate=cost,
        name="far",
    )(right, done, *flat(groups))


def swap(array, axis, size, mask):
    return lax.ppermute(array, axis, [(i, i ^ mask) for i in range(size)])


def after(array, *others):
    return lax.optimization_barrier((array, *others))[0]


def per_device(peramb, sink_ops, op_table, row_slot, pair_source, op_index, listed_rows):
    n_cols = lax.axis_size("col")
    n_pair = lax.axis_size("tpair")
    rows, _, eigen = op_table.shape
    slots = row_slot.reshape(-1, LANES)

    def across(array, mask):
        return swap(array, "tpair", n_pair, mask)

    def beside(array):
        return swap(array, "col", n_cols, 1)

    if n_cols != 4 or n_pair != 8 or rows % 32:
        own = jnp.concatenate([op_table[:, 0], op_table[:, 1]], axis=1)
        whole = lax.all_gather(own, "tpair", axis=0, tiled=True)
        half = whole.shape[0] // 2
        mixed = mix(op_index, listed_rows, sink_ops, peramb, [1] * n_cols)
        blocks = [[mixed[0]]] + [[swap(mixed[j], "col", n_cols, j)] for j in range(1, n_cols)]
        partial = assemble([[0]], [[whole[:half]]], pair_source, op_index, slots, eigen)
        return contract(
            [[half]], [[whole[half:]]], partial, pair_source, op_index, slots, blocks
        )
    half = rows // 2
    own = lax.dynamic_slice_in_dim(op_table, lax.axis_index("col") % 2 * half, half, 0)
    own = jnp.concatenate([own[:, 0], own[:, 1]], axis=1)
    beside_own = beside(own)
    z1 = across(own, 2)
    z2 = across(own, 4)
    x0 = across(own, 1)
    mixed = mix(op_index, listed_rows, sink_ops, peramb, [1, 1, 2])
    crossed = swap(mixed[2], "col", n_cols, 2)
    beside_mixed = beside(mixed[1])
    beside_x0 = beside(after(x0, mixed[0]))
    z12 = after(jnp.concatenate([z1, after(z2, x0)]), mixed[0])
    z3 = across(after(own, z12, beside_x0), 6)
    x12 = across(z12, 1)
    x3 = across(after(z3, beside_x0), 1)
    beside_x12 = [beside(x12[:half]), beside(x12[half:])]

    def add(found, *earlier):
        places = [place for place, _ in found]
        pieces = [piece if isinstance(piece, list) else [piece] for _, piece in found]
        return assemble(places, pieces, pair_source, op_index, slots, eigen, *earlier)

    first = add([
        ([(0, 0)], own), ([(0, 1)], beside_own),
        ([(1, 0)], x0), ([(1, 1)], beside_x0),
        ([(2, 0), (4, 0)], z12), ([(2, 1), (4, 1)], beside(z12)),
        ([(6, 0)], z3), ([(6, 1)], beside(z3)),
    ])
    spins = [crossed[1:, :, s : s + 1] for s in range(NS)]
    over = [beside(after(some, first)) for some in spins]
    blocks = [[mixed[0]], [beside_mixed], [crossed], over]
    last = beside(after(x3, first))
    second = add([([(3, 0), (5, 0)], x12), ([(3, 1), (5, 1)], beside_x12)], first)
    late, places = [[x3], [last]], [[(7, 0)], [(7, 1)]]
    return contract(places, late, second, pair_source, op_index, slots, blocks)


def solution(mesh):
    in_specs = (
        P("tpair", None, None, "col"),
        P("tpair", None, None, None, None),
        P("tpair", None, None),
        P(),
        P("tpair"),
        P("tpair", None),
        P("tpair", None),
    )
    out_specs = P("tpair", None, "col", None, None)
    return jax.shard_map(
        per_device, mesh=mesh, in_specs=in_specs, out_specs=out_specs, check_vma=False
    )
```

```python
import functools

import jax
import jax.numpy as jnp
from jax import lax
from jax.experimental import pallas as pl
from jax.experimental.pallas import tpu as pltpu
from jax.sharding import PartitionSpec as P

NS = 4
LANES = 128
VMEM_LIMIT = 24 * 1024 * 1024
BF16, F32 = jnp.bfloat16, jnp.float32


def iota(shape, dim):
    return lax.broadcasted_iota(jnp.int32, shape, dim)


def dot(a, b):
    return jnp.dot(a, b, preferred_element_type=F32)


def column(row):
    wide = jnp.broadcast_to(row, (LANES, LANES)).astype(F32)
    return jnp.transpose(wide).astype(jnp.int32)


def one_hot(col, first, width):
    tiles = [
        jnp.where(col - (first + n) == iota((col.shape[0], LANES), 1), 1.0, 0.0)
        for n in range(0, width, LANES)
    ]
    return jnp.concatenate(tiles, axis=1).astype(BF16)


def mix_kernel(op_ref, listed_ref, sink_ref, peramb_ref, *refs):
    outs, (left, held, sems) = refs[:-3], refs[-3:]
    n_cols = sum(out.shape[0] for out in outs)
    products, listed = listed_ref.shape
    eigen, local_cols = sink_ref.shape[-1], peramb_ref.shape[-1]
    loads = [
        pltpu.make_async_copy(
            peramb_ref.at[0, :, pl.ds(s * eigen, eigen), :], held.at[s], sems.at[s]
        )
        for s in range(NS)
    ]
    for load in loads:
        load.start()
    own2 = 2 * listed // n_cols
    me = lax.axis_index("col")
    row = iota((2 * listed, 2 * listed), 0)
    wanted = ((row // own2) ^ me) * (own2 // 2) + (row % own2) // 2 + (row % 2) * listed
    order = jnp.where(wanted == iota((2 * listed, 2 * listed), 1), 1.0, 0.0).astype(BF16)
    for k in range(products):
        op = op_ref[k, 0]
        onehot = one_hot(column(listed_ref[k : k + 1, :]), 0, eigen)
        real = dot(onehot, sink_ref[0, op, 0])
        imag = dot(onehot, sink_ref[0, op, 1])
        top = jnp.concatenate([real, -imag], axis=1)
        bottom = jnp.concatenate([imag, real], axis=1)
        both = jnp.concatenate([top, bottom], axis=0).astype(BF16)
        rows = dot(order, both).astype(BF16)
        for j in range(n_cols):
            at = (j * products + k) * own2
            left[at : at + own2, :] = rows[j * own2 : (j + 1) * own2]
    for s in range(NS):
        loads[s].wait()
        mixed = dot(left[...], held[s].reshape(2 * eigen, local_cols)).astype(BF16)
        j = 0
        for out in outs:
            for n in range(out.shape[0]):
                for k in range(products):
                    at = (j * products + k) * own2
                    out[n, k, s] = mixed[at : at + own2]
                j += 1


def mix(op_index, listed_rows, sink_ops, peramb, groups):
    products, listed = listed_rows.shape
    eigen = sink_ops.shape[-1]
    local_cols = peramb.shape[3]
    own2 = 2 * listed // sum(groups)
    blocks = [
        jax.ShapeDtypeStruct((group, products, NS, own2, local_cols), BF16) for group in groups
    ]
    vmem = pl.BlockSpec(memory_space=pltpu.VMEM)
    return pl.pallas_call(
        mix_kernel,
        in_specs=[
            pl.BlockSpec(memory_space=pltpu.SMEM), vmem, vmem, pl.BlockSpec(memory_space=pltpu.HBM)
        ],
        out_specs=[vmem] * len(groups),
        out_shape=blocks,
        scratch_shapes=[
            pltpu.VMEM((products * 2 * listed, 2 * eigen), BF16),
            pltpu.VMEM((NS, 2, eigen, local_cols), BF16),
            pltpu.SemaphoreType.DMA((NS,)),
        ],
        compiler_params=pltpu.CompilerParams(vmem_limit_bytes=VMEM_LIMIT),
        cost_estimate=pl.CostEstimate(flops=1000, bytes_accessed=1000, transcendentals=0),
        name="mix",
    )(op_index, listed_rows, sink_ops, pltpu.with_memory_space_constraint(peramb, pltpu.HBM))


def add_pieces(places, scalars_ref, slot_ref, pieces, products, eigen):
    nops, source_ref, op_ref = scalars_ref
    blocks = eigen // LANES
    pair, side = lax.axis_index("tpair"), lax.axis_index("col") % 2
    cols = []
    for k in products:
        op = source_ref[0] * nops + op_ref[k, 1]
        cols += [
            column(slot_ref[pl.ds(op * blocks + b, 1), :]) for b in range(blocks)
        ]
    col = jnp.concatenate(cols, axis=0)
    tiles, tables = [], []
    for owners, parts in zip(places, pieces):
        height = sum(part.shape[0] for part in parts) // len(owners)
        for owner in owners:
            first = owner
            if isinstance(owner, tuple):
                first = (2 * (pair ^ owner[0]) + (side ^ owner[1])) * height
            tiles.append(one_hot(col, first, height))
        tables += [part[...] for part in parts]
    return dot(jnp.concatenate(tiles, axis=1), jnp.concatenate(tables, axis=0))


def grouped(counts, refs):
    groups = []
    for count in counts:
        groups.append(refs[:count])
        refs = refs[count:]
    return groups, refs


def assemble_kernel(places, counts, nops, source_ref, op_ref, slot_ref, *refs):
    pieces, (out_ref,) = grouped(counts, refs)
    products, eigen = out_ref.shape[0], out_ref.shape[2]
    total = add_pieces(
        places, (nops, source_ref, op_ref), slot_ref, pieces, range(products), eigen
    )
    total = total.astype(BF16)
    for k in range(products):
        rows = slice(k * eigen, (k + 1) * eigen)
        out_ref[k, :eigen] = total[rows, :eigen]
        out_ref[k, eigen:] = total[rows, eigen:]


def assemble(places, pieces, nops, source, op_index, slots, eigen):
    products = op_index.shape[0]
    vmem = pl.BlockSpec(memory_space=pltpu.VMEM)
    smem = pl.BlockSpec(memory_space=pltpu.SMEM)
    return pl.pallas_call(
        functools.partial(assemble_kernel, places, [len(group) for group in pieces], nops),
        in_specs=[smem, smem] + [vmem] * (1 + sum(len(group) for group in pieces)),
        out_specs=vmem,
        out_shape=jax.ShapeDtypeStruct((products, 2 * eigen, eigen), BF16),
        compiler_params=pltpu.CompilerParams(vmem_limit_bytes=VMEM_LIMIT),
        cost_estimate=pl.CostEstimate(flops=1000, bytes_accessed=1000, transcendentals=0),
        name="assemble",
    )(source, op_index, slots, *[part for group in pieces for part in group])


def block_rows(parts, k):
    found = [part[0, k] for part in parts]
    return jnp.concatenate([f.reshape(-1, f.shape[-1]) for f in found], axis=0)


def times_right(blocks, masks, right, k):
    eigen = right.shape[2]
    local_cols = blocks[0][0].shape[4]
    me = lax.axis_index("col")
    per_time = eigen // local_cols
    direct = [block_rows(parts, k) for parts in blocks]
    rows = direct[0].shape[0]
    odd = iota((rows, local_cols), 0) % 2 == 1
    turned = []
    for x in direct:
        wide = x.astype(F32)
        y = jnp.where(odd, pltpu.roll(wide, 1, 0), -pltpu.roll(wide, rows - 1, 0))
        turned.append(y.astype(BF16))
    if per_time == 1:
        lhs = jnp.concatenate(
            [jnp.concatenate(direct, axis=0), jnp.concatenate(turned, axis=0)], axis=1
        )
        whole = dot(lhs, right[k]).astype(BF16)
        results = [whole[n * rows : (n + 1) * rows] for n in range(len(masks))]
    else:
        results = []
        for n, mask in enumerate(masks):
            first = pl.multiple_of(((me ^ mask) % per_time) * local_cols, local_cols)
            second = pl.multiple_of(eigen + first, local_cols)
            part = dot(direct[n], right[k, pl.ds(first, local_cols), :])
            part += dot(turned[n], right[k, pl.ds(second, local_cols), :])
            if n % per_time:
                results[-1] += part
            else:
                results.append(part)
        results = [result.astype(BF16) for result in results]
    times = [(me ^ mask) // per_time for mask in masks[::per_time]]
    return list(zip(times, results))


def near_kernel(places, masks, counts, nops, source_ref, op_ref, slot_ref, partial_ref, *refs):
    groups, (right, done) = grouped(counts, refs)
    pieces, blocks = groups[: len(places)], groups[len(places) :]
    products, eigen = right.shape[0], right.shape[2]
    scalars = (nops, source_ref, op_ref)
    for k in range(products):
        total = add_pieces(places, scalars, slot_ref, pieces, [k], eigen).astype(BF16)
        right[k, :eigen] = partial_ref[k, :eigen] + total[:, :eigen]
        right[k, eigen:] = partial_ref[k, eigen:] + total[:, eigen:]
    for k in range(products):
        for n, (_, result) in enumerate(times_right(blocks, masks, right, k)):
            done[k, n] = result.reshape(done.shape[2:])


def far_kernel(near_masks, masks, counts, right, near_ref, *refs):
    blocks, (out_ref, done, near_sems, sems) = grouped(counts, refs)
    products, eigen = right.shape[0], right.shape[2]
    near_times, times = near_ref.shape[1], done.shape[1]
    per_time = len(masks) // times
    me = lax.axis_index("col")

    def send(source, k, time, sem):
        at = pl.multiple_of(time * eigen, eigen)
        copy = pltpu.make_async_copy(source, out_ref.at[k, :, :, :, pl.ds(at, eigen)], sem)
        copy.start()
        return copy

    copies = []
    for k in range(products):
        for n in range(near_times):
            time = (me ^ near_masks[n * per_time]) // per_time
            copies.append(send(near_ref.at[k, n], k, time, near_sems.at[k, n]))
    for k in range(products):
        for n, (time, result) in enumerate(times_right(blocks, masks, right, k)):
            done[k, n] = result.reshape(done.shape[2:])
            copies.append(send(done.at[k, n], k, time, sems.at[k, n]))
    for copy in copies:
        copy.wait()


def flat(groups):
    return [part for group in groups for part in group]


def contract(places, pieces, partial, nops, source, op_index, slots, blocks):
    _, products, _, own2, local_cols = blocks[0][0].shape
    n_cols = len(blocks)
    eigen = partial.shape[2]
    times = n_cols * local_cols // eigen
    near = n_cols // 2
    near_masks, far_masks = list(range(near)), list(range(near, n_cols))
    vmem = pl.BlockSpec(memory_space=pltpu.VMEM)
    smem = pl.BlockSpec(memory_space=pltpu.SMEM)
    params = pltpu.CompilerParams(vmem_limit_bytes=VMEM_LIMIT)
    cost = pl.CostEstimate(flops=1000 * 10**6, bytes_accessed=1000, transcendentals=0)
    half = (products, times // 2, NS, own2 // 2, 2, eigen)
    groups = pieces + blocks[:near]
    right, done = pl.pallas_call(
        functools.partial(near_kernel, places, near_masks, [len(g) for g in groups], nops),
        in_specs=[smem, smem] + [vmem] * (2 + len(flat(groups))),
        out_specs=[vmem, vmem],
        out_shape=[
            jax.ShapeDtypeStruct((products, 2 * eigen, eigen), BF16),
            jax.ShapeDtypeStruct(half, BF16),
        ],
        compiler_params=params,
        cost_estimate=cost,
        name="near",
    )(source, op_index, slots, partial, *flat(groups))
    groups = blocks[near:]
    return pl.pallas_call(
        functools.partial(far_kernel, near_masks, far_masks, [len(g) for g in groups]),
        in_specs=[vmem] * (2 + len(flat(groups))),
        out_specs=pl.BlockSpec(memory_space=pl.ANY),
        out_shape=jax.ShapeDtypeStruct((products, NS, own2 // 2, 2, times * eigen), BF16),
        scratch_shapes=[
            pltpu.VMEM(half, BF16),
            pltpu.SemaphoreType.DMA(half[:2]),
            pltpu.SemaphoreType.DMA(half[:2]),
        ],
        compiler_params=params,
        cost_estimate=cost,
        name="far",
    )(right, done, *flat(groups))


def swap(array, axis, size, mask):
    return lax.ppermute(array, axis, [(i, i ^ mask) for i in range(size)])


def after(array, *others):
    return lax.optimization_barrier((array, *others))[0]


def per_device(peramb, sink_ops, op_table, row_slot, pair_source, op_index, listed_rows):
    n_cols = lax.axis_size("col")
    n_pair = lax.axis_size("tpair")
    rows, _, eigen = op_table.shape
    slots = row_slot.reshape(-1, LANES)
    nops = sink_ops.shape[1]

    def across(array, mask):
        return swap(array, "tpair", n_pair, mask)

    def beside(array):
        return swap(array, "col", n_cols, 1)

    if n_cols != 4 or n_pair != 8 or rows % 32:
        own = jnp.concatenate([op_table[:, 0], op_table[:, 1]], axis=1)
        whole = lax.all_gather(own, "tpair", axis=0, tiled=True)
        half = whole.shape[0] // 2
        mixed = mix(op_index, listed_rows, sink_ops, peramb, [1] * n_cols)
        blocks = [[mixed[0]]] + [[swap(mixed[j], "col", n_cols, j)] for j in range(1, n_cols)]
        partial = assemble([[0]], [[whole[:half]]], nops, pair_source, op_index, slots, eigen)
        return contract(
            [[half]], [[whole[half:]]], partial, nops, pair_source, op_index, slots, blocks
        )
    half = rows // 2
    own = lax.dynamic_slice_in_dim(op_table, lax.axis_index("col") % 2 * half, half, 0)
    own = jnp.concatenate([own[:, 0], own[:, 1]], axis=1)
    beside_own = beside(own)
    z1 = across(own, 2)
    z2 = across(own, 4)
    x0 = across(own, 1)
    mixed = mix(op_index, listed_rows, sink_ops, peramb, [1, 1, 2])
    crossed = swap(mixed[2], "col", n_cols, 2)
    beside_mixed = beside(mixed[1])
    beside_x0 = beside(after(x0, mixed[0]))
    z12 = after(jnp.concatenate([z1, after(z2, x0)]), mixed[0])
    z3 = across(after(own, z12), 6)
    x12 = across(z12, 1)
    x3 = across(after(z3, x12, beside_x0, beside_mixed), 1)
    early = [
        ([(0, 0)], own), ([(0, 1)], beside_own),
        ([(1, 0)], x0), ([(1, 1)], beside_x0),
        ([(2, 0), (4, 0)], z12), ([(2, 1), (4, 1)], beside(z12)),
        ([(6, 0)], z3), ([(6, 1)], beside(z3)),
        ([(3, 0), (5, 0)], x12),
    ]
    places, pieces = [p for p, _ in early], [[piece] for _, piece in early]
    partial = assemble(places, pieces, nops, pair_source, op_index, slots, eigen)
    spins = [crossed[1:, :, : NS - 1], crossed[1:, :, NS - 1 :]]
    over = [beside(after(some, partial)) for some in spins]
    blocks = [[mixed[0]], [beside_mixed], [crossed], over]
    late = [[x3], [beside(after(x3, partial))], [beside(x12)]]
    places = [[(7, 0)], [(7, 1)], [(3, 1), (5, 1)]]
    return contract(places, late, partial, nops, pair_source, op_index, slots, blocks)


def solution(mesh):
    in_specs = (
        P("tpair", None, None, "col"),
        P("tpair", None, None, None, None),
        P("tpair", None, None),
        P(),
        P("tpair"),
        P("tpair", None),
        P("tpair", None),
    )
    out_specs = P("tpair", None, "col", None, None)
    return jax.shard_map(
        per_device, mesh=mesh, in_specs=in_specs, out_specs=out_specs, check_vma=False
    )
```

```python
import functools

import jax
import jax.numpy as jnp
from jax import lax
from jax.experimental import pallas as pl
from jax.experimental.pallas import tpu as pltpu
from jax.sharding import PartitionSpec as P

NS = 4
LANES = 128
VMEM_LIMIT = 24 * 1024 * 1024
BF16, F32 = jnp.bfloat16, jnp.float32


def iota(shape, dim):
    return lax.broadcasted_iota(jnp.int32, shape, dim)


def dot(a, b):
    return jnp.dot(a, b, preferred_element_type=F32)


def column(row):
    wide = jnp.broadcast_to(row, (LANES, LANES)).astype(F32)
    return jnp.transpose(wide).astype(jnp.int32)


def one_hot(col, first, width):
    tiles = [
        jnp.where(col - (first + n) == iota((col.shape[0], LANES), 1), 1.0, 0.0)
        for n in range(0, width, LANES)
    ]
    return jnp.concatenate(tiles, axis=1).astype(BF16)


def mix_kernel(op_ref, listed_ref, sink_ref, peramb_ref, *refs):
    outs, (left, held, sems) = refs[:-3], refs[-3:]
    n_cols = sum(out.shape[0] for out in outs)
    products, listed = listed_ref.shape
    eigen, local_cols = sink_ref.shape[-1], peramb_ref.shape[-1]
    loads = [
        pltpu.make_async_copy(
            peramb_ref.at[0, :, pl.ds(s * eigen, eigen), :], held.at[s], sems.at[s]
        )
        for s in range(NS)
    ]
    for load in loads:
        load.start()
    own2 = 2 * listed // n_cols
    me = lax.axis_index("col")
    row = iota((2 * listed, 2 * listed), 0)
    wanted = ((row // own2) ^ me) * (own2 // 2) + (row % own2) // 2 + (row % 2) * listed
    order = jnp.where(wanted == iota((2 * listed, 2 * listed), 1), 1.0, 0.0).astype(BF16)
    for k in range(products):
        op = op_ref[k, 0]
        onehot = one_hot(column(listed_ref[k : k + 1, :]), 0, eigen)
        real = dot(onehot, sink_ref[0, op, 0])
        imag = dot(onehot, sink_ref[0, op, 1])
        top = jnp.concatenate([real, -imag], axis=1)
        bottom = jnp.concatenate([imag, real], axis=1)
        both = jnp.concatenate([top, bottom], axis=0).astype(BF16)
        rows = dot(order, both).astype(BF16)
        for j in range(n_cols):
            at = (j * products + k) * own2
            left[at : at + own2, :] = rows[j * own2 : (j + 1) * own2]
    for s in range(NS):
        loads[s].wait()
        mixed = dot(left[...], held[s].reshape(2 * eigen, local_cols)).astype(BF16)
        j = 0
        for out in outs:
            for n in range(out.shape[0]):
                for k in range(products):
                    at = (j * products + k) * own2
                    out[n, k, s] = mixed[at : at + own2]
                j += 1


def mix(op_index, listed_rows, sink_ops, peramb, groups):
    products, listed = listed_rows.shape
    eigen = sink_ops.shape[-1]
    local_cols = peramb.shape[3]
    own2 = 2 * listed // sum(groups)
    blocks = [
        jax.ShapeDtypeStruct((group, products, NS, own2, local_cols), BF16) for group in groups
    ]
    vmem = pl.BlockSpec(memory_space=pltpu.VMEM)
    return pl.pallas_call(
        mix_kernel,
        in_specs=[
            pl.BlockSpec(memory_space=pltpu.SMEM), vmem, vmem, pl.BlockSpec(memory_space=pltpu.HBM)
        ],
        out_specs=[vmem] * len(groups),
        out_shape=blocks,
        scratch_shapes=[
            pltpu.VMEM((products * 2 * listed, 2 * eigen), BF16),
            pltpu.VMEM((NS, 2, eigen, local_cols), BF16),
            pltpu.SemaphoreType.DMA((NS,)),
        ],
        compiler_params=pltpu.CompilerParams(vmem_limit_bytes=VMEM_LIMIT),
        cost_estimate=pl.CostEstimate(flops=1000, bytes_accessed=1000, transcendentals=0),
        name="mix",
    )(op_index, listed_rows, sink_ops, pltpu.with_memory_space_constraint(peramb, pltpu.HBM))


def add_pieces(places, scalars_ref, slot_ref, pieces, products, eigen):
    nops, source_ref, op_ref = scalars_ref
    blocks = eigen // LANES
    pair, side = lax.axis_index("tpair"), lax.axis_index("col") % 2
    cols = []
    for k in products:
        op = source_ref[0] * nops + op_ref[k, 1]
        cols += [
            column(slot_ref[pl.ds(op * blocks + b, 1), :]) for b in range(blocks)
        ]
    col = jnp.concatenate(cols, axis=0)
    tiles, tables = [], []
    for owners, parts in zip(places, pieces):
        height = sum(part.shape[0] for part in parts) // len(owners)
        for owner in owners:
            first = owner
            if isinstance(owner, tuple):
                first = (2 * (pair ^ owner[0]) + (side ^ owner[1])) * height
            tiles.append(one_hot(col, first, height))
        tables += [part[...] for part in parts]
    return dot(jnp.concatenate(tiles, axis=1), jnp.concatenate(tables, axis=0))


def grouped(counts, refs):
    groups = []
    for count in counts:
        groups.append(refs[:count])
        refs = refs[count:]
    return groups, refs


def assemble_kernel(places, counts, nops, source_ref, op_ref, slot_ref, *refs):
    pieces, (out_ref,) = grouped(counts, refs)
    products, eigen = out_ref.shape[0], out_ref.shape[2]
    total = add_pieces(
        places, (nops, source_ref, op_ref), slot_ref, pieces, range(products), eigen
    )
    total = total.astype(BF16)
    for k in range(products):
        rows = slice(k * eigen, (k + 1) * eigen)
        out_ref[k, :eigen] = total[rows, :eigen]
        out_ref[k, eigen:] = total[rows, eigen:]


def assemble(places, pieces, nops, source, op_index, slots, eigen):
    products = op_index.shape[0]
    vmem = pl.BlockSpec(memory_space=pltpu.VMEM)
    smem = pl.BlockSpec(memory_space=pltpu.SMEM)
    return pl.pallas_call(
        functools.partial(assemble_kernel, places, [len(group) for group in pieces], nops),
        in_specs=[smem, smem] + [vmem] * (1 + sum(len(group) for group in pieces)),
        out_specs=vmem,
        out_shape=jax.ShapeDtypeStruct((products, 2 * eigen, eigen), BF16),
        compiler_params=pltpu.CompilerParams(vmem_limit_bytes=VMEM_LIMIT),
        cost_estimate=pl.CostEstimate(flops=1000, bytes_accessed=1000, transcendentals=0),
        name="assemble",
    )(source, op_index, slots, *[part for group in pieces for part in group])


def block_rows(parts, k):
    found = [part[0, k] for part in parts]
    return jnp.concatenate([f.reshape(-1, f.shape[-1]) for f in found], axis=0)


def times_right(blocks, masks, right, k):
    eigen = right.shape[2]
    local_cols = blocks[0][0].shape[4]
    me = lax.axis_index("col")
    per_time = eigen // local_cols
    direct = [block_rows(parts, k) for parts in blocks]
    rows = direct[0].shape[0]
    odd = iota((rows, local_cols), 0) % 2 == 1
    turned = []
    for x in direct:
        wide = x.astype(F32)
        y = jnp.where(odd, pltpu.roll(wide, 1, 0), -pltpu.roll(wide, rows - 1, 0))
        turned.append(y.astype(BF16))
    if per_time == 1:
        whole = dot(jnp.concatenate(direct, axis=0), right[k, :eigen])
        whole += dot(jnp.concatenate(turned, axis=0), right[k, eigen:])
        whole = whole.astype(BF16)
        results = [whole[n * rows : (n + 1) * rows] for n in range(len(masks))]
    else:
        results = []
        for n, mask in enumerate(masks):
            first = pl.multiple_of(((me ^ mask) % per_time) * local_cols, local_cols)
            second = pl.multiple_of(eigen + first, local_cols)
            part = dot(direct[n], right[k, pl.ds(first, local_cols), :])
            part += dot(turned[n], right[k, pl.ds(second, local_cols), :])
            if n % per_time:
                results[-1] += part
            else:
                results.append(part)
        results = [result.astype(BF16) for result in results]
    times = [(me ^ mask) // per_time for mask in masks[::per_time]]
    return list(zip(times, results))


def near_kernel(places, masks, counts, nops, source_ref, op_ref, slot_ref, partial_ref, *refs):
    groups, (right, done) = grouped(counts, refs)
    pieces, blocks = groups[: len(places)], groups[len(places) :]
    products, eigen = right.shape[0], right.shape[2]
    scalars = (nops, source_ref, op_ref)
    for k in range(products):
        total = add_pieces(places, scalars, slot_ref, pieces, [k], eigen).astype(BF16)
        right[k, :eigen] = partial_ref[k, :eigen] + total[:, :eigen]
        right[k, eigen:] = partial_ref[k, eigen:] + total[:, eigen:]
    for k in range(products):
        for n, (_, result) in enumerate(times_right(blocks, masks, right, k)):
            done[k, n] = result.reshape(done.shape[2:])


def far_kernel(near_masks, masks, counts, right, near_ref, *refs):
    blocks, (out_ref, done, near_sems, sems) = grouped(counts, refs)
    products, eigen = right.shape[0], right.shape[2]
    near_times, times = near_ref.shape[1], done.shape[1]
    per_time = len(masks) // times
    me = lax.axis_index("col")

    def send(source, k, time, sem):
        at = pl.multiple_of(time * eigen, eigen)
        copy = pltpu.make_async_copy(source, out_ref.at[k, :, :, :, pl.ds(at, eigen)], sem)
        copy.start()
        return copy

    copies = []
    for k in range(products):
        for n in range(near_times):
            time = (me ^ near_masks[n * per_time]) // per_time
            copies.append(send(near_ref.at[k, n], k, time, near_sems.at[k, n]))
    for k in range(products):
        for n, (time, result) in enumerate(times_right(blocks, masks, right, k)):
            done[k, n] = result.reshape(done.shape[2:])
            copies.append(send(done.at[k, n], k, time, sems.at[k, n]))
    for copy in copies:
        copy.wait()


def flat(groups):
    return [part for group in groups for part in group]


def contract(places, pieces, partial, nops, source, op_index, slots, blocks):
    _, products, _, own2, local_cols = blocks[0][0].shape
    n_cols = len(blocks)
    eigen = partial.shape[2]
    times = n_cols * local_cols // eigen
    near = n_cols // 2
    near_masks, far_masks = list(range(near)), list(range(near, n_cols))
    vmem = pl.BlockSpec(memory_space=pltpu.VMEM)
    smem = pl.BlockSpec(memory_space=pltpu.SMEM)
    params = pltpu.CompilerParams(vmem_limit_bytes=VMEM_LIMIT)
    cost = pl.CostEstimate(flops=1000 * 10**6, bytes_accessed=1000, transcendentals=0)
    half = (products, times // 2, NS, own2 // 2, 2, eigen)
    groups = pieces + blocks[:near]
    right, done = pl.pallas_call(
        functools.partial(near_kernel, places, near_masks, [len(g) for g in groups], nops),
        in_specs=[smem, smem] + [vmem] * (2 + len(flat(groups))),
        out_specs=[vmem, vmem],
        out_shape=[
            jax.ShapeDtypeStruct((products, 2 * eigen, eigen), BF16),
            jax.ShapeDtypeStruct(half, BF16),
        ],
        compiler_params=params,
        cost_estimate=cost,
        name="near",
    )(source, op_index, slots, partial, *flat(groups))
    groups = blocks[near:]
    return pl.pallas_call(
        functools.partial(far_kernel, near_masks, far_masks, [len(g) for g in groups]),
        in_specs=[vmem] * (2 + len(flat(groups))),
        out_specs=pl.BlockSpec(memory_space=pl.ANY),
        out_shape=jax.ShapeDtypeStruct((products, NS, own2 // 2, 2, times * eigen), BF16),
        scratch_shapes=[
            pltpu.VMEM(half, BF16),
            pltpu.SemaphoreType.DMA(half[:2]),
            pltpu.SemaphoreType.DMA(half[:2]),
        ],
        compiler_params=params,
        cost_estimate=cost,
        name="far",
    )(right, done, *flat(groups))


def swap(array, axis, size, mask):
    return lax.ppermute(array, axis, [(i, i ^ mask) for i in range(size)])


def after(array, *others):
    return lax.optimization_barrier((array, *others))[0]


def per_device(peramb, sink_ops, op_table, row_slot, pair_source, op_index, listed_rows):
    n_cols = lax.axis_size("col")
    n_pair = lax.axis_size("tpair")
    rows, _, eigen = op_table.shape
    slots = row_slot.reshape(-1, LANES)
    nops = sink_ops.shape[1]

    def across(array, mask):
        return swap(array, "tpair", n_pair, mask)

    def beside(array):
        return swap(array, "col", n_cols, 1)

    if n_cols != 4 or n_pair != 8 or rows % 32:
        own = jnp.concatenate([op_table[:, 0], op_table[:, 1]], axis=1)
        whole = lax.all_gather(own, "tpair", axis=0, tiled=True)
        half = whole.shape[0] // 2
        mixed = mix(op_index, listed_rows, sink_ops, peramb, [1] * n_cols)
        blocks = [[mixed[0]]] + [[swap(mixed[j], "col", n_cols, j)] for j in range(1, n_cols)]
        partial = assemble([[0]], [[whole[:half]]], nops, pair_source, op_index, slots, eigen)
        return contract(
            [[half]], [[whole[half:]]], partial, nops, pair_source, op_index, slots, blocks
        )
    half = rows // 2
    own = lax.dynamic_slice_in_dim(op_table, lax.axis_index("col") % 2 * half, half, 0)
    own = jnp.concatenate([own[:, 0], own[:, 1]], axis=1)
    beside_own = beside(own)
    z1 = across(own, 2)
    z2 = across(own, 4)
    x0 = across(own, 1)
    mixed = mix(op_index, listed_rows, sink_ops, peramb, [1, 1, 2])
    crossed = swap(mixed[2], "col", n_cols, 2)
    beside_mixed = beside(mixed[1])
    beside_x0 = beside(after(x0, mixed[0]))
    z12 = after(jnp.concatenate([z1, after(z2, x0)]), mixed[0])
    z3 = across(after(own, z12), 6)
    x12 = across(z12, 1)
    x3 = across(after(z3, x12, beside_x0, beside_mixed), 1)
    early = [
        ([(0, 0)], own), ([(0, 1)], beside_own),
        ([(1, 0)], x0), ([(1, 1)], beside_x0),
        ([(2, 0), (4, 0)], z12), ([(2, 1), (4, 1)], beside(z12)),
        ([(6, 0)], z3), ([(6, 1)], beside(z3)),
        ([(3, 0), (5, 0)], x12),
    ]
    places, pieces = [p for p, _ in early], [[piece] for _, piece in early]
    partial = assemble(places, pieces, nops, pair_source, op_index, slots, eigen)
    spins = [crossed[1:, :, : NS - 1], crossed[1:, :, NS - 1 :]]
    over = [beside(after(some, partial)) for some in spins]
    blocks = [[mixed[0]], [beside_mixed], [crossed], over]
    late = [[x3], [beside(after(x3, partial))], [beside(x12)]]
    places = [[(7, 0)], [(7, 1)], [(3, 1), (5, 1)]]
    return contract(places, late, partial, nops, pair_source, op_index, slots, blocks)


def solution(mesh):
    in_specs = (
        P("tpair", None, None, "col"),
        P("tpair", None, None, None, None),
        P("tpair", None, None),
        P(),
        P("tpair"),
        P("tpair", None),
        P("tpair", None),
    )
    out_specs = P("tpair", None, "col", None, None)
    return jax.shard_map(
        per_device, mesh=mesh, in_specs=in_specs, out_specs=out_specs, check_vma=False
    )
```
